32 devices in a mesh: dp: 8 (over z, y), fsdp: 4 (over x, core).
Axes of the slice: x: 2, y: 2, z: 4, core: 2. Of those that a mesh axis runs over, the one named last changes fastest.
Arguments:
- images: bfloat16 [128, 32, 32, 256], P(('dp', 'fsdp')), may hold values from -6 to 6
- image_sizes: int32 [128, 2], P(('dp', 'fsdp')), may hold values from 16 to 32, as said below
- out_grad: bfloat16 [128, 16, 16, 256], P(('dp', 'fsdp')), may hold values from -6 to 6
- weight_one: float32 [147456], P(('dp', 'fsdp')), may hold values from -0.125 to 0.125
- first_one: float32 [147456], P(('dp', 'fsdp')), may hold values from -6 to 6
- second_one: float32 [147456], P(('dp', 'fsdp')), may hold values from 0.4194304 to 1.6777216
- weight_two: float32 [36864], P(('dp', 'fsdp')), may hold values from -0.25 to 0.25
- first_two: float32 [36864], P(('dp', 'fsdp')), may hold values from -16 to 16
- second_two: float32 [36864], P(('dp', 'fsdp')), may hold values from 0.5308416 to 2.1233664
- weight_three: float32 [36864], P(('dp', 'fsdp')), may hold values from -0.25 to 0.25
- first_three: float32 [36864], P(('dp', 'fsdp')), may hold values from -24 to 24
- second_three: float32 [36864], P(('dp', 'fsdp')), may hold values from 1.47456 to 5.89824
- weight_four: float32 [16384], P(('dp', 'fsdp')), may hold values from -48 to 48
- first_four: float32 [16384], P(('dp', 'fsdp')), may hold values from -0.875 to 0.875
- second_four: float32 [16384], P(('dp', 'fsdp')), may hold values from 0.000262144 to 0.001048576
- biases: float32 [448], replicated
- first_bias: float32 [448], replicated
- second_bias: float32 [448], replicated, as said below
Outputs:
- block_out: bfloat16 [128, 16, 16, 256], P(('dp', 'fsdp'))
- image_grad: bfloat16 [128, 32, 32, 256], P(('dp', 'fsdp'))
- first_one_new: float32 [147456], P(('dp', 'fsdp'))
- second_one_new: float32 [147456], P(('dp', 'fsdp'))
- weight_one_new: float32 [147456], P(('dp', 'fsdp'))
- copy_one: bfloat16 [147456], P(('dp', 'fsdp'))
- first_two_new: float32 [36864], P(('dp', 'fsdp'))
- second_two_new: float32 [36864], P(('dp', 'fsdp'))
- weight_two_new: float32 [36864], P(('dp', 'fsdp'))
- copy_two: bfloat16 [36864], P(('dp', 'fsdp'))
- first_three_new: float32 [36864], P(('dp', 'fsdp'))
- second_three_new: float32 [36864], P(('dp', 'fsdp'))
- weight_three_new: float32 [36864], P(('dp', 'fsdp'))
- copy_three: bfloat16 [36864], P(('dp', 'fsdp'))
- first_four_new: float32 [16384], P(('dp', 'fsdp'))
- second_four_new: float32 [16384], P(('dp', 'fsdp'))
- weight_four_new: float32 [16384], P(('dp', 'fsdp'))
- copy_four: bfloat16 [16384], P(('dp', 'fsdp'))
- first_bias_new: float32 [448], replicated
- second_bias_new: float32 [448], replicated
- biases_new: float32 [448], replicated
- copy_bias: bfloat16 [448], replicated
The draws below stay inside these ranges and needn't reach their ends.
Inputs may be any that keep to these rules, and one draw needn't show every extreme that they name: `image_sizes`: each height and width is 16, 24 or 32; the first image is 32 x 32. `second_bias`: Positive.
All inputs are finite; a program needn't handle non-finite values.
Results may differ from the reference program's by a relative error of at most 0.0069.
Values may be sent and summed in bfloat16 or wider, within the bound.
No kernel may reach another device: no remote copies, remote signals or barrier semaphores. Data moves between devices by JAX's collectives and lax.ppermute only.
A program may use at most 192 MiB of HBM per device.

```python
import math
import jax
import jax.numpy as jnp
from jax import lax

C = 256
HID = 64
IMG_DEV = 4
SIDE = 32
STEP = 10
IMAGES = 128


def draw_image_sizes(key, part):
    key = jax.random.fold_in(key, 11)
    drawn = jax.random.randint(key, (IMAGES, 2), 0, 10)
    quarter = SIDE // 4
    sides = jnp.where(drawn < 4, 2 * quarter, jnp.where(drawn < 7, 3 * quarter, 4 * quarter))
    leading = (jnp.arange(IMAGES) == 0)[:, None]
    return jnp.where(leading, SIDE, sides).astype(jnp.int32)


def segment_values(first_value, second_value, third_value, last_value):
    spots = jnp.arange(3 * HID + C)
    return jnp.where(spots < HID, first_value, jnp.where(spots < 2 * HID, second_value, jnp.where(spots < 3 * HID, third_value, last_value))).astype(jnp.float32)


def draw_biases(key, part):
    key = jax.random.fold_in(key, 23)
    scales = segment_values(0.5, 0.5, 0.5, 32.0)
    normal_values = jnp.clip(jax.random.normal(key, (3 * HID + C,), jnp.float32), -6.0, 6.0)
    return normal_values * scales


def draw_first_bias(key, part):
    key = jax.random.fold_in(key, 37)
    pixels = (0.5 * IMAGES * SIDE * SIDE) ** 0.5
    scales = segment_values(0.11, 0.18, 0.3, 0.0039) * 0.11 * pixels
    normal_values = jnp.clip(jax.random.normal(key, (3 * HID + C,), jnp.float32), -6.0, 6.0)
    return normal_values * scales


def draw_second_bias(key, part):
    key = jax.random.fold_in(key, 41)
    pixels = 0.5 * IMAGES * SIDE * SIDE
    rms_values = segment_values(0.11, 0.18, 0.3, 0.0039)
    spread = jnp.exp(jax.random.uniform(key, (3 * HID + C,), jnp.float32, 0.0, 1.3862944))
    return 0.001 * pixels * rms_values * rms_values * spread


def level_of(rng, extent, split, least, high):
    level = 1.0
    for dim, parts in split:
        heights = jax.random.uniform(jax.random.fold_in(jax.random.fold_in(rng, 6), dim), (parts,), jnp.float32, least / len(split), high / len(split))
        level = level * jnp.repeat(jnp.exp(heights), extent[dim] // parts).reshape((-1,) + (1,) * (len(extent) - 1 - dim))
    return level


def noise(rng, shape, scale, most, pieces=(), kind=jnp.bfloat16):
    array = jax.random.normal(rng, shape, jnp.float32) * scale
    if len(pieces) > 0:
        array = level_of(rng, shape, pieces, -0.22, 0.18) * array
    return jnp.clip(array, min=-most, max=most).astype(kind)


def setup_inputs(seed: int = 0) -> dict:
    streams_of = jax.random.split(jax.random.key(seed), 19)
    return {
        "images": noise(streams_of[0], (IMAGES, SIDE, SIDE, C), 1.0, 6.0, ((0, 32),)),
        "image_sizes": draw_image_sizes(jax.random.fold_in(streams_of[18], 71), 0),
        "out_grad": noise(streams_of[2], (IMAGES, SIDE // 2, SIDE // 2, C), 1.0, 6.0, ((0, 32),)),
        "weight_one": noise(streams_of[3], (9 * C * HID,), (9 * C) ** -0.5, 0.125, ((0, 32),), jnp.float32),
        "first_one": noise(streams_of[4], (9 * C * HID,), (0.0062 * (IMAGES * SIDE * SIDE) ** 0.5), 6.0, ((0, 32),), jnp.float32),
        "second_one": jnp.clip(jnp.exp(math.log(1.6777216) - 1.3862944 * jax.random.uniform(streams_of[5], (9 * C * HID,), jnp.float32) ** level_of(streams_of[5], (9 * C * HID,), ((0, 32),), -0.2, 0.2)), 0.4194304, 1.6777216),
        "weight_two": noise(streams_of[6], (9 * HID * HID,), (9 * HID) ** -0.5, 0.25, ((0, 32),), jnp.float32),
        "first_two": noise(streams_of[7], (9 * HID * HID,), (0.0070 * (IMAGES * SIDE * SIDE) ** 0.5), 16.0, ((0, 32),), jnp.float32),
        "second_two": jnp.clip(jnp.exp(math.log(2.1233664) - 1.3862944 * jax.random.uniform(streams_of[8], (9 * HID * HID,), jnp.float32) ** level_of(streams_of[8], (9 * HID * HID,), ((0, 32),), -0.2, 0.2)), 0.5308416, 2.1233664),
        "weight_three": noise(streams_of[9], (9 * HID * HID,), (9 * HID) ** -0.5, 0.25, ((0, 32),), jnp.float32),
        "first_three": noise(streams_of[10], (9 * HID * HID,), (0.0117 * (IMAGES * SIDE * SIDE) ** 0.5), 24.0, ((0, 32),), jnp.float32),
        "second_three": jnp.clip(jnp.exp(math.log(5.89824) - 1.3862944 * jax.random.uniform(streams_of[11], (9 * HID * HID,), jnp.float32) ** level_of(streams_of[11], (9 * HID * HID,), ((0, 32),), -0.2, 0.2)), 1.47456, 5.89824),
        "weight_four": noise(streams_of[12], (HID * C,), 8.0, 48.0, ((0, 32),), jnp.float32),
        "first_four": noise(streams_of[13], (HID * C,), (0.000156 * (IMAGES * SIDE * SIDE) ** 0.5), 0.875, ((0, 32),), jnp.float32),
        "second_four": jnp.clip(jnp.exp(math.log(0.001048576) - 1.3862944 * jax.random.uniform(streams_of[14], (HID * C,), jnp.float32) ** level_of(streams_of[14], (HID * C,), ((0, 32),), -0.2, 0.2)), 0.000262144, 0.001048576),
        "biases": draw_biases(jax.random.fold_in(streams_of[18], 71), 0),
        "first_bias": draw_first_bias(jax.random.fold_in(streams_of[18], 71), 0),
        "second_bias": draw_second_bias(jax.random.fold_in(streams_of[18], 71), 0),
    }


@jax.custom_vjp
def low(v):
    return lax.optimization_barrier(v.astype(jnp.bfloat16)).astype(jnp.float32)

@jax.custom_vjp
def low_back(v):
    return v

def low_keep(v):
    return (low(v), None)

def low_pass(kept, grad):
    return (grad,)

def back_keep(v):
    return (v, None)

def back_low(kept, grad):
    return (low(grad),)
low.defvjp(low_keep, low_pass)
low_back.defvjp(back_keep, back_low)
GAIN = 1.0 / 64.0
BETA_ONE = 0.9
BETA_TWO = 0.999
DECAY = 0.01
EPSILON = 1e-08

def conv_same(active, kernel):
    return lax.conv_general_dilated(active, kernel, (1, 1), 'SAME', dimension_numbers=('NHWC', 'HWIO', 'NHWC'), precision=lax.Precision.HIGHEST)

def image_masks(image_sizes):
    places = jnp.arange(SIDE, dtype=jnp.int32)
    inside = (places[None, :, None] < image_sizes[:, 0, None, None]) & (places[None, None, :] < image_sizes[:, 1, None, None])
    halves = jnp.arange(SIDE // 2, dtype=jnp.int32)
    pooled = (halves[None, :, None] < (image_sizes[:, 0] // 2)[:, None, None]) & (halves[None, None, :] < (image_sizes[:, 1] // 2)[:, None, None])
    return (inside.astype(jnp.float32)[..., None], pooled.astype(jnp.float32)[..., None])

def forward(inside, pooled, images, weight_one, weight_two, weight_three, weight_four, biases):
    base = images * inside
    active = low(jax.nn.silu(base))
    conv_out = low_back(conv_same(active, low(weight_one.reshape(3, 3, C, HID))) + biases[0:HID])
    active = low(jax.nn.silu(conv_out) * inside)
    conv_out = low_back(conv_same(active, low(weight_two.reshape(3, 3, HID, HID))) + biases[HID:2 * HID])
    active = low(jax.nn.silu(conv_out) * inside)
    conv_out = low_back(conv_same(active, low(weight_three.reshape(3, 3, HID, HID))) + biases[2 * HID:3 * HID])
    active = low(jax.nn.silu(conv_out) * inside)
    last = jnp.einsum('nhwc,co->nhwo', active, low(weight_four.reshape(HID, C)), precision=lax.Precision.HIGHEST)
    last = low_back(last + biases[3 * HID:])
    summed = base + GAIN * last
    count, side_h, side_w, width = summed.shape
    return lax.optimization_barrier(jnp.mean(summed.reshape(count, side_h // 2, 2, side_w // 2, 2, width), axis=(2, 4))) * pooled

def adamw_update(weight, gradient, first_old, second_old, step_rate):
    first_new = BETA_ONE * first_old + (1.0 - BETA_ONE) * gradient
    second_new = BETA_TWO * second_old + (1.0 - BETA_TWO) * gradient * gradient
    first_hat = first_new / (1.0 - BETA_ONE ** STEP)
    second_hat = second_new / (1.0 - BETA_TWO ** STEP)
    weight_new = weight - step_rate * (first_hat / (jnp.sqrt(second_hat) + EPSILON) + DECAY * weight)
    return (first_new, second_new, weight_new, weight_new.astype(jnp.bfloat16))

def reference(images, image_sizes, out_grad, weight_one, first_one, second_one, weight_two, first_two, second_two, weight_three, first_three, second_three, weight_four, first_four, second_four, biases, first_bias, second_bias):
    groups = IMAGES // IMG_DEV
    image_groups = images.reshape(groups, IMG_DEV, SIDE, SIDE, C)
    size_groups = image_sizes.reshape(groups, IMG_DEV, 2)
    grad_groups = out_grad.reshape(groups, IMG_DEV, SIDE // 2, SIDE // 2, C)
    params = (weight_one, weight_two, weight_three, weight_four, biases)

    def group_step(totals, packed):
        image_block, size_block, cot_block = packed
        inside, pooled = image_masks(size_block)

        def local(image_value, one, two, three, four, bias_all):
            return forward(inside, pooled, image_value, one, two, three, four, bias_all)
        result, pull = jax.vjp(local, image_block.astype(jnp.float32), *params)
        grads = pull(cot_block.astype(jnp.float32))
        totals = tuple((total + grad_part for total, grad_part in zip(totals, grads[1:])))
        return (totals, (result.astype(jnp.bfloat16), grads[0].astype(jnp.bfloat16)))
    start = tuple((jnp.zeros_like(param) for param in params))
    totals, (outs_block, grads_block) = lax.scan(group_step, start, (image_groups, size_groups, grad_groups))
    block_out = outs_block.reshape(IMAGES, SIDE // 2, SIDE // 2, C)
    image_grad = grads_block.reshape(IMAGES, SIDE, SIDE, C)
    bias_rates = jnp.where(jnp.arange(3 * HID + C) < 3 * HID, 0.5, 32.0)
    upd_one = adamw_update(weight_one, totals[0], first_one, second_one, (9.0 * C) ** (-0.5))
    upd_two = adamw_update(weight_two, totals[1], first_two, second_two, (9.0 * HID) ** (-0.5))
    upd_three = adamw_update(weight_three, totals[2], first_three, second_three, (9.0 * HID) ** (-0.5))
    upd_four = adamw_update(weight_four, totals[3], first_four, second_four, 8.0)
    upd_bias = adamw_update(biases, totals[4], first_bias, second_bias, bias_rates)
    return (block_out, image_grad, upd_one[0], upd_one[1], upd_one[2], upd_one[3], upd_two[0], upd_two[1], upd_two[2], upd_two[3], upd_three[0], upd_three[1], upd_three[2], upd_three[3], upd_four[0], upd_four[1], upd_four[2], upd_four[3], upd_bias[0], upd_bias[1], upd_bias[2], upd_bias[3])
```

```python
import functools

import jax
import jax.numpy as jnp
from jax import lax
from jax.experimental import pallas as pl
from jax.experimental.pallas import tpu as pltpu
from jax.sharding import PartitionSpec as P

C = 256
HID = 64
STEP = 10
SIDE = 32
HALF = SIDE // 2
ROWS = HALF * SIDE
PAD = SIDE

GAIN = 1.0 / 64.0
BETA_ONE = 0.9
BETA_TWO = 0.999
DECAY = 0.01
EPSILON = 1e-08
AXES = ("dp", "fsdp")

COMPACT = (9 * C * HID // 128, 9 * HID * HID // 128, 9 * HID * HID // 128, HID * C // 128)
BIASES = 3 * HID + C

F32 = jnp.float32
BF16 = jnp.bfloat16


def sigmoid(value):
    return 0.5 * jnp.tanh(0.5 * value) + 0.5


def dot(left, right):
    return jnp.dot(left, right, preferred_element_type=F32)


def dot_rows(left, right):
    return lax.dot_general(left, right, (((0,), (0,)), ((), ())), preferred_element_type=F32)


def swap_halves(value):
    return pltpu.roll(value, HID, 1)


def low_lanes(shape):
    return lax.broadcasted_iota(jnp.int32, shape, 1) < HID


def shard_rows(shards):
    return tuple(rows // shards for rows in COMPACT)


def unpack_weights(shards, me_ref, mine_ref, stage, taps_one, taps_two, taps_three, taps_four):
    one, two, three, four = shard_rows(shards)
    total = one + two + three + four
    held = mine_ref.shape[1]
    stage[...] = mine_ref[...].reshape(shards * held, 128).astype(F32)

    def place(shard, carry):
        owner = me_ref[0] ^ place_mask(shards, shard) if shards > 1 else shard
        start = shard * held
        for taps, rows, at in (
            (taps_one, one, 0),
            (taps_two, two, one),
            (taps_three, three, one + two),
        ):
            value = stage[pl.ds(start + at, rows), :]
            first = owner * (2 * rows)
            taps[pl.ds(first, rows, stride=2), :] = value
            taps[pl.ds(first + 1, rows, stride=2), :] = swap_halves(value)
        at = start + one + two + three
        first = owner * (four // 2)
        for row in range(four // 2):
            taps_four[0, pl.ds(first + row, 1), :] = stage[pl.ds(at + 2 * row, 1), :]
            taps_four[1, pl.ds(first + row, 1), :] = stage[pl.ds(at + 2 * row + 1, 1), :]
        return carry

    lax.fori_loop(0, shards, place, 0)


def tap_blocks(taps, width, col_tap):
    rows = [taps[(row_tap * 3 + col_tap) * width : (row_tap * 3 + col_tap + 1) * width, :] for row_tap in range(3)]
    low = low_lanes((width, 128))
    zero = jnp.zeros((width, 128), F32)
    turned = [swap_halves(value) for value in rows]
    return (
        jnp.where(low, rows[0], zero),
        jnp.where(low, rows[1], turned[0]),
        jnp.where(low, rows[2], turned[1]),
        jnp.where(low, zero, turned[2]),
    )


def main_kernel(
    shards,
    me_ref,
    sizes_ref,
    mine_ref,
    bias_ref,
    img_ref,
    og_ref,
    out_ref,
    grad_ref,
    send_ref,
    bias_out_ref,
    stage,
    taps_one,
    taps_two,
    taps_three,
    taps_four,
    fwd_one,
    back_one,
    fwd_two,
    back_two,
    fwd_three,
    back_three,
    fwd_four,
    back_four,
    spread_up,
    pool_down,
    act_even,
    act_odd,
    slope_even,
    slope_odd,
    act_one,
    act_two,
    act_three,
    spread_low,
    slope_one,
    slope_two,
    turned,
    sum_even,
    sum_odd,
    sum_two,
    sum_three,
    sum_four,
    sum_bias,
):
    step = pl.program_id(0)
    steps = pl.num_programs(0)

    @pl.when(step == 0)
    def prepare():
        unpack_weights(
            shards, me_ref, mine_ref, stage, taps_one, taps_two, taps_three, taps_four
        )
        for col_tap in range(3):
            lanes = slice(col_tap * 128, (col_tap + 1) * 128)
            more = slice(384 + col_tap * 128, 384 + (col_tap + 1) * 128)
            blocks = tap_blocks(taps_one, C, col_tap)
            for place, block in enumerate(blocks):
                fwd_one[place * C : (place + 1) * C, lanes] = block.astype(BF16)
            back_one[lanes, 0:C] = blocks[1].T.astype(BF16)
            back_one[lanes, C : 2 * C] = blocks[2].T.astype(BF16)
            back_one[more, 0:C] = blocks[3].T.astype(BF16)
            back_one[more, C : 2 * C] = blocks[0].T.astype(BF16)
            for taps, fwd, back in (
                (taps_two, fwd_two, back_two),
                (taps_three, fwd_three, back_three),
            ):
                blocks = tap_blocks(taps, HID, col_tap)
                for place, which in enumerate((1, 2, 3, 0)):
                    fwd[place * HID : (place + 1) * HID, lanes] = blocks[which].astype(BF16)
                back[lanes, :] = jnp.concatenate([blocks[1], blocks[2]], axis=0).T.astype(BF16)
                back[more, :] = jnp.concatenate([blocks[3], blocks[0]], axis=0).T.astype(BF16)
        four = jnp.concatenate([taps_four[0], taps_four[1]], axis=1)
        both = jnp.concatenate([four, four], axis=0)
        fwd_four[...] = both.astype(BF16)
        back_four[...] = both.T.astype(BF16)
        pix = lax.broadcasted_iota(jnp.int32, (256, 128), 0)
        spot = lax.broadcasted_iota(jnp.int32, (256, 128), 1)
        spread_up[...] = jnp.where(pix // 2 == spot, 1.0, 0.0).astype(BF16)
        spot = lax.broadcasted_iota(jnp.int32, (128, 256), 0)
        pix = lax.broadcasted_iota(jnp.int32, (128, 256), 1)
        pool_down[...] = jnp.where(pix // 2 == spot, 0.25, 0.0).astype(BF16)
        act_even[ROWS : ROWS + PAD, :] = jnp.zeros((PAD, C), BF16)
        act_odd[0:PAD, :] = jnp.zeros((PAD, C), BF16)
        for act in (act_one, act_two):
            act[0:PAD, :] = jnp.zeros((PAD, 128), BF16)
            act[PAD + ROWS :, :] = jnp.zeros((PAD, 128), BF16)
        turned[0:PAD, :] = jnp.zeros((PAD, 384), BF16)
        turned[PAD + ROWS :, :] = jnp.zeros((PAD, 384), BF16)
        for total in (sum_even, sum_odd, sum_two, sum_three, sum_four, sum_bias):
            total[...] = jnp.zeros(total.shape, F32)

    height = sizes_ref[step, 0]
    width = sizes_ref[step, 1]
    spot = lax.broadcasted_iota(jnp.int32, (ROWS, 128), 0)
    col = jnp.bitwise_and(spot, SIDE - 1)
    inside = (spot < height * HALF) & (col < width)
    mask = jnp.where(inside, 1.0, 0.0)
    wide_mask = jnp.concatenate([mask, mask], axis=1)
    first_col = col == 0
    last_col = col == SIDE - 1
    low = low_lanes((ROWS, 128))
    low_wide = jnp.concatenate([low, low, low], axis=1)

    for parity, act, slope, at in ((0, act_even, slope_even, 0), (1, act_odd, slope_odd, PAD)):
        base = img_ref[0, :, parity].reshape(ROWS, C).astype(F32) * wide_mask
        sigma = sigmoid(base)
        active = base * sigma
        act[at : at + ROWS, :] = active.astype(BF16)
        slope[...] = (sigma + active * (1.0 - sigma)) * wide_mask

    def shift_sum(parts):
        before = jnp.where(first_col, 0.0, pltpu.roll(parts[:, 0:128], 1, 0))
        after = jnp.where(last_col, 0.0, pltpu.roll(parts[:, 256:384], ROWS - 1, 0))
        return before + parts[:, 128:256] + after

    def activate(conv):
        sigma = sigmoid(conv)
        active = conv * sigma
        return active * mask, (sigma + active * (1.0 - sigma)) * mask

    even = act_even[0:ROWS, :]
    odd = act_odd[PAD : PAD + ROWS, :]
    window = jnp.concatenate(
        [act_odd[0:ROWS, :], even, odd, act_even[PAD : PAD + ROWS, :]], axis=1
    )
    conv = shift_sum(dot(window, fwd_one[...])) + bias_ref[0:1, 0:128]
    active, slope = activate(conv)
    act_one[PAD : PAD + ROWS, :] = active.astype(BF16)
    slope_one[...] = slope

    def rows_around(act):
        here = act[PAD : PAD + ROWS, :]
        around = jnp.where(low, act[2 * PAD : 2 * PAD + ROWS, :], act[0:ROWS, :])
        return jnp.concatenate([here, around], axis=1)

    conv = shift_sum(dot(rows_around(act_one), fwd_two[...])) + bias_ref[1:2, 0:128]
    active, slope = activate(conv)
    act_two[PAD : PAD + ROWS, :] = active.astype(BF16)
    slope_two[...] = slope
    conv = shift_sum(dot(rows_around(act_two), fwd_three[...])) + bias_ref[2:3, 0:128]
    active, slope_three = activate(conv)
    act_three[...] = active.astype(BF16)

    pooled = lax.broadcasted_iota(jnp.int32, (256, C), 0)
    pooled_mask = (pooled < height * (HALF // 2)) & (
        jnp.bitwise_and(pooled, HALF - 1) < width // 2
    )
    cot = jnp.where(pooled_mask, og_ref[0].reshape(256, C).astype(F32), 0.0)
    cot_low = cot.astype(BF16)
    pieces = []
    spread = []
    for half in range(2):
        rows = slice(half * 256, (half + 1) * 256)
        base_mean = dot(pool_down[...], img_ref[0, :, 0].reshape(ROWS, C)[rows]) + dot(
            pool_down[...], img_ref[0, :, 1].reshape(ROWS, C)[rows]
        )
        act_mean = dot(pool_down[...], act_three[rows, :]).astype(BF16)
        last = dot(act_mean, fwd_four[...]) + bias_ref[3:4, :]
        pieces.append(base_mean + GAIN * last)
        spread.append(dot(spread_up[...], cot_low[half * 128 : (half + 1) * 128]))
    result = jnp.where(pooled_mask, jnp.concatenate(pieces, axis=0), 0.0)
    out_ref[0] = result.reshape(HALF, HALF, C).astype(BF16)
    spread = jnp.concatenate(spread, axis=0)
    spread_low[...] = spread.astype(BF16)

    part = dot_rows(act_three[...], spread_low[...])
    for row in range(0, 128, 64):
        sum_four[row : row + 64, :] = sum_four[row : row + 64, :] + part[row : row + 64, :]
    sum_bias[3:4, :] += jnp.sum(cot, axis=0, keepdims=True)
    grad = dot(spread_low[...], back_four[...]) * (GAIN * 0.25) * slope_three

    def turn(grad, row):
        sum_bias[row : row + 1, 0:128] += jnp.sum(grad, axis=0, keepdims=True)
        turned[PAD : PAD + ROWS, 0:128] = jnp.where(
            last_col, 0.0, pltpu.roll(grad, ROWS - 1, 0)
        ).astype(BF16)
        turned[PAD : PAD + ROWS, 128:256] = grad.astype(BF16)
        turned[PAD : PAD + ROWS, 256:384] = jnp.where(
            first_col, 0.0, pltpu.roll(grad, 1, 0)
        ).astype(BF16)
        here = turned[PAD : PAD + ROWS, :]
        around = jnp.where(low_wide, turned[2 * PAD : 2 * PAD + ROWS, :], turned[0:ROWS, :])
        return jnp.concatenate([here, around], axis=1)

    window = turn(grad, 2)
    sum_three[...] += dot_rows(act_two[PAD : PAD + ROWS, :], window)
    grad = dot(window, back_three[...]) * slope_two[...]
    window = turn(grad, 1)
    sum_two[...] += dot_rows(act_one[PAD : PAD + ROWS, :], window)
    grad = dot(window, back_two[...]) * slope_one[...]
    window = turn(grad, 0)
    sum_even[...] += dot_rows(even, window)
    sum_odd[...] += dot_rows(odd, window)
    back = dot(window, back_one[...])
    spread = 0.25 * spread
    for parity, slope in ((0, slope_even), (1, slope_odd)):
        value = spread * wide_mask + back[:, parity * C : (parity + 1) * C] * slope[...]
        grad_ref[0, :, parity] = value.reshape(HALF, SIDE, C).astype(BF16)

    @pl.when(step == steps - 1)
    def finish():
        for row_even, row_odd, taps, width_in in (
            (sum_even, sum_odd, taps_one, C),
            (sum_two.at[0:HID], sum_two.at[HID:128], taps_two, HID),
            (sum_three.at[0:HID], sum_three.at[HID:128], taps_three, HID),
        ):
            for col_tap in range(3):
                here = slice(col_tap * 128, (col_tap + 1) * 128)
                around = slice(384 + col_tap * 128, 384 + (col_tap + 1) * 128)
                even_here, even_around = row_even[:, here], row_even[:, around]
                odd_here, odd_around = row_odd[:, here], row_odd[:, around]
                for row_tap, value in (
                    (0, swap_halves(even_here) + odd_around),
                    (1, even_here + swap_halves(odd_here)),
                    (2, swap_halves(even_around) + odd_here),
                ):
                    at = (row_tap * 3 + col_tap) * width_in
                    taps[at : at + width_in, :] = value
        last = (sum_four[0:HID, :] + sum_four[HID:128, :]) * (GAIN * 0.25)
        taps_four[0] = last[:, 0:128]
        taps_four[1] = last[:, 128:256]
        sums = sum_bias[...]
        tail = sums[:, 0:128]
        bias_out_ref[...] = jnp.concatenate(
            [tail + swap_halves(tail), sums[:, 0:128], sums[:, 128:256]], axis=1
        )
        one, two, three, four = shard_rows(shards)
        held = send_ref.shape[1]

        def collect(shard, carry):
            start = shard * held
            for taps, rows, at in (
                (taps_one, one, 0),
                (taps_two, two, one),
                (taps_three, three, one + two),
            ):
                first = shard * (2 * rows)
                upper = taps[pl.ds(first, rows, stride=2), :]
                lower = taps[pl.ds(first + 1, rows, stride=2), :]
                stage[pl.ds(start + at, rows), :] = jnp.where(
                    low_lanes((rows, 128)), upper, swap_halves(lower)
                )
            at = start + one + two + three
            first = shard * (four // 2)
            for row in range(four // 2):
                stage[pl.ds(at + 2 * row, 1), :] = taps_four[0, pl.ds(first + row, 1), :]
                stage[pl.ds(at + 2 * row + 1, 1), :] = taps_four[1, pl.ds(first + row, 1), :]
            return carry

        lax.fori_loop(0, shards, collect, 0)
        send_ref[...] = stage[...].reshape(shards, held, 128).astype(BF16)


def run_main(shards, me, sizes, mine, bias_rows, images, out_grad):
    count = images.shape[0]
    held = mine.shape[1]
    images = images.reshape(count, HALF, 2, SIDE, C)
    whole = lambda shape: pl.BlockSpec(shape, lambda i: (0,) * len(shape))
    smem = pl.BlockSpec(memory_space=pltpu.SMEM)
    vmem = pltpu.VMEM
    padded = ROWS + PAD
    out, grad, send, bias = pl.pallas_call(
        functools.partial(main_kernel, shards),
        grid=(count,),
        in_specs=[
            smem,
            smem,
            whole((shards, held, 128)),
            whole((8, C)),
            pl.BlockSpec((1, HALF, 2, SIDE, C), lambda i: (i, 0, 0, 0, 0)),
            pl.BlockSpec((1, HALF, HALF, C), lambda i: (i, 0, 0, 0)),
        ],
        out_specs=[
            pl.BlockSpec((1, HALF, HALF, C), lambda i: (i, 0, 0, 0)),
            pl.BlockSpec((1, HALF, 2, SIDE, C), lambda i: (i, 0, 0, 0, 0)),
            whole((shards, held, 128)),
            whole((8, 384)),
        ],
        out_shape=[
            jax.ShapeDtypeStruct((count, HALF, HALF, C), BF16),
            jax.ShapeDtypeStruct((count, HALF, 2, SIDE, C), BF16),
            jax.ShapeDtypeStruct((shards, held, 128), BF16),
            jax.ShapeDtypeStruct((8, 384), F32),
        ],
        scratch_shapes=[
            vmem((shards * held, 128), F32),
            vmem((9 * C, 128), F32),
            vmem((9 * HID, 128), F32),
            vmem((9 * HID, 128), F32),
            vmem((2, HID, 128), F32),
            vmem((4 * C, 384), BF16),
            vmem((768, 2 * C), BF16),
            vmem((4 * HID, 384), BF16),
            vmem((768, 128), BF16),
            vmem((4 * HID, 384), BF16),
            vmem((768, 128), BF16),
            vmem((128, C), BF16),
            vmem((C, 128), BF16),
            vmem((256, 128), BF16),
            vmem((128, 256), BF16),
            vmem((padded, C), BF16),
            vmem((padded, C), BF16),
            vmem((ROWS, C), F32),
            vmem((ROWS, C), F32),
            vmem((padded + PAD, 128), BF16),
            vmem((padded + PAD, 128), BF16),
            vmem((ROWS, 128), BF16),
            vmem((ROWS, C), BF16),
            vmem((ROWS, 128), F32),
            vmem((ROWS, 128), F32),
            vmem((padded + PAD, 384), BF16),
            vmem((C, 768), F32),
            vmem((C, 768), F32),
            vmem((128, 768), F32),
            vmem((128, 768), F32),
            vmem((128, C), F32),
            vmem((8, C), F32),
        ],
        compiler_params=pltpu.CompilerParams(
            dimension_semantics=("arbitrary",), vmem_limit_bytes=56 * 1024 * 1024
        ),
        name="block",
    )(me, sizes, mine, bias_rows, images, out_grad)
    bias_part = jnp.concatenate(
        [bias[0, 0:HID], bias[1, 0:HID], bias[2, 0:HID], bias[3, 128:384] * GAIN]
    )
    return out, grad.reshape(count, SIDE, SIDE, C), send, bias_part


def adamw_update(weight, gradient, first_old, second_old, step_rate):
    first_new = BETA_ONE * first_old + (1.0 - BETA_ONE) * gradient
    second_new = BETA_TWO * second_old + (1.0 - BETA_TWO) * gradient * gradient
    first_hat = first_new / (1.0 - BETA_ONE**STEP)
    second_hat = second_new / (1.0 - BETA_TWO**STEP)
    weight_new = weight - step_rate * (
        first_hat / (jnp.sqrt(second_hat) + EPSILON) + DECAY * weight
    )
    return (first_new, second_new, weight_new, weight_new.astype(BF16))


def exchange(value, mask, count):
    return lax.ppermute(value, AXES, [(i, i ^ mask) for i in range(count)])


def gather_shards(value, devices):
    held = value[None]
    for low, top in bit_groups(devices):
        parts = [held] + [
            exchange(held, mask << low, devices) for mask in range(1, 1 << (top - low))
        ]
        held = jnp.concatenate(parts, axis=0)
    return held


def bit_groups(devices):
    groups = []
    top = devices.bit_length() - 1
    while top > 1:
        low = max(top - 2, 1)
        groups.append((low, top))
        top = low
    groups.append((0, 1))
    return groups


def place_mask(devices, place):
    mask = 0
    for low, top in bit_groups(devices):
        width = top - low
        mask = mask | ((place & ((1 << width) - 1)) << low)
        place = place >> width
    return mask


def local(devices, *args):
    (
        images,
        image_sizes,
        out_grad,
        weight_one,
        first_one,
        second_one,
        weight_two,
        first_two,
        second_two,
        weight_three,
        first_three,
        second_three,
        weight_four,
        first_four,
        second_four,
        biases,
        first_bias,
        second_bias,
    ) = args
    weights = (weight_one, weight_two, weight_three, weight_four)
    moments = (
        (first_one, second_one),
        (first_two, second_two),
        (first_three, second_three),
        (first_four, second_four),
    )
    rates = ((9.0 * C) ** (-0.5), (9.0 * HID) ** (-0.5), (9.0 * HID) ** (-0.5), 8.0)
    sizes = [weight.shape[0] for weight in weights]
    total = sum(sizes)
    packed = all(size % 128 == 0 for size in sizes) and sizes[3] % 256 == 0 and devices & (devices - 1) == 0
    low = jnp.concatenate([weight.astype(BF16) for weight in weights])
    me = lax.axis_index("dp") * lax.axis_size("fsdp") + lax.axis_index("fsdp")
    if packed:
        shards = devices
        mine = gather_shards(low.reshape(total // 128, 128), devices)
    else:
        shards = 1
        full = lax.all_gather(low, AXES, axis=0, tiled=False)
        parts = []
        at = 0
        for size in sizes:
            parts.append(full[:, at : at + size].reshape(-1))
            at += size
        mine = jnp.concatenate(parts).reshape(1, -1, 128)
    pair = lambda v: jnp.tile(v, C // HID)
    bias_rows = jnp.stack(
        [pair(biases[0:HID]), pair(biases[HID : 2 * HID]), pair(biases[2 * HID : 3 * HID]), biases[3 * HID :]]
        + [jnp.zeros((C,), F32)] * 4
    )
    me_arg = jnp.reshape(me, (1,)).astype(jnp.int32)
    block_out, image_grad, send, bias_part = run_main(
        shards, me_arg, image_sizes, mine, bias_rows, images, out_grad
    )
    if packed:
        moved = lax.all_to_all(send, AXES, 0, 0, tiled=False)
        summed = jnp.sum(moved.astype(F32), axis=0).reshape(-1)
    else:
        flat = send.reshape(-1).astype(F32)
        parts = []
        at = 0
        for size in sizes:
            parts.append(flat[at : at + size * devices].reshape(devices, size))
            at += size * devices
        summed = lax.psum_scatter(
            jnp.concatenate(parts, axis=1).reshape(-1), AXES, scatter_dimension=0, tiled=True
        )
    bias_total = lax.psum(bias_part, AXES)
    updates = []
    at = 0
    for weight, (first, second), rate, size in zip(weights, moments, rates, sizes):
        updates += list(adamw_update(weight, summed[at : at + size], first, second, rate))
        at += size
    bias_rates = jnp.where(jnp.arange(BIASES) < 3 * HID, 0.5, 32.0)
    updates += list(adamw_update(biases, bias_total, first_bias, second_bias, bias_rates))
    return (block_out, image_grad, *updates)


def solution(mesh):
    devices = mesh.shape["dp"] * mesh.shape["fsdp"]
    split = P(AXES)
    return jax.shard_map(
        functools.partial(local, devices),
        mesh=mesh,
        in_specs=(
            P(AXES, None, None, None),
            P(AXES, None),
            P(AXES, None, None, None),
            *([split] * 12),
            P(),
            P(),
            P(),
        ),
        out_specs=(
            P(AXES, None, None, None),
            P(AXES, None, None, None),
            *([split] * 16),
            P(),
            P(),
            P(),
            P(),
        ),
        check_vma=False,
    )
```

```python
import functools

import jax
import jax.numpy as jnp
from jax import lax
from jax.experimental import pallas as pl
from jax.experimental.pallas import tpu as pltpu
from jax.sharding import PartitionSpec as P

C = 256
HID = 64
STEP = 10
SIDE = 32
HALF = SIDE // 2
ROWS = HALF * SIDE
PAD = SIDE

GAIN = 1.0 / 64.0
BETA_ONE = 0.9
BETA_TWO = 0.999
DECAY = 0.01
EPSILON = 1e-08
AXES = ("dp", "fsdp")
UNROLL = 4

COMPACT = (9 * C * HID // 128, 9 * HID * HID // 128, 9 * HID * HID // 128, HID * C // 128)
BIASES = 3 * HID + C

F32 = jnp.float32
BF16 = jnp.bfloat16


def sigmoid(value):
    return 0.5 * jnp.tanh(0.5 * value) + 0.5


def dot(left, right):
    return jnp.dot(left, right, preferred_element_type=F32)


def dot_rows(left, right):
    return lax.dot_general(left, right, (((0,), (0,)), ((), ())), preferred_element_type=F32)


def swap_halves(value):
    return pltpu.roll(value, HID, 1)


def low_lanes(shape):
    return lax.broadcasted_iota(jnp.int32, shape, 1) < HID


def shard_layout(shards):
    one, two, three, four = (rows // shards for rows in COMPACT)
    first = -(-(one + 4) // 8) * 8
    return 2 * one, first, 2 * two, four


def shard_held(shards):
    _, first, two, four = shard_layout(shards)
    return -(-(first + two + four) // 16) * 16


def pack_kernel(one_ref, two_ref, three_ref, four_ref, out_ref, stage, rows_of_64):
    _, first, two, four = shard_layout(COMPACT[0] // one_ref.shape[0])
    stage[...] = jnp.zeros(stage.shape, F32)

    def spread_rows(ref):
        value = ref[...]
        rows = value.shape[0]
        rows_of_64[pl.ds(0, rows, stride=2), :] = value
        rows_of_64[pl.ds(1, rows, stride=2), :] = swap_halves(value)

    spread_rows(one_ref)
    rest = 2 * one_ref.shape[0] - first
    low = low_lanes((rest, 128))
    stage[0:rest, :] = jnp.where(
        low, rows_of_64[0:rest, :], swap_halves(rows_of_64[first : first + rest, :])
    )
    stage[rest:first, :] = rows_of_64[rest:first, :]
    spread_rows(two_ref)
    value = rows_of_64[0:two, :]
    spread_rows(three_ref)
    stage[first : first + two, :] = jnp.where(
        low_lanes((two, 128)), value, swap_halves(rows_of_64[0:two, :])
    )
    stage[first + two : first + two + four, :] = four_ref[...]
    out_ref[...] = stage[...].astype(BF16)


def run_pack(held, weights):
    return pl.pallas_call(
        pack_kernel,
        out_shape=jax.ShapeDtypeStruct((held, 128), BF16),
        scratch_shapes=[pltpu.VMEM((held, 128), F32), pltpu.VMEM((80, 128), F32)],
        cost_estimate=pl.CostEstimate(flops=8192, bytes_accessed=48 * 1024, transcendentals=0),
        name="pack",
    )(*weights)


def pair_masks(sizes_ref, step):
    height = sizes_ref[step, 0]
    width = sizes_ref[step, 1]
    spot = lax.broadcasted_iota(jnp.int32, (ROWS, 128), 0)
    col = jnp.bitwise_and(spot, SIDE - 1)
    inside = (spot < height * HALF) & (col < width)
    return jnp.where(inside, 1.0, 0.0), col == 0, col == SIDE - 1


def pooled_inside(sizes_ref, step):
    spot = lax.broadcasted_iota(jnp.int32, (HALF * HALF, C), 0)
    return (spot < sizes_ref[step, 0] * (HALF // 2)) & (
        jnp.bitwise_and(spot, HALF - 1) < sizes_ref[step, 1] // 2
    )


def prepare_kernel(
    sizes_ref, bias_ref, img_ref, og_ref, even_ref, odd_ref, spread_ref, bias_rows_ref
):
    step = pl.program_id(0)

    @pl.when(step == 0)
    def biases():
        parts = [bias_ref[:, at : at + 128] for at in (0, 128, 256)]
        last = jnp.concatenate([bias_ref[:, 384:448], jnp.zeros((1, HID), F32)], axis=1)
        parts.append(last)
        turned = [swap_halves(part) for part in parts]
        low = low_lanes((1, 128))
        zero = jnp.zeros((1, 128), F32)
        rows = [
            (jnp.where(low, parts[0], turned[0]), zero),
            (jnp.where(low, turned[0], parts[0]), zero),
            (jnp.where(low, parts[1], turned[1]), zero),
            (jnp.where(low, turned[1], turned[2]), jnp.where(low, turned[2], turned[3])),
        ]
        for row, pair in enumerate(rows):
            bias_rows_ref[row : row + 1, :] = jnp.concatenate(pair, axis=1)
        bias_rows_ref[4:8, :] = jnp.zeros((4, C), F32)

    mask, _, _ = pair_masks(sizes_ref, step)
    wide_mask = jnp.concatenate([mask, mask], axis=1)
    even_ref[0, ROWS : ROWS + PAD, :] = jnp.zeros((PAD, C), BF16)
    odd_ref[0, 0:PAD, :] = jnp.zeros((PAD, C), BF16)
    for parity, act, at in ((0, even_ref, 0), (1, odd_ref, PAD)):
        base = img_ref[0, :, parity].reshape(ROWS, C).astype(F32) * wide_mask
        act[0, at : at + ROWS, :] = (base * sigmoid(base)).astype(BF16)
    pix = lax.broadcasted_iota(jnp.int32, (256, 128), 0)
    spot = lax.broadcasted_iota(jnp.int32, (256, 128), 1)
    spread_up = jnp.where(pix // 2 == spot, 1.0, 0.0).astype(BF16)
    cot = jnp.where(
        pooled_inside(sizes_ref, step), og_ref[0].reshape(HALF * HALF, C).astype(F32), 0.0
    ).astype(BF16)
    for half in range(2):
        value = dot(spread_up, cot[half * 128 : (half + 1) * 128])
        spread_ref[0, half * 256 : (half + 1) * 256, :] = value.astype(BF16)


def block_of(shape):
    rest = (0,) * (len(shape) - 1)
    return pl.BlockSpec(shape, lambda i: (i,) + rest)


def whole(shape):
    return pl.BlockSpec(shape, lambda i: (0,) * len(shape))


def run_prepare(sizes, biases, images, out_grad):
    count = images.shape[0]
    padded = ROWS + PAD
    return pl.pallas_call(
        prepare_kernel,
        grid=(count,),
        in_specs=[
            pl.BlockSpec(memory_space=pltpu.SMEM),
            whole((1, BIASES)),
            block_of((1, HALF, 2, SIDE, C)),
            block_of((1, HALF, HALF, C)),
        ],
        out_specs=[
            block_of((1, padded, C)),
            block_of((1, padded, C)),
            block_of((1, ROWS, C)),
            whole((8, C)),
        ],
        out_shape=[
            jax.ShapeDtypeStruct((count, padded, C), BF16),
            jax.ShapeDtypeStruct((count, padded, C), BF16),
            jax.ShapeDtypeStruct((count, ROWS, C), BF16),
            jax.ShapeDtypeStruct((8, C), F32),
        ],
        compiler_params=pltpu.CompilerParams(
            dimension_semantics=("arbitrary",), vmem_limit_bytes=60 * 1024 * 1024
        ),
        cost_estimate=pl.CostEstimate(
            flops=count * 2 * 512 * 128 * 256, bytes_accessed=count * 1600 * 1024, transcendentals=count * 262144
        ),
        name="prepare",
    )(sizes, biases, images, out_grad)


def unpack_weights(shards, me_ref, pieces, stage, taps_one, taps_two, taps_three, taps_four):
    one, first, two, four = shard_layout(shards)
    held = pieces[0].shape[1]
    for which, piece in enumerate(pieces):
        group = piece.shape[0]
        stage[which * group * held : (which + 1) * group * held, :] = (
            piece[...].reshape(group * held, 128).astype(F32)
        )

    def place(shard, carry):
        owner = me_ref[0] ^ place_mask(shards, shard) if shards > 1 else shard
        start = pl.multiple_of(shard * held, 8)
        value = stage[pl.ds(start, first), :]
        at = pl.multiple_of(owner * one, 8)
        taps_one[pl.ds(at, first), :] = value
        taps_one[pl.ds(at + first, one - first), :] = swap_halves(value[0 : one - first])
        value = stage[pl.ds(start + first, two), :]
        taps_two[pl.ds(owner * two, two), :] = value
        taps_three[pl.ds(owner * two, two), :] = swap_halves(value)
        at = start + first + two
        for row in range(four // 2):
            row_at = owner * (four // 2) + row
            taps_four[0, pl.ds(row_at, 1), :] = stage[pl.ds(at + 2 * row, 1), :]
            taps_four[1, pl.ds(row_at, 1), :] = stage[pl.ds(at + 2 * row + 1, 1), :]
        return carry

    lax.fori_loop(0, shards, place, 0, unroll=UNROLL if shards > 1 else 1)


def tap_blocks(taps, width, col_tap):
    rows = [
        taps[(row_tap * 3 + col_tap) * width : (row_tap * 3 + col_tap + 1) * width, :]
        for row_tap in range(3)
    ]
    low = low_lanes((width, 128))
    zero = jnp.zeros((width, 128), F32)
    turned = [swap_halves(value) for value in rows]
    return (
        jnp.where(low, rows[0], zero),
        jnp.where(low, rows[1], turned[0]),
        jnp.where(low, rows[2], turned[1]),
        jnp.where(low, zero, turned[2]),
    )


def block_kernel(
    shards,
    pieces_count,
    me_ref,
    sizes_ref,
    bias_ref,
    even_ref,
    odd_ref,
    spread_ref,
    *refs,
):
    pieces = refs[:pieces_count]
    (
        send_ref,
        turned_ref,
        act_three_ref,
        back_one_ref,
        fwd_four_ref,
        stage,
        taps_one,
        taps_two,
        taps_three,
        taps_four,
        fwd_one,
        fwd_two,
        back_two,
        fwd_three,
        back_three,
        back_four,
        act_one,
        act_two,
        slope_one,
        slope_two,
        turned,
        sum_even,
        sum_odd,
        sum_two,
        sum_three,
        sum_four,
        sum_bias,
    ) = refs[pieces_count:]
    step = pl.program_id(0)
    steps = pl.num_programs(0)

    @pl.when(step == 0)
    def prepare():
        unpack_weights(
            shards, me_ref, pieces, stage, taps_one, taps_two, taps_three, taps_four
        )
        for col_tap in range(3):
            lanes = slice(col_tap * 128, (col_tap + 1) * 128)
            more = slice(384 + col_tap * 128, 384 + (col_tap + 1) * 128)
            blocks = tap_blocks(taps_one, C, col_tap)
            for place, block in enumerate(blocks):
                fwd_one[place * C : (place + 1) * C, lanes] = block.astype(BF16)
            back_one_ref[lanes, 0:C] = blocks[1].T.astype(BF16)
            back_one_ref[lanes, C : 2 * C] = blocks[2].T.astype(BF16)
            back_one_ref[more, 0:C] = blocks[3].T.astype(BF16)
            back_one_ref[more, C : 2 * C] = blocks[0].T.astype(BF16)
            for taps, fwd, back in (
                (taps_two, fwd_two, back_two),
                (taps_three, fwd_three, back_three),
            ):
                blocks = tap_blocks(taps, HID, col_tap)
                for place, which in enumerate((1, 2, 3, 0)):
                    fwd[place * HID : (place + 1) * HID, lanes] = blocks[which].astype(BF16)
                back[lanes, :] = jnp.concatenate([blocks[1], blocks[2]], axis=0).T.astype(BF16)
                back[more, :] = jnp.concatenate([blocks[3], blocks[0]], axis=0).T.astype(BF16)
        four = jnp.concatenate([taps_four[0], taps_four[1]], axis=1)
        both = jnp.concatenate([four, four], axis=0)
        fwd_four_ref[...] = both.astype(BF16)
        back_four[...] = both.T.astype(BF16)
        for act in (act_one, act_two):
            act[0:PAD, :] = jnp.zeros((PAD, 128), BF16)
            act[PAD + ROWS :, :] = jnp.zeros((PAD, 128), BF16)
        turned[0:PAD, :] = jnp.zeros((PAD, 384), BF16)
        turned[PAD + ROWS :, :] = jnp.zeros((PAD, 384), BF16)
        for total in (sum_even, sum_odd, sum_two, sum_three, sum_four, sum_bias):
            total[...] = jnp.zeros(total.shape, F32)

    mask, first_col, last_col = pair_masks(sizes_ref, step)
    low = low_lanes((ROWS, 128))
    low_wide = jnp.concatenate([low, low, low], axis=1)

    def shift_sum(parts):
        before = jnp.where(first_col, 0.0, pltpu.roll(parts[:, 0:128], 1, 0))
        after = jnp.where(last_col, 0.0, pltpu.roll(parts[:, 256:384], ROWS - 1, 0))
        return before + parts[:, 128:256] + after

    def activate(conv):
        sigma = sigmoid(conv)
        active = conv * sigma
        return active * mask, (sigma + active * (1.0 - sigma)) * mask

    even = even_ref[0, 0:ROWS, :]
    odd = odd_ref[0, PAD : PAD + ROWS, :]
    window = jnp.concatenate(
        [odd_ref[0, 0:ROWS, :], even, odd, even_ref[0, PAD : PAD + ROWS, :]], axis=1
    )
    conv = shift_sum(dot(window, fwd_one[...])) + bias_ref[0:1, 0:128]
    active, slope = activate(conv)
    act_one[PAD : PAD + ROWS, :] = active.astype(BF16)
    slope_one[...] = slope

    def rows_around(act):
        here = act[PAD : PAD + ROWS, :]
        around = jnp.where(low, act[2 * PAD : 2 * PAD + ROWS, :], act[0:ROWS, :])
        return jnp.concatenate([here, around], axis=1)

    conv = shift_sum(dot(rows_around(act_one), fwd_two[...])) + bias_ref[1:2, 0:128]
    active, slope = activate(conv)
    act_two[PAD : PAD + ROWS, :] = active.astype(BF16)
    slope_two[...] = slope
    conv = shift_sum(dot(rows_around(act_two), fwd_three[...])) + bias_ref[2:3, 0:128]
    active, slope_three = activate(conv)
    act_three_ref[0] = active.astype(BF16)

    part = dot_rows(act_three_ref[0], spread_ref[0])
    sum_four[0:HID, :] = sum_four[0:HID, :] + part[0:HID, :]
    sum_four[HID:128, :] = sum_four[HID:128, :] + part[HID:128, :]
    sum_bias[3:4, :] += jnp.sum(spread_ref[0].astype(F32), axis=0, keepdims=True)
    grad = dot(spread_ref[0], back_four[...]) * (GAIN * 0.25) * slope_three

    def turn(grad, row):
        sum_bias[row : row + 1, 0:128] += jnp.sum(grad, axis=0, keepdims=True)
        turned[PAD : PAD + ROWS, 0:128] = jnp.where(
            last_col, 0.0, pltpu.roll(grad, ROWS - 1, 0)
        ).astype(BF16)
        turned[PAD : PAD + ROWS, 128:256] = grad.astype(BF16)
        turned[PAD : PAD + ROWS, 256:384] = jnp.where(
            first_col, 0.0, pltpu.roll(grad, 1, 0)
        ).astype(BF16)
        here = turned[PAD : PAD + ROWS, :]
        around = jnp.where(low_wide, turned[2 * PAD : 2 * PAD + ROWS, :], turned[0:ROWS, :])
        return jnp.concatenate([here, around], axis=1)

    window = turn(grad, 2)
    sum_three[...] += dot_rows(act_two[PAD : PAD + ROWS, :], window)
    grad = dot(window, back_three[...]) * slope_two[...]
    window = turn(grad, 1)
    sum_two[...] += dot_rows(act_one[PAD : PAD + ROWS, :], window)
    grad = dot(window, back_two[...]) * slope_one[...]
    window = turn(grad, 0)
    turned_ref[0] = window
    sum_even[...] += dot_rows(even, window)
    sum_odd[...] += dot_rows(odd, window)

    @pl.when(step == steps - 1)
    def finish():
        for row_even, row_odd, taps, width_in in (
            (sum_even, sum_odd, taps_one, C),
            (sum_two.at[0:HID], sum_two.at[HID:128], taps_two, HID),
            (sum_three.at[0:HID], sum_three.at[HID:128], taps_three, HID),
        ):
            for col_tap in range(3):
                here = slice(col_tap * 128, (col_tap + 1) * 128)
                around = slice(384 + col_tap * 128, 384 + (col_tap + 1) * 128)
                even_here, even_around = row_even[:, here], row_even[:, around]
                odd_here, odd_around = row_odd[:, here], row_odd[:, around]
                for row_tap, value in (
                    (0, swap_halves(even_here) + odd_around),
                    (1, even_here + swap_halves(odd_here)),
                    (2, swap_halves(even_around) + odd_here),
                ):
                    at = (row_tap * 3 + col_tap) * width_in
                    taps[at : at + width_in, :] = value
        last = (sum_four[0:HID, :] + sum_four[HID:128, :]) * (GAIN * 0.25)
        taps_four[0] = last[:, 0:128]
        taps_four[1] = last[:, 128:256]
        sums = sum_bias[...]
        tail = sums[:, 0:128]
        tail = tail + swap_halves(tail)
        outer = sums[3:4, :] * (GAIN * 0.5)
        outer = (outer[:, 0:128], outer[:, 128:256])
        bias_high = jnp.concatenate(
            [
                tail[0:3],
                swap_halves(outer[0]),
                outer[0],
                swap_halves(outer[1]),
                outer[1],
                jnp.zeros((1, 128), F32),
            ],
            axis=0,
        )
        one, first, two, four = shard_layout(shards)
        held = send_ref.shape[1]
        gap = 2 * first - one - 8

        def collect(shard, carry):
            start = pl.multiple_of(shard * held, 8)
            at = pl.multiple_of(shard * one, 8)
            high = [swap_halves(taps_one[pl.ds(at + first, one - first), :])]
            if gap:
                high.append(jnp.zeros((gap, 128), F32))
            stage[pl.ds(start, first), :] = jnp.where(
                low_lanes((first, 128)),
                taps_one[pl.ds(at, first), :],
                jnp.concatenate(high + [bias_high], axis=0),
            )
            stage[pl.ds(start + first, two), :] = jnp.where(
                low_lanes((two, 128)),
                taps_two[pl.ds(shard * two, two), :],
                swap_halves(taps_three[pl.ds(shard * two, two), :]),
            )
            at = start + first + two
            for row in range(four // 2):
                row_at = shard * (four // 2) + row
                stage[pl.ds(at + 2 * row, 1), :] = taps_four[0, pl.ds(row_at, 1), :]
                stage[pl.ds(at + 2 * row + 1, 1), :] = taps_four[1, pl.ds(row_at, 1), :]
            return carry

        lax.fori_loop(0, shards, collect, 0, unroll=UNROLL if shards > 1 else 1)
        send_ref[...] = stage[...].reshape(shards, held, 128).astype(BF16)


def run_block(shards, me, sizes, bias_rows, even, odd, spread, pieces):
    count = even.shape[0]
    held = pieces[0].shape[1]
    smem = pl.BlockSpec(memory_space=pltpu.SMEM)
    vmem = pltpu.VMEM
    padded = ROWS + PAD
    return pl.pallas_call(
        functools.partial(block_kernel, shards, len(pieces)),
        grid=(count,),
        in_specs=[
            smem,
            smem,
            whole((8, C)),
            block_of((1, padded, C)),
            block_of((1, padded, C)),
            block_of((1, ROWS, C)),
            *[whole(piece.shape) for piece in pieces],
        ],
        out_specs=[
            whole((shards, held, 128)),
            block_of((1, ROWS, 768)),
            block_of((1, ROWS, 128)),
            whole((768, 2 * C)),
            whole((128, C)),
        ],
        out_shape=[
            jax.ShapeDtypeStruct((shards, held, 128), BF16),
            jax.ShapeDtypeStruct((count, ROWS, 768), BF16),
            jax.ShapeDtypeStruct((count, ROWS, 128), BF16),
            jax.ShapeDtypeStruct((768, 2 * C), BF16),
            jax.ShapeDtypeStruct((128, C), BF16),
        ],
        scratch_shapes=[
            vmem((shards * held, 128), F32),
            vmem((9 * C, 128), F32),
            vmem((9 * HID, 128), F32),
            vmem((9 * HID, 128), F32),
            vmem((2, HID, 128), F32),
            vmem((4 * C, 384), BF16),
            vmem((4 * HID, 384), BF16),
            vmem((768, 128), BF16),
            vmem((4 * HID, 384), BF16),
            vmem((768, 128), BF16),
            vmem((C, 128), BF16),
            vmem((padded + PAD, 128), BF16),
            vmem((padded + PAD, 128), BF16),
            vmem((ROWS, 128), F32),
            vmem((ROWS, 128), F32),
            vmem((padded + PAD, 384), BF16),
            vmem((C, 768), F32),
            vmem((C, 768), F32),
            vmem((128, 768), F32),
            vmem((128, 768), F32),
            vmem((128, C), F32),
            vmem((8, C), F32),
        ],
        compiler_params=pltpu.CompilerParams(
            dimension_semantics=("arbitrary",), vmem_limit_bytes=60 * 1024 * 1024
        ),
        cost_estimate=pl.CostEstimate(
            flops=count * 1_200_000_000, bytes_accessed=count * 2_000_000, transcendentals=count * 196608
        ),
        name="block",
    )(me, sizes, bias_rows, even, odd, spread, *pieces)


def finish_kernel(
    sizes_ref, bias_ref, img_ref, spread_ref, turned_ref, act_ref, back_ref, four_ref, out_ref, grad_ref
):
    step = pl.program_id(0)
    mask, _, _ = pair_masks(sizes_ref, step)
    wide_mask = jnp.concatenate([mask, mask], axis=1)
    spot = lax.broadcasted_iota(jnp.int32, (128, 256), 0)
    pix = lax.broadcasted_iota(jnp.int32, (128, 256), 1)
    pool_down = jnp.where(pix // 2 == spot, 0.25, 0.0).astype(BF16)
    pieces = []
    for half in range(2):
        rows = slice(half * 256, (half + 1) * 256)
        base_mean = dot(pool_down, img_ref[0, :, 0].reshape(ROWS, C)[rows]) + dot(
            pool_down, img_ref[0, :, 1].reshape(ROWS, C)[rows]
        )
        act_mean = dot(pool_down, act_ref[0, rows, :]).astype(BF16)
        pieces.append(base_mean + GAIN * (dot(act_mean, four_ref[...]) + bias_ref[3:4, :]))
    result = jnp.where(pooled_inside(sizes_ref, step), jnp.concatenate(pieces, axis=0), 0.0)
    out_ref[0] = result.reshape(HALF, HALF, C).astype(BF16)
    spread = 0.25 * spread_ref[0].astype(F32)
    back = dot(turned_ref[0], back_ref[...])
    for parity in range(2):
        base = img_ref[0, :, parity].reshape(ROWS, C).astype(F32)
        sigma = sigmoid(base)
        slope = (sigma + base * sigma * (1.0 - sigma)) * wide_mask
        value = spread + back[:, parity * C : (parity + 1) * C] * slope
        grad_ref[0, :, parity] = value.reshape(HALF, SIDE, C).astype(BF16)


def run_finish(sizes, bias_rows, images, spread, turned, act_three, back_one, fwd_four):
    count = images.shape[0]
    return pl.pallas_call(
        finish_kernel,
        grid=(count,),
        in_specs=[
            pl.BlockSpec(memory_space=pltpu.SMEM),
            whole((8, C)),
            block_of((1, HALF, 2, SIDE, C)),
            block_of((1, ROWS, C)),
            block_of((1, ROWS, 768)),
            block_of((1, ROWS, 128)),
            whole((768, 2 * C)),
            whole((128, C)),
        ],
        out_specs=[block_of((1, HALF, HALF, C)), block_of((1, HALF, 2, SIDE, C))],
        out_shape=[
            jax.ShapeDtypeStruct((count, HALF, HALF, C), BF16),
            jax.ShapeDtypeStruct((count, HALF, 2, SIDE, C), BF16),
        ],
        compiler_params=pltpu.CompilerParams(
            dimension_semantics=("arbitrary",), vmem_limit_bytes=60 * 1024 * 1024
        ),
        cost_estimate=pl.CostEstimate(
            flops=count * 450_000_000, bytes_accessed=count * 2_500_000, transcendentals=count * 262144
        ),
        name="finish",
    )(sizes, bias_rows, images, spread, turned, act_three, back_one, fwd_four)


def adamw_update(weight, gradient, first_old, second_old, step_rate):
    first_new = BETA_ONE * first_old + (1.0 - BETA_ONE) * gradient
    second_new = BETA_TWO * second_old + (1.0 - BETA_TWO) * gradient * gradient
    first_hat = first_new / (1.0 - BETA_ONE**STEP)
    second_hat = second_new / (1.0 - BETA_TWO**STEP)
    weight_new = weight - step_rate * (
        first_hat / (jnp.sqrt(second_hat) + EPSILON) + DECAY * weight
    )
    return (first_new, second_new, weight_new, weight_new.astype(BF16))


RATES = ((9.0 * C) ** (-0.5), (9.0 * HID) ** (-0.5), (9.0 * HID) ** (-0.5), 8.0)


def update_kernel(moved_ref, *refs):
    olds, news, total, rows_of_64 = refs[:15], refs[15:35], refs[35], refs[36]
    total[...] = jnp.sum(moved_ref[...].astype(F32), axis=0)
    one, first, two, four = shard_layout(COMPACT[0] // olds[0].shape[0])

    def joined(rows):
        return jnp.where(
            low_lanes((rows, 128)),
            rows_of_64[pl.ds(0, rows, stride=2), :],
            swap_halves(rows_of_64[pl.ds(1, rows, stride=2), :]),
        )

    rows_of_64[0:first, :] = total[0:first, :]
    rows_of_64[first:one, :] = swap_halves(total[0 : one - first, :])
    gradients = [joined(one // 2)]
    rows_of_64[0:two, :] = total[first : first + two, :]
    gradients.append(joined(two // 2))
    rows_of_64[0:two, :] = swap_halves(total[first : first + two, :])
    gradients.append(joined(two // 2))
    gradients.append(total[first + two : first + two + four, :])
    rows = total[first - 8 : first, :]
    turned = swap_halves(rows)
    low = low_lanes((1, 128))
    parts = [jnp.where(low, turned[row : row + 1], rows[row + 1 : row + 2]) for row in (0, 2, 4)]
    parts.append(turned[6:7])
    gradients.append(jnp.concatenate(parts, axis=1)[:, 0:BIASES])
    rate = jnp.where(lax.broadcasted_iota(jnp.int32, (1, BIASES), 1) < 3 * HID, 0.5, 32.0)
    for which, gradient in enumerate(gradients):
        weight, first_old, second_old = (ref[...] for ref in olds[3 * which : 3 * which + 3])
        values = adamw_update(
            weight, gradient, first_old, second_old, rate if which == 4 else RATES[which]
        )
        for ref, value in zip(news[4 * which : 4 * which + 4], values):
            ref[...] = value


def run_update(moved, olds):
    shapes = []
    for which in range(5):
        shape = olds[3 * which].shape
        shapes += [jax.ShapeDtypeStruct(shape, F32)] * 3 + [jax.ShapeDtypeStruct(shape, BF16)]
    return pl.pallas_call(
        update_kernel,
        out_shape=shapes,
        scratch_shapes=[pltpu.VMEM(moved.shape[1:], F32), pltpu.VMEM((80, 128), F32)],
        cost_estimate=pl.CostEstimate(flops=500_000, bytes_accessed=700_000, transcendentals=8192),
        name="update",
    )(moved, *olds)


def exchange(value, mask, count):
    return lax.ppermute(value, AXES, [(i, i ^ mask) for i in range(count)])


def gather_shards(value, devices, beside):
    groups = bit_groups(devices)
    held = value[None]
    for low, top in groups[:-2]:
        parts = [held] + [
            exchange(held, mask << low, devices) for mask in range(1, 1 << (top - low))
        ]
        if beside is not None:
            parts, beside = lax.optimization_barrier((parts, beside))
        held = jnp.concatenate(parts, axis=0)
    low, top = groups[-2]
    pieces = [held] + [exchange(held, mask << low, devices) for mask in range(1, 1 << (top - low))]
    return pieces + [exchange(piece, 1, devices) for piece in pieces], beside


def bit_groups(devices):
    groups = []
    top = devices.bit_length() - 1
    while top > 1:
        low = max(top - 2, 1)
        groups.append((low, top))
        top = low
    groups.append((0, 1))
    return groups


def place_mask(devices, place):
    mask = 0
    for low, top in bit_groups(devices):
        width = top - low
        mask = mask | ((place & ((1 << width) - 1)) << low)
        place = place >> width
    return mask


def local(devices, *args):
    (
        images,
        image_sizes,
        out_grad,
        weight_one,
        first_one,
        second_one,
        weight_two,
        first_two,
        second_two,
        weight_three,
        first_three,
        second_three,
        weight_four,
        first_four,
        second_four,
        biases,
        first_bias,
        second_bias,
    ) = args
    weights = (weight_one, weight_two, weight_three, weight_four)
    olds = (
        (weight_one, first_one, second_one),
        (weight_two, first_two, second_two),
        (weight_three, first_three, second_three),
        (weight_four, first_four, second_four),
    )
    count = images.shape[0]
    images = images.reshape(count, HALF, 2, SIDE, C)
    sizes = [weight.shape[0] for weight in weights]
    total = sum(sizes)
    packed = (
        all(size % 128 == 0 for size in sizes)
        and sizes[3] % 256 == 0
        and devices >= 8
        and devices & (devices - 1) == 0
    )
    me = lax.axis_index("dp") * lax.axis_size("fsdp") + lax.axis_index("fsdp")
    me = jnp.reshape(me, (1,)).astype(jnp.int32)
    shards = devices if packed else 1
    held = shard_held(shards)
    prepared = run_prepare(image_sizes, biases.reshape(1, BIASES), images, out_grad)
    if packed:
        mine = run_pack(held, [weight.reshape(-1, 128) for weight in weights])
        pieces, prepared = gather_shards(mine, devices, prepared)
    else:
        low = jnp.concatenate([weight.astype(BF16) for weight in weights])
        full = lax.all_gather(low, AXES, axis=0, tiled=False)
        parts = []
        at = 0
        for size in sizes:
            parts.append(full[:, at : at + size].reshape(-1))
            at += size
        one, first, two, four = shard_layout(1)
        rows = parts[0].reshape(one, HID)
        rows = jnp.concatenate(
            [rows[:first], jnp.pad(rows[first:], ((0, 2 * first - one), (0, 0)))], axis=1
        )
        both = jnp.concatenate([part.reshape(two, HID) for part in parts[1:3]], axis=1)
        full = jnp.concatenate([rows, both, parts[3].reshape(four, 128)], axis=0)
        pieces = [jnp.pad(full, ((0, held - full.shape[0]), (0, 0)))[None]]
    even, odd, spread, bias_rows = prepared
    send, turned, act_three, back_one, fwd_four = run_block(
        shards, me, image_sizes, bias_rows, even, odd, spread, pieces
    )
    if packed:
        moved = lax.all_to_all(send, AXES, 0, 0, tiled=False)
    block_out, image_grad = run_finish(
        image_sizes, bias_rows, images, spread, turned, act_three, back_one, fwd_four
    )
    image_grad = image_grad.reshape(count, SIDE, SIDE, C)
    if packed:
        flat = [array.reshape(-1, 128) for three in olds for array in three]
        flat += [array.reshape(1, BIASES) for array in (biases, first_bias, second_bias)]
        updates = [array.reshape(-1) for array in run_update(moved, flat)]
        return (block_out, image_grad, *updates)
    rows = send[0].astype(F32)
    one, first, two, four = shard_layout(1)
    parts = [
        jnp.concatenate([rows[:first, :HID], rows[: one - first, HID:]], axis=0),
        rows[first : first + two, :HID],
        rows[first : first + two, HID:],
        rows[first + two : first + two + four],
    ]
    parts = [part.reshape(devices, -1) for part in parts]
    bias_part = rows[first - 8 : first - 1, HID:].reshape(-1)
    bias_total = lax.psum(bias_part, AXES)
    summed = lax.psum_scatter(
        jnp.concatenate(parts, axis=1).reshape(-1), AXES, scatter_dimension=0, tiled=True
    )
    updates = []
    at = 0
    for (weight, first, second), rate, size in zip(olds, RATES, sizes):
        updates += list(adamw_update(weight, summed[at : at + size], first, second, rate))
        at += size
    bias_rates = jnp.where(jnp.arange(BIASES) < 3 * HID, 0.5, 32.0)
    updates += list(adamw_update(biases, bias_total, first_bias, second_bias, bias_rates))
    return (block_out, image_grad, *updates)


def solution(mesh):
    devices = mesh.shape["dp"] * mesh.shape["fsdp"]
    split = P(AXES)
    return jax.shard_map(
        functools.partial(local, devices),
        mesh=mesh,
        in_specs=(
            P(AXES, None, None, None),
            P(AXES, None),
            P(AXES, None, None, None),
            *([split] * 12),
            P(),
            P(),
            P(),
        ),
        out_specs=(
            P(AXES, None, None, None),
            P(AXES, None, None, None),
            *([split] * 16),
            P(),
            P(),
            P(),
            P(),
        ),
        check_vma=False,
    )
```

```python
import functools

import jax
import jax.numpy as jnp
from jax import lax
from jax.experimental import pallas as pl
from jax.experimental.pallas import tpu as pltpu
from jax.sharding import PartitionSpec as P

C = 256
HID = 64
STEP = 10
SIDE = 32
HALF = SIDE // 2
ROWS = HALF * SIDE
PAD = SIDE

GAIN = 1.0 / 64.0
BETA_ONE = 0.9
BETA_TWO = 0.999
DECAY = 0.01
EPSILON = 1e-08
AXES = ("dp", "fsdp")
UNROLL = 8
UPDATE_MB = 60
SPREAD_BYTES = 58 * 1024 * 1024
ACTIVE_BYTES = 56 * 1024 * 1024
BLOCK_BYTES = 52 * 1024 * 1024
LAG = 1
MERGE = 2
EDGE = 8
KEEP_TYPE = jnp.float32

COMPACT = (9 * C * HID // 128, 9 * HID * HID // 128, 9 * HID * HID // 128, HID * C // 128)
BIASES = 3 * HID + C

F32 = jnp.float32
BF16 = jnp.bfloat16


def silu(value):
    half = 0.5 * value
    return half * (1.0 + jnp.tanh(half))


def silu_and_slope(value):
    half = 0.5 * value
    turn = jnp.tanh(half)
    above = 1.0 + turn
    return half * above, above + half * (1.0 - turn * turn)


def dot(left, right):
    return jnp.dot(left, right, preferred_element_type=F32)


def dot_rows(left, right):
    return lax.dot_general(left, right, (((0,), (0,)), ((), ())), preferred_element_type=F32)


def swap_halves(value):
    return pltpu.roll(value, HID, 1)


def low_lanes(shape):
    return lax.broadcasted_iota(jnp.int32, shape, 1) < HID


def shard_layout(shards):
    one, two, three, four = (rows // shards for rows in COMPACT)
    first = -(-(one + 4) // 8) * 8
    return 2 * one, first, 2 * two, four


def shard_held(shards):
    _, first, two, four = shard_layout(shards)
    return -(-(first + two + four) // 16) * 16


def pack_kernel(one_ref, two_ref, three_ref, four_ref, out_ref, stage, rows_of_64):
    _, first, two, four = shard_layout(COMPACT[0] // one_ref.shape[0])
    stage[...] = jnp.zeros(stage.shape, F32)

    def spread_rows(ref):
        value = ref[...]
        rows = value.shape[0]
        rows_of_64[pl.ds(0, rows, stride=2), :] = value
        rows_of_64[pl.ds(1, rows, stride=2), :] = swap_halves(value)

    spread_rows(one_ref)
    rest = 2 * one_ref.shape[0] - first
    low = low_lanes((rest, 128))
    stage[0:rest, :] = jnp.where(
        low, rows_of_64[0:rest, :], swap_halves(rows_of_64[first : first + rest, :])
    )
    stage[rest:first, :] = rows_of_64[rest:first, :]
    spread_rows(two_ref)
    value = rows_of_64[0:two, :]
    spread_rows(three_ref)
    stage[first : first + two, :] = jnp.where(
        low_lanes((two, 128)), value, swap_halves(rows_of_64[0:two, :])
    )
    stage[first + two : first + two + four, :] = four_ref[...]
    out_ref[...] = stage[...].astype(BF16)


def run_pack(held, weights):
    return pl.pallas_call(
        pack_kernel,
        out_shape=pltpu.VMEM((held, 128), BF16),
        scratch_shapes=[pltpu.VMEM((held, 128), F32), pltpu.VMEM((80, 128), F32)],
        cost_estimate=pl.CostEstimate(flops=8192, bytes_accessed=48 * 1024, transcendentals=0),
        name="pack",
    )(*in_hbm(*weights))


def pair_inside(sizes_ref, image):
    shape = (HALF, SIDE, 128)
    row = lax.broadcasted_iota(jnp.int32, shape, 0)
    col = lax.broadcasted_iota(jnp.int32, shape, 1)
    inside = (row < sizes_ref[0, image] // 2) & (col < sizes_ref[1, image])
    return jnp.where(inside, 1.0, 0.0).reshape(ROWS, 128)


def pooled_inside(sizes_ref, step):
    spot = lax.broadcasted_iota(jnp.int32, (HALF * HALF, C), 0)
    return (spot < sizes_ref[0, step] * (HALF // 2)) & (
        jnp.bitwise_and(spot, HALF - 1) < sizes_ref[1, step] // 2
    )


def spread_kernel(sizes_ref, bias_ref, og_ref, spread_ref, bias_rows_ref):
    parts = [bias_ref[:, at : at + 128] for at in (0, 128, 256)]
    last = jnp.concatenate([bias_ref[:, 384:448], jnp.zeros((1, HID), F32)], axis=1)
    parts.append(last)
    turned = [swap_halves(part) for part in parts]
    low = low_lanes((1, 128))
    zero = jnp.zeros((1, 128), F32)
    rows = [
        (jnp.where(low, parts[0], turned[0]), zero),
        (jnp.where(low, turned[0], parts[0]), zero),
        (jnp.where(low, parts[1], turned[1]), zero),
        (jnp.where(low, turned[1], turned[2]), jnp.where(low, turned[2], turned[3])),
    ]
    for row, pair in enumerate(rows):
        bias_rows_ref[row : row + 1, :] = jnp.concatenate(pair, axis=1)
    total = jnp.zeros((1, C), F32)
    pix = lax.broadcasted_iota(jnp.int32, (256, 128), 0)
    spot = lax.broadcasted_iota(jnp.int32, (256, 128), 1)
    spread_up = jnp.where(pix // 2 == spot, 1.0, 0.0).astype(BF16)
    for image in range(og_ref.shape[0]):
        cot = jnp.where(
            pooled_inside(sizes_ref, image),
            og_ref[image].reshape(HALF * HALF, C).astype(F32),
            0.0,
        )
        total = total + jnp.sum(cot, axis=0, keepdims=True)
        cot = cot.astype(BF16)
        for half in range(2):
            value = dot(spread_up, cot[half * 128 : (half + 1) * 128])
            spread_ref[image, half * 256 : (half + 1) * 256, :] = value.astype(BF16)
    bias_rows_ref[4:8, :] = jnp.concatenate([total * GAIN, jnp.zeros((3, C), F32)], axis=0)


def active_kernel(sizes_ref, img_ref, even_ref, odd_ref):
    step = pl.program_id(0)
    mask = pair_inside(sizes_ref, step)
    wide_mask = jnp.concatenate([mask, mask], axis=1)
    even_ref[step, ROWS : ROWS + PAD, :] = jnp.zeros((PAD, C), BF16)
    odd_ref[step, 0:PAD, :] = jnp.zeros((PAD, C), BF16)
    for parity, act, at in ((0, even_ref, 0), (1, odd_ref, PAD)):
        base = img_ref[0, :, parity].reshape(ROWS, C).astype(F32)
        act[step, at : at + ROWS, :] = (silu(base) * wide_mask).astype(BF16)


def in_vmem(*arrays):
    return [pltpu.with_memory_space_constraint(array, pltpu.VMEM) for array in arrays]


def in_hbm(*arrays):
    return [pltpu.with_memory_space_constraint(array, pltpu.HBM) for array in arrays]


def block_of(shape):
    rest = (0,) * (len(shape) - 1)
    return pl.BlockSpec(shape, lambda i: (i,) + rest)


def whole(shape):
    return pl.BlockSpec(shape, lambda i: (0,) * len(shape))


def run_spread(sizes, biases, out_grad):
    count = out_grad.shape[0]
    vmem = pl.BlockSpec(memory_space=pltpu.VMEM)
    return pl.pallas_call(
        spread_kernel,
        in_specs=[pl.BlockSpec(memory_space=pltpu.SMEM), vmem, vmem],
        out_specs=[vmem, vmem],
        out_shape=[
            pltpu.VMEM((count, ROWS, C), BF16),
            pltpu.VMEM((8, C), F32),
        ],
        compiler_params=pltpu.CompilerParams(vmem_limit_bytes=SPREAD_BYTES),
        cost_estimate=pl.CostEstimate(
            flops=count * 2 * 512 * 128 * 256, bytes_accessed=count * 400_000, transcendentals=0
        ),
        name="spread",
    )(sizes, *in_hbm(biases, out_grad))


def run_active(sizes, images):
    count = images.shape[0]
    padded = ROWS + PAD
    return pl.pallas_call(
        active_kernel,
        grid=(count,),
        in_specs=[
            pl.BlockSpec(memory_space=pltpu.SMEM),
            block_of((1, HALF, 2, SIDE, C)),
        ],
        out_specs=[pl.BlockSpec(memory_space=pltpu.VMEM)] * 2,
        out_shape=[
            pltpu.VMEM((count, padded, C), BF16),
            pltpu.VMEM((count, padded, C), BF16),
        ],
        compiler_params=pltpu.CompilerParams(
            dimension_semantics=("arbitrary",), vmem_limit_bytes=ACTIVE_BYTES
        ),
        cost_estimate=pl.CostEstimate(
            flops=count * 3_000_000, bytes_accessed=count * 1_100_000, transcendentals=count * 262144
        ),
        name="active",
    )(sizes, *in_hbm(images))


def unpack_weights(shards, me_ref, pieces, stage, taps_one, taps_two, taps_three, taps_four):
    one, first, two, four = shard_layout(shards)
    held = pieces[0].shape[1]
    for which, piece in enumerate(pieces):
        group = piece.shape[0]
        stage[which * group * held : (which + 1) * group * held, :] = (
            piece[...].reshape(group * held, 128).astype(F32)
        )

    def place(shard, carry):
        owner = me_ref[0] ^ place_mask(shards, shard) if shards > 1 else shard
        start = pl.multiple_of(shard * held, 8)
        value = stage[pl.ds(start, first), :]
        at = pl.multiple_of(owner * one, 8)
        taps_one[pl.ds(at, first), :] = value
        taps_one[pl.ds(at + first, one - first), :] = swap_halves(value[0 : one - first])
        value = stage[pl.ds(start + first, two), :]
        taps_two[pl.ds(owner * two, two), :] = value
        taps_three[pl.ds(owner * two, two), :] = swap_halves(value)
        at = start + first + two
        for row in range(four // 2):
            row_at = owner * (four // 2) + row
            taps_four[0, pl.ds(row_at, 1), :] = stage[pl.ds(at + 2 * row, 1), :]
            taps_four[1, pl.ds(row_at, 1), :] = stage[pl.ds(at + 2 * row + 1, 1), :]
        return carry

    lax.fori_loop(0, shards, place, 0, unroll=UNROLL if shards > 1 else 1)


def tap_blocks(taps, width, col_tap):
    rows = [
        taps[(row_tap * 3 + col_tap) * width : (row_tap * 3 + col_tap + 1) * width, :]
        for row_tap in range(3)
    ]
    low = low_lanes((width, 128))
    zero = jnp.zeros((width, 128), F32)
    turned = [swap_halves(value) for value in rows]
    return (
        jnp.where(low, rows[0], zero),
        jnp.where(low, rows[1], turned[0]),
        jnp.where(low, rows[2], turned[1]),
        jnp.where(low, zero, turned[2]),
    )


def block_kernel(
    shards,
    me_ref,
    sizes_ref,
    bias_ref,
    even_ref,
    odd_ref,
    spread_ref,
    *refs,
):
    outs = 6
    pieces, refs = refs[: len(refs) - BLOCK_SCRATCH - outs], refs[len(refs) - BLOCK_SCRATCH - outs :]
    keep_ref, send_ref, turned_hbm, act_three_hbm, back_one_hbm, fwd_four_ref = refs[:outs]
    (
        turned_ref,
        act_three_ref,
        back_one_ref,
        sems,
        stage,
        taps_one,
        taps_two,
        taps_three,
        taps_four,
        fwd_one,
        fwd_two,
        back_two,
        fwd_three,
        back_three,
        back_four,
        act_one,
        act_two,
        slope_one,
        slope_two,
        turned,
        masks,
        shifts,
        sum_one,
        sum_two,
        sum_three,
        sum_four,
        sum_bias,
    ) = refs[outs:]
    images = even_ref.shape[0]
    for which in range(2 * images):
        none = jnp.zeros((HALF, EDGE, 128), F32)
        shifts[which, :, 0:EDGE, :] = none
        shifts[which, :, EDGE + SIDE : 2 * EDGE + SIDE, :] = none
    stores = []

    def store(source, target):
        copy = pltpu.make_async_copy(source, target, sems.at[len(stores)])
        copy.start()
        stores.append(copy)

    unpack_weights(shards, me_ref, pieces, stage, taps_one, taps_two, taps_three, taps_four)
    for col_tap in range(3):
        lanes = slice(col_tap * 128, (col_tap + 1) * 128)
        more = slice(384 + col_tap * 128, 384 + (col_tap + 1) * 128)
        blocks = tap_blocks(taps_one, C, col_tap)
        for place, block in enumerate(blocks):
            fwd_one[place * C : (place + 1) * C, lanes] = block.astype(BF16)
        back_one_ref[lanes, 0:C] = (0.5 * blocks[1]).T.astype(BF16)
        back_one_ref[lanes, C : 2 * C] = (0.5 * blocks[2]).T.astype(BF16)
        back_one_ref[more, 0:C] = (0.5 * blocks[3]).T.astype(BF16)
        back_one_ref[more, C : 2 * C] = (0.5 * blocks[0]).T.astype(BF16)
        for taps, fwd, back in (
            (taps_two, fwd_two, back_two),
            (taps_three, fwd_three, back_three),
        ):
            blocks = tap_blocks(taps, HID, col_tap)
            for place, which in enumerate((1, 2, 3, 0)):
                fwd[place * HID : (place + 1) * HID, lanes] = blocks[which].astype(BF16)
            here = jnp.concatenate([blocks[1], blocks[2]], axis=0).T
            around = jnp.concatenate([blocks[3], blocks[0]], axis=0).T
            back[lanes, 0:128] = (0.5 * here).astype(BF16)
            back[lanes, 128:256] = (0.5 * around).astype(BF16)
    four = jnp.concatenate([taps_four[0], taps_four[1]], axis=1)
    both = jnp.concatenate([four, four], axis=0)
    fwd_four_ref[...] = both.astype(BF16)
    back_four[...] = (0.5 * both).T.astype(BF16)
    store(back_one_ref, back_one_hbm)

    low = low_lanes((ROWS, 128))
    low_wide = jnp.concatenate([low, low, low], axis=1)

    def rows_before(value):
        return jnp.concatenate([jnp.zeros((PAD, value.shape[1]), value.dtype), value[:-PAD]], axis=0)

    def rows_after(value):
        return jnp.concatenate([value[PAD:], jnp.zeros((PAD, value.shape[1]), value.dtype)], axis=0)

    def add_to(total, value, slot):
        total[...] = value if slot == 0 else total[...] + value

    def image_phases(slot):
        masks[slot] = pair_inside(sizes_ref, slot)
        first, second, around_grad = act_one.at[slot], act_two.at[slot], turned.at[slot]
        left, right = shifts.at[2 * slot], shifts.at[2 * slot + 1]

        def by_rows(value):
            return value.reshape(HALF, SIDE, 128)

        def shift_sum(parts):
            left[:, EDGE : EDGE + SIDE, :] = by_rows(parts[:, 0:128])
            right[:, EDGE : EDGE + SIDE, :] = by_rows(parts[:, 256:384])
            before = left[:, EDGE - 1 : EDGE - 1 + SIDE, :]
            after = right[:, EDGE + 1 : EDGE + 1 + SIDE, :]
            return (before + by_rows(parts[:, 128:256]) + after).reshape(ROWS, 128)

        def activate(conv):
            active, slope = silu_and_slope(conv)
            return (active * masks[slot]).astype(BF16), slope * masks[slot]

        def keep_active(act, active):
            act[:, 0:128] = active
            act[:, 128:256] = jnp.where(low, rows_after(active), rows_before(active))

        def turn(grad, row, into):
            add_to(sum_bias.at[row : row + 1, 0:128], jnp.sum(grad, axis=0, keepdims=True), slot)
            left[:, EDGE : EDGE + SIDE, :] = by_rows(grad)
            parts = (
                left[:, EDGE + 1 : EDGE + 1 + SIDE, :].reshape(ROWS, 128),
                grad,
                left[:, EDGE - 1 : EDGE - 1 + SIDE, :].reshape(ROWS, 128),
            )
            value = jnp.concatenate([part.astype(BF16) for part in parts], axis=1)
            into[:, 0:384] = value
            return value

        def back_through(window, kernel):
            parts = dot(window, kernel)
            around = parts[:, 128:256]
            return parts[:, 0:128], around

        def back_sum(pair):
            here, around = pair
            return here + jnp.where(low, rows_before(around), rows_after(around))

        window = jnp.concatenate(
            [
                odd_ref[slot, 0:ROWS, :],
                even_ref[slot, 0:ROWS, :],
                odd_ref[slot, PAD : PAD + ROWS, :],
                even_ref[slot, PAD : PAD + ROWS, :],
            ],
            axis=1,
        )
        parts = dot(window, fwd_one[...])
        yield
        active, slope = activate(shift_sum(parts) + bias_ref[0:1, 0:128])
        keep_active(first, active)
        slope_one[slot] = slope
        yield
        parts = dot(first[...], fwd_two[...])
        yield
        active, slope = activate(shift_sum(parts) + bias_ref[1:2, 0:128])
        keep_active(second, active)
        slope_two[slot] = slope
        yield
        parts = dot(second[...], fwd_three[...])
        back = dot(spread_ref[slot], back_four[...])
        yield
        active, slope = activate(shift_sum(parts) + bias_ref[2:3, 0:128])
        act_three_ref[slot] = active
        turn(back * (GAIN * 0.25) * slope, 2, around_grad)
        yield
        back = back_through(around_grad[:, 0:384], back_three[...])
        add_to(sum_four, dot_rows(spread_ref[slot], act_three_ref[slot]), slot)
        add_to(sum_three, dot_rows(second[...], around_grad[:, 0:384]), slot)
        store(act_three_ref.at[slot], act_three_hbm.at[slot])
        yield
        turn(back_sum(back) * slope_two[slot], 1, around_grad)
        yield
        back = back_through(around_grad[:, 0:384], back_two[...])
        add_to(sum_two, dot_rows(first[...], around_grad[:, 0:384]), slot)
        yield
        window = turn(back_sum(back) * slope_one[slot], 0, turned_ref.at[slot])
        turned_ref[slot, :, 384:768] = jnp.where(low_wide, rows_after(window), rows_before(window))
        yield
        store(turned_ref.at[slot], turned_hbm.at[slot])
        if slot % MERGE == MERGE - 1 or slot == images - 1:
            first_slot = slot - slot % MERGE
            slots = range(first_slot, slot + 1)
            both = jnp.concatenate(
                [
                    jnp.concatenate(
                        [even_ref[at, 0:ROWS, :], odd_ref[at, PAD : PAD + ROWS, :]], axis=1
                    )
                    for at in slots
                ],
                axis=0,
            )
            window = turned_ref[first_slot : slot + 1].reshape(len(slots) * ROWS, 768)
            add_to(sum_one, dot_rows(both, window), first_slot)

    waiting = [image_phases(slot) for slot in range(images)]
    turn_number = 0
    while waiting:
        for place, phases in enumerate(list(waiting)):
            if turn_number >= LAG * place or len(waiting) < images:
                if next(phases, waiting) is waiting:
                    waiting.remove(phases)
        turn_number += 1

    for col_tap in range(3):
        here = slice(col_tap * 128, (col_tap + 1) * 128)
        around = slice(384 + col_tap * 128, 384 + (col_tap + 1) * 128)
        even_here, even_around = sum_one[0:C, here], sum_one[0:C, around]
        odd_here, odd_around = sum_one[C : 2 * C, here], sum_one[C : 2 * C, around]
        for row_tap, value in (
            (0, swap_halves(even_here) + odd_around),
            (1, even_here + swap_halves(odd_here)),
            (2, swap_halves(even_around) + odd_here),
        ):
            at = (row_tap * 3 + col_tap) * C
            taps_one[at : at + C, :] = value
        for total, taps in ((sum_two, taps_two), (sum_three, taps_three)):
            even_here, odd_here, even_next, odd_before = (
                total[part * HID : (part + 1) * HID, here] for part in range(4)
            )
            for row_tap, value in (
                (0, swap_halves(even_here) + odd_before),
                (1, even_here + swap_halves(odd_here)),
                (2, odd_here + swap_halves(even_next)),
            ):
                at = (row_tap * 3 + col_tap) * HID
                taps[at : at + HID, :] = value
    last = sum_four[...].T * (GAIN * 0.25)
    last = last[0:HID, :] + last[HID:128, :]
    taps_four[0] = last[:, 0:128]
    taps_four[1] = last[:, 128:256]
    sums = sum_bias[...]
    tail = sums[:, 0:128]
    tail = tail + swap_halves(tail)
    outer = bias_ref[4:5, :]
    outer = (outer[:, 0:128], outer[:, 128:256])
    bias_high = jnp.concatenate(
        [
            tail[0:3],
            swap_halves(outer[0]),
            outer[0],
            swap_halves(outer[1]),
            outer[1],
            jnp.zeros((1, 128), F32),
        ],
        axis=0,
    )
    one, first, two, four = shard_layout(shards)
    held = shard_held(shards)
    gap = 2 * first - one - 8

    def collect(place, carry):
        start = pl.multiple_of(place * held, 8)
        shard = place
        if shards > 1:
            half = jnp.bitwise_xor(place // (shards // 2), jnp.bitwise_and(me_ref[0], 1))
            shard = 2 * lax.rem(place, shards // 2) + half
        at = pl.multiple_of(shard * one, 8)
        high = [swap_halves(taps_one[pl.ds(at + first, one - first), :])]
        if gap:
            high.append(jnp.zeros((gap, 128), F32))
        stage[pl.ds(start, first), :] = jnp.where(
            low_lanes((first, 128)),
            taps_one[pl.ds(at, first), :],
            jnp.concatenate(high + [bias_high], axis=0),
        )
        stage[pl.ds(start + first, two), :] = jnp.where(
            low_lanes((two, 128)),
            taps_two[pl.ds(shard * two, two), :],
            swap_halves(taps_three[pl.ds(shard * two, two), :]),
        )
        at = start + first + two
        for row in range(four // 2):
            row_at = shard * (four // 2) + row
            stage[pl.ds(at + 2 * row, 1), :] = taps_four[0, pl.ds(row_at, 1), :]
            stage[pl.ds(at + 2 * row + 1, 1), :] = taps_four[1, pl.ds(row_at, 1), :]
        return carry

    lax.fori_loop(0, shards, collect, 0, unroll=UNROLL if shards > 1 else 1)
    rows = keep_ref.shape[0] * held
    keep_ref[...] = stage[0:rows, :].reshape(keep_ref.shape).astype(keep_ref.dtype)
    send_ref[...] = stage[shards * held - rows :, :].reshape(send_ref.shape).astype(BF16)
    for copy in stores:
        copy.wait()


BLOCK_SCRATCH = 27


def run_block(shards, me, sizes, bias_rows, even, odd, spread, pieces):
    count = even.shape[0]
    held = pieces[0].shape[1]
    part = max(shards // 2, 1)
    smem = pl.BlockSpec(memory_space=pltpu.SMEM)
    hbm = pl.BlockSpec(memory_space=pl.ANY)
    inside = pl.BlockSpec(memory_space=pltpu.VMEM)
    vmem = pltpu.VMEM
    place = pltpu.VMEM if shards > 1 else pltpu.HBM
    return pl.pallas_call(
        functools.partial(block_kernel, shards),
        in_specs=[smem, smem, *[inside] * (4 + len(pieces))],
        out_specs=[inside, inside, hbm, hbm, hbm, inside],
        out_shape=[
            place((part, held, 128), KEEP_TYPE if shards > 1 else F32),
            place((part, held, 128), BF16),
            pltpu.HBM((count, ROWS, 768), BF16),
            pltpu.HBM((count, ROWS, 128), BF16),
            pltpu.HBM((768, 2 * C), BF16),
            pltpu.HBM((128, C), BF16),
        ],
        scratch_shapes=[
            vmem((count, ROWS, 768), BF16),
            vmem((count, ROWS, 128), BF16),
            vmem((768, 2 * C), BF16),
            pltpu.SemaphoreType.DMA((2 * count + 1,)),
            vmem((shards * held, 128), F32),
            vmem((9 * C, 128), F32),
            vmem((9 * HID, 128), F32),
            vmem((9 * HID, 128), F32),
            vmem((2, HID, 128), F32),
            vmem((4 * C, 384), BF16),
            vmem((4 * HID, 384), BF16),
            vmem((384, 256), BF16),
            vmem((4 * HID, 384), BF16),
            vmem((384, 256), BF16),
            vmem((C, 128), BF16),
            vmem((count, ROWS, 256), BF16),
            vmem((count, ROWS, 256), BF16),
            vmem((count, ROWS, 128), F32),
            vmem((count, ROWS, 128), F32),
            vmem((count, ROWS, 384), BF16),
            vmem((count, ROWS, 128), F32),
            vmem((2 * count, HALF, SIDE + 2 * EDGE, 128), F32),
            vmem((2 * C, 768), F32),
            vmem((256, 384), F32),
            vmem((256, 384), F32),
            vmem((C, 128), F32),
            vmem((8, C), F32),
        ],
        compiler_params=pltpu.CompilerParams(vmem_limit_bytes=BLOCK_BYTES),
        cost_estimate=pl.CostEstimate(
            flops=count * 1_200_000_000, bytes_accessed=count * 2_000_000, transcendentals=count * 196608
        ),
        name="block",
    )(me, sizes, *(in_vmem if shards > 1 else in_hbm)(bias_rows, even, odd, spread, *pieces))


def finish_kernel(
    sizes_ref, bias_ref, img_ref, spread_ref, turned_ref, act_ref, back_ref, four_ref, out_ref, grad_ref
):
    step = pl.program_id(0)
    mask = pair_inside(sizes_ref, step)
    wide_mask = jnp.concatenate([mask, mask], axis=1)
    spot = lax.broadcasted_iota(jnp.int32, (128, 256), 0)
    pix = lax.broadcasted_iota(jnp.int32, (128, 256), 1)
    pool_down = jnp.where(pix // 2 == spot, 0.25, 0.0).astype(BF16)
    pieces = []
    for half in range(2):
        rows = slice(half * 256, (half + 1) * 256)
        base_mean = dot(pool_down, img_ref[0, :, 0].reshape(ROWS, C)[rows]) + dot(
            pool_down, img_ref[0, :, 1].reshape(ROWS, C)[rows]
        )
        act_mean = dot(pool_down, act_ref[0, rows, :]).astype(BF16)
        pieces.append(base_mean + GAIN * (dot(act_mean, four_ref[...]) + bias_ref[3:4, :]))
    result = jnp.where(pooled_inside(sizes_ref, step), jnp.concatenate(pieces, axis=0), 0.0)
    out_ref[0] = result.reshape(HALF, HALF, C).astype(BF16)
    spread = 0.25 * spread_ref[0].astype(F32)
    back = dot(turned_ref[0], back_ref[...])
    for parity in range(2):
        _, slope = silu_and_slope(img_ref[0, :, parity].reshape(ROWS, C).astype(F32))
        slope = slope * wide_mask
        value = spread + back[:, parity * C : (parity + 1) * C] * slope
        grad_ref[0, :, parity] = value.reshape(HALF, SIDE, C).astype(BF16)


def run_finish(sizes, bias_rows, images, spread, turned, act_three, back_one, fwd_four):
    count = images.shape[0]
    return pl.pallas_call(
        finish_kernel,
        grid=(count,),
        in_specs=[
            pl.BlockSpec(memory_space=pltpu.SMEM),
            whole((8, C)),
            block_of((1, HALF, 2, SIDE, C)),
            block_of((1, ROWS, C)),
            block_of((1, ROWS, 768)),
            block_of((1, ROWS, 128)),
            whole((768, 2 * C)),
            whole((128, C)),
        ],
        out_specs=[block_of((1, HALF, HALF, C)), block_of((1, HALF, 2, SIDE, C))],
        out_shape=[
            jax.ShapeDtypeStruct((count, HALF, HALF, C), BF16),
            jax.ShapeDtypeStruct((count, HALF, 2, SIDE, C), BF16),
        ],
        compiler_params=pltpu.CompilerParams(
            dimension_semantics=("arbitrary",), vmem_limit_bytes=60 * 1024 * 1024
        ),
        cost_estimate=pl.CostEstimate(
            flops=count * 450_000_000, bytes_accessed=count * 2_500_000, transcendentals=count * 262144
        ),
        name="finish",
    )(sizes, *in_hbm(bias_rows, images, spread, turned, act_three, back_one, fwd_four))


def adamw_update(weight, gradient, first_old, second_old, step_rate):
    first_new = BETA_ONE * first_old + (1.0 - BETA_ONE) * gradient
    second_new = BETA_TWO * second_old + (1.0 - BETA_TWO) * gradient * gradient
    first_hat = first_new / (1.0 - BETA_ONE**STEP)
    second_hat = second_new / (1.0 - BETA_TWO**STEP)
    weight_new = weight - step_rate * (
        first_hat / (jnp.sqrt(second_hat) + EPSILON) + DECAY * weight
    )
    return (first_new, second_new, weight_new, weight_new.astype(BF16))


RATES = ((9.0 * C) ** (-0.5), (9.0 * HID) ** (-0.5), (9.0 * HID) ** (-0.5), 8.0)


def update_kernel(moved_ref, *refs):
    olds, news, total, rows_of_64 = refs[:15], refs[15:35], refs[35], refs[36]
    total[...] = jnp.sum(moved_ref[...].astype(F32), axis=0)
    one, first, two, four = shard_layout(COMPACT[0] // olds[0].shape[0])

    def joined(rows):
        return jnp.where(
            low_lanes((rows, 128)),
            rows_of_64[pl.ds(0, rows, stride=2), :],
            swap_halves(rows_of_64[pl.ds(1, rows, stride=2), :]),
        )

    rows_of_64[0:first, :] = total[0:first, :]
    rows_of_64[first:one, :] = swap_halves(total[0 : one - first, :])
    gradients = [joined(one // 2)]
    rows_of_64[0:two, :] = total[first : first + two, :]
    gradients.append(joined(two // 2))
    rows_of_64[0:two, :] = swap_halves(total[first : first + two, :])
    gradients.append(joined(two // 2))
    gradients.append(total[first + two : first + two + four, :])
    rows = total[first - 8 : first, :]
    turned = swap_halves(rows)
    low = low_lanes((1, 128))
    parts = [jnp.where(low, turned[row : row + 1], rows[row + 1 : row + 2]) for row in (0, 2, 4)]
    parts.append(turned[6:7])
    gradients.append(jnp.concatenate(parts, axis=1)[:, 0:BIASES])
    rate = jnp.where(lax.broadcasted_iota(jnp.int32, (1, BIASES), 1) < 3 * HID, 0.5, 32.0)
    for which, gradient in enumerate(gradients):
        weight, first_old, second_old = (ref[...] for ref in olds[3 * which : 3 * which + 3])
        values = adamw_update(
            weight, gradient, first_old, second_old, rate if which == 4 else RATES[which]
        )
        for ref, value in zip(news[4 * which : 4 * which + 4], values):
            ref[...] = value.reshape(ref.shape)


def run_update(moved, olds):
    shapes = []
    for which in range(5):
        shape = olds[3 * which].shape
        low_shape = shape if which < 4 else shape[1:]
        shapes += [jax.ShapeDtypeStruct(shape, F32)] * 3 + [jax.ShapeDtypeStruct(low_shape, BF16)]
    return pl.pallas_call(
        update_kernel,
        out_shape=shapes,
        scratch_shapes=[pltpu.VMEM(moved.shape[1:], F32), pltpu.VMEM((80, 128), F32)],
        compiler_params=pltpu.CompilerParams(vmem_limit_bytes=UPDATE_MB * 1024 * 1024),
        cost_estimate=pl.CostEstimate(flops=500_000, bytes_accessed=700_000, transcendentals=8192),
        name="update",
    )(*in_vmem(moved), *in_hbm(*olds))


def exchange(value, mask, count):
    return lax.ppermute(value, AXES, [(i, i ^ mask) for i in range(count)])


def gather_shards(value, devices, beside):
    groups = bit_groups(devices)
    early, late = beside
    held = value[None]
    for low, top in groups[:-2]:
        parts = [held] + [
            exchange(held, mask << low, devices) for mask in range(1, 1 << (top - low))
        ]
        parts, early = lax.optimization_barrier((parts, early))
        held = jnp.concatenate(parts, axis=0)
    low, top = groups[-2]
    pieces = [exchange(held, mask << low, devices) for mask in range(1, 1 << (top - low))]
    pieces, late = lax.optimization_barrier((pieces, late))
    pieces = [held] + pieces
    return pieces + [exchange(piece, 1, devices) for piece in pieces], early, late


def bit_groups(devices):
    groups = []
    top = devices.bit_length() - 1
    while top > 1:
        low = max(top - 2, 1)
        groups.append((low, top))
        top = low
    groups.append((0, 1))
    return groups


def place_mask(devices, place):
    mask = 0
    for low, top in bit_groups(devices):
        width = top - low
        mask = mask | ((place & ((1 << width) - 1)) << low)
        place = place >> width
    return mask


def local(devices, *args):
    (
        images,
        image_sizes,
        out_grad,
        weight_one,
        first_one,
        second_one,
        weight_two,
        first_two,
        second_two,
        weight_three,
        first_three,
        second_three,
        weight_four,
        first_four,
        second_four,
        biases,
        first_bias,
        second_bias,
    ) = args
    weights = (weight_one, weight_two, weight_three, weight_four)
    olds = (
        (weight_one, first_one, second_one),
        (weight_two, first_two, second_two),
        (weight_three, first_three, second_three),
        (weight_four, first_four, second_four),
    )
    count = images.shape[0]
    image_sizes = image_sizes.T
    images = images.reshape(count, HALF, 2, SIDE, C)
    sizes = [weight.shape[0] for weight in weights]
    total = sum(sizes)
    packed = (
        all(size % 128 == 0 for size in sizes)
        and sizes[3] % 256 == 0
        and devices >= 8
        and devices & (devices - 1) == 0
    )
    me = lax.axis_index("dp") * lax.axis_size("fsdp") + lax.axis_index("fsdp")
    me = jnp.reshape(me, (1,)).astype(jnp.int32)
    shards = devices if packed else 1
    held = shard_held(shards)
    beside = (
        run_spread(image_sizes, biases.reshape(1, BIASES), out_grad),
        run_active(image_sizes, images),
    )
    if packed:
        mine = run_pack(held, [weight.reshape(-1, 128) for weight in weights])
        pieces, *beside = gather_shards(mine, devices, beside)
    else:
        low = jnp.concatenate([weight.astype(BF16) for weight in weights])
        full = lax.all_gather(low, AXES, axis=0, tiled=False)
        parts = []
        at = 0
        for size in sizes:
            parts.append(full[:, at : at + size].reshape(-1))
            at += size
        one, first, two, four = shard_layout(1)
        rows = parts[0].reshape(one, HID)
        rows = jnp.concatenate(
            [rows[:first], jnp.pad(rows[first:], ((0, 2 * first - one), (0, 0)))], axis=1
        )
        both = jnp.concatenate([part.reshape(two, HID) for part in parts[1:3]], axis=1)
        full = jnp.concatenate([rows, both, parts[3].reshape(four, 128)], axis=0)
        pieces = [jnp.pad(full, ((0, held - full.shape[0]), (0, 0)))[None]]
    (spread, bias_rows), (even, odd) = beside
    keep, send, turned, act_three, back_one, fwd_four = run_block(
        shards, me, image_sizes, bias_rows, even, odd, spread, pieces
    )
    if packed:
        merged = (keep + exchange(send, 1, devices).astype(F32)).astype(BF16)
        merged, turned = lax.optimization_barrier((merged, turned))
        groups = [list(range(core, devices, 2)) for core in range(2)]
        moved = lax.all_to_all(merged, AXES, 0, 0, axis_index_groups=groups, tiled=False)
    block_out, image_grad = run_finish(
        image_sizes, bias_rows, images, spread, turned, act_three, back_one, fwd_four
    )
    image_grad = image_grad.reshape(count, SIDE, SIDE, C)
    if packed:
        flat = [array.reshape(-1, 128) for three in olds for array in three]
        flat += [array.reshape(1, BIASES) for array in (biases, first_bias, second_bias)]
        updates = [array.reshape(-1) for array in run_update(moved, flat)]
        return (block_out, image_grad, *updates)
    rows = keep[0]
    one, first, two, four = shard_layout(1)
    parts = [
        jnp.concatenate([rows[:first, :HID], rows[: one - first, HID:]], axis=0),
        rows[first : first + two, :HID],
        rows[first : first + two, HID:],
        rows[first + two : first + two + four],
    ]
    parts = [part.reshape(devices, -1) for part in parts]
    bias_part = rows[first - 8 : first - 1, HID:].reshape(-1)
    bias_total = lax.psum(bias_part, AXES)
    summed = lax.psum_scatter(
        jnp.concatenate(parts, axis=1).reshape(-1), AXES, scatter_dimension=0, tiled=True
    )
    updates = []
    at = 0
    for (weight, first, second), rate, size in zip(olds, RATES, sizes):
        updates += list(adamw_update(weight, summed[at : at + size], first, second, rate))
        at += size
    bias_rates = jnp.where(jnp.arange(BIASES) < 3 * HID, 0.5, 32.0)
    updates += list(adamw_update(biases, bias_total, first_bias, second_bias, bias_rates))
    return (block_out, image_grad, *updates)


def solution(mesh):
    devices = mesh.shape["dp"] * mesh.shape["fsdp"]
    split = P(AXES)
    return jax.shard_map(
        functools.partial(local, devices),
        mesh=mesh,
        in_specs=(
            P(AXES, None, None, None),
            P(AXES, None),
            P(AXES, None, None, None),
            *([split] * 12),
            P(),
            P(),
            P(),
        ),
        out_specs=(
            P(AXES, None, None, None),
            P(AXES, None, None, None),
            *([split] * 16),
            P(),
            P(),
            P(),
            P(),
        ),
        check_vma=False,
    )
```

```python
import functools

import jax
import jax.numpy as jnp
from jax import lax
from jax.experimental import pallas as pl
from jax.experimental.pallas import tpu as pltpu
from jax.sharding import PartitionSpec as P

C = 256
HID = 64
STEP = 10
SIDE = 32
HALF = SIDE // 2
ROWS = HALF * SIDE
PAD = SIDE

GAIN = 1.0 / 64.0
BETA_ONE = 0.9
BETA_TWO = 0.999
DECAY = 0.01
EPSILON = 1e-08
AXES = ("dp", "fsdp")
UNROLL = 16
SPREAD_BYTES = 58 * 1024 * 1024
ACTIVE_BYTES = 56 * 1024 * 1024
BLOCK_BYTES = 40 * 1024 * 1024
FINISH_BYTES = 24 * 1024 * 1024
FOLD_BYTES = 24 * 1024 * 1024
FINISH_SPLIT = 2
CHUNK = 64
LAG = 1
MERGE = 2
EDGE = 8
KEEP_TYPE = jnp.float32

COMPACT = (9 * C * HID // 128, 9 * HID * HID // 128, 9 * HID * HID // 128, HID * C // 128)
BIASES = 3 * HID + C

F32 = jnp.float32
BF16 = jnp.bfloat16


def silu(value):
    half = 0.5 * value
    return half * (1.0 + jnp.tanh(half))


def silu_and_slope(value):
    half = 0.5 * value
    turn = jnp.tanh(half)
    above = 1.0 + turn
    return half * above, above + half * (1.0 - turn * turn)


def dot(left, right):
    return jnp.dot(left, right, preferred_element_type=F32)


def dot_rows(left, right):
    return lax.dot_general(left, right, (((0,), (0,)), ((), ())), preferred_element_type=F32)


def swap_halves(value):
    return pltpu.roll(value, HID, 1)


def low_lanes(shape):
    return lax.broadcasted_iota(jnp.int32, shape, 1) < HID


def shard_layout(shards):
    one, two, three, four = (rows // shards for rows in COMPACT)
    first = -(-(one + 4) // 8) * 8
    return 2 * one, first, 2 * two, four


def shard_held(shards):
    _, first, two, four = shard_layout(shards)
    return -(-(first + two + four) // 16) * 16


def pack_kernel(one_ref, two_ref, three_ref, four_ref, out_ref, stage, rows_of_64):
    _, first, two, four = shard_layout(COMPACT[0] // one_ref.shape[0])
    stage[...] = jnp.zeros(stage.shape, F32)

    def spread_rows(ref):
        value = ref[...]
        rows = value.shape[0]
        rows_of_64[pl.ds(0, rows, stride=2), :] = value
        rows_of_64[pl.ds(1, rows, stride=2), :] = swap_halves(value)

    spread_rows(one_ref)
    rest = 2 * one_ref.shape[0] - first
    low = low_lanes((rest, 128))
    stage[0:rest, :] = jnp.where(
        low, rows_of_64[0:rest, :], swap_halves(rows_of_64[first : first + rest, :])
    )
    stage[rest:first, :] = rows_of_64[rest:first, :]
    spread_rows(two_ref)
    value = rows_of_64[0:two, :]
    spread_rows(three_ref)
    stage[first : first + two, :] = jnp.where(
        low_lanes((two, 128)), value, swap_halves(rows_of_64[0:two, :])
    )
    stage[first + two : first + two + four, :] = four_ref[...]
    out_ref[...] = stage[...].astype(BF16)


def run_pack(held, weights):
    return pl.pallas_call(
        pack_kernel,
        out_shape=pltpu.VMEM((held, 128), BF16),
        scratch_shapes=[pltpu.VMEM((held, 128), F32), pltpu.VMEM((80, 128), F32)],
        cost_estimate=pl.CostEstimate(flops=8192, bytes_accessed=48 * 1024, transcendentals=0),
        name="pack",
    )(*in_hbm(*weights))


def pair_inside(sizes_ref, image):
    shape = (HALF, SIDE, 128)
    row = lax.broadcasted_iota(jnp.int32, shape, 0)
    col = lax.broadcasted_iota(jnp.int32, shape, 1)
    inside = (row < sizes_ref[0, image] // 2) & (col < sizes_ref[1, image])
    return jnp.where(inside, 1.0, 0.0).reshape(ROWS, 128)


def pooled_inside(sizes_ref, step):
    spot = lax.broadcasted_iota(jnp.int32, (HALF * HALF, C), 0)
    return (spot < sizes_ref[0, step] * (HALF // 2)) & (
        jnp.bitwise_and(spot, HALF - 1) < sizes_ref[1, step] // 2
    )


def spread_kernel(sizes_ref, bias_ref, og_ref, spread_ref, bias_rows_ref):
    parts = [bias_ref[:, at : at + 128] for at in (0, 128, 256)]
    last = jnp.concatenate([bias_ref[:, 384:448], jnp.zeros((1, HID), F32)], axis=1)
    parts.append(last)
    turned = [swap_halves(part) for part in parts]
    low = low_lanes((1, 128))
    zero = jnp.zeros((1, 128), F32)
    rows = [
        (jnp.where(low, parts[0], turned[0]), zero),
        (jnp.where(low, turned[0], parts[0]), zero),
        (jnp.where(low, parts[1], turned[1]), zero),
        (jnp.where(low, turned[1], turned[2]), jnp.where(low, turned[2], turned[3])),
    ]
    for row, pair in enumerate(rows):
        bias_rows_ref[row : row + 1, :] = jnp.concatenate(pair, axis=1)
    total = jnp.zeros((1, C), F32)
    pix = lax.broadcasted_iota(jnp.int32, (256, 128), 0)
    spot = lax.broadcasted_iota(jnp.int32, (256, 128), 1)
    spread_up = jnp.where(pix // 2 == spot, 1.0, 0.0).astype(BF16)
    for image in range(og_ref.shape[0]):
        cot = jnp.where(
            pooled_inside(sizes_ref, image),
            og_ref[image].reshape(HALF * HALF, C).astype(F32),
            0.0,
        )
        total = total + jnp.sum(cot, axis=0, keepdims=True)
        cot = cot.astype(BF16)
        for half in range(2):
            value = dot(spread_up, cot[half * 128 : (half + 1) * 128])
            spread_ref[image, half * 256 : (half + 1) * 256, :] = value.astype(BF16)
    bias_rows_ref[4:8, :] = jnp.concatenate([total * GAIN, jnp.zeros((3, C), F32)], axis=0)


def active_kernel(sizes_ref, img_ref, even_ref, odd_ref, mask_ref):
    step = pl.program_id(0)
    mask = pair_inside(sizes_ref, step)
    mask_ref[step] = mask
    wide_mask = jnp.concatenate([mask, mask], axis=1)
    for parity, act in ((0, even_ref), (1, odd_ref)):
        base = img_ref[0, :, parity].reshape(ROWS, C).astype(F32)
        act[step] = (silu(base) * wide_mask).astype(BF16)


def in_vmem(*arrays):
    return [pltpu.with_memory_space_constraint(array, pltpu.VMEM) for array in arrays]


def in_hbm(*arrays):
    return [pltpu.with_memory_space_constraint(array, pltpu.HBM) for array in arrays]


def block_of(shape):
    rest = (0,) * (len(shape) - 1)
    return pl.BlockSpec(shape, lambda i: (i,) + rest)


def whole(shape):
    return pl.BlockSpec(shape, lambda i: (0,) * len(shape))


def run_spread(sizes, biases, out_grad):
    count = out_grad.shape[0]
    vmem = pl.BlockSpec(memory_space=pltpu.VMEM)
    return pl.pallas_call(
        spread_kernel,
        in_specs=[pl.BlockSpec(memory_space=pltpu.SMEM), vmem, vmem],
        out_specs=[vmem, vmem],
        out_shape=[
            pltpu.VMEM((count, ROWS, C), BF16),
            pltpu.VMEM((8, C), F32),
        ],
        compiler_params=pltpu.CompilerParams(vmem_limit_bytes=SPREAD_BYTES),
        cost_estimate=pl.CostEstimate(
            flops=count * 2 * 512 * 128 * 256, bytes_accessed=count * 400_000, transcendentals=0
        ),
        name="spread",
    )(sizes, *in_hbm(biases, out_grad))


def run_active(sizes, images):
    count = images.shape[0]
    return pl.pallas_call(
        active_kernel,
        grid=(count,),
        in_specs=[
            pl.BlockSpec(memory_space=pltpu.SMEM),
            block_of((1, HALF, 2, SIDE, C)),
        ],
        out_specs=[pl.BlockSpec(memory_space=pltpu.VMEM)] * 3,
        out_shape=[
            pltpu.VMEM((count, ROWS, C), BF16),
            pltpu.VMEM((count, ROWS, C), BF16),
            pltpu.VMEM((count, ROWS, 128), F32),
        ],
        compiler_params=pltpu.CompilerParams(
            dimension_semantics=("arbitrary",), vmem_limit_bytes=ACTIVE_BYTES
        ),
        cost_estimate=pl.CostEstimate(
            flops=count * 3_000_000, bytes_accessed=count * 1_100_000, transcendentals=count * 262144
        ),
        name="active",
    )(sizes, *in_hbm(images))


def unpack_weights(shards, me, pieces, stage, taps_one, taps_two, taps_three, taps_four):
    one, first, two, four = shard_layout(shards)
    held = pieces[0].shape[1]
    for which, piece in enumerate(pieces):
        group = piece.shape[0]
        stage[which * group * held : (which + 1) * group * held, :] = (
            piece[...].reshape(group * held, 128).astype(F32)
        )

    def place(shard, carry):
        owner = me ^ place_mask(shards, shard) if shards > 1 else shard
        start = pl.multiple_of(shard * held, 8)
        value = stage[pl.ds(start, first), :]
        at = pl.multiple_of(owner * one, 8)
        taps_one[pl.ds(at, first), :] = value
        taps_one[pl.ds(at + first, one - first), :] = swap_halves(value[0 : one - first])
        value = stage[pl.ds(start + first, two), :]
        taps_two[pl.ds(owner * two, two), :] = value
        taps_three[pl.ds(owner * two, two), :] = swap_halves(value)
        at = start + first + two
        for row in range(four // 2):
            row_at = owner * (four // 2) + row
            taps_four[0, pl.ds(row_at, 1), :] = stage[pl.ds(at + 2 * row, 1), :]
            taps_four[1, pl.ds(row_at, 1), :] = stage[pl.ds(at + 2 * row + 1, 1), :]
        return carry

    lax.fori_loop(0, shards, place, 0, unroll=UNROLL if shards > 1 else 1)


def tap_blocks(taps, width, col_tap):
    rows = [
        taps[(row_tap * 3 + col_tap) * width : (row_tap * 3 + col_tap + 1) * width, :]
        for row_tap in range(3)
    ]
    low = low_lanes((width, 128))
    zero = jnp.zeros((width, 128), F32)
    turned = [swap_halves(value) for value in rows]
    return (
        jnp.where(low, rows[0], zero),
        jnp.where(low, rows[1], turned[0]),
        jnp.where(low, rows[2], turned[1]),
        jnp.where(low, zero, turned[2]),
    )


def block_kernel(
    shards,
    fetched,
    bias_ref,
    even_ref,
    odd_ref,
    masks,
    spread_ref,
    img_hbm,
    *refs,
):
    olds, refs = refs[:fetched], refs[fetched:]
    outs = 7 + fetched
    cut = len(refs) - BLOCK_SCRATCH - outs
    pieces, refs = refs[:cut], refs[cut:]
    keep_ref, send_ref, turned_ref, act_three_ref, back_one_ref, fwd_four_ref, img_ref = refs[:7]
    news = refs[7:outs]
    (
        sems,
        stage,
        taps_one,
        taps_two,
        taps_three,
        taps_four,
        fwd_one,
        fwd_two,
        back_two,
        fwd_three,
        back_three,
        back_four,
        act_one,
        act_two,
        slope_one,
        slope_two,
        turned,
        shifts,
        sum_one,
        sum_two,
        sum_three,
        sum_four,
        sum_bias,
    ) = refs[outs:]
    images = even_ref.shape[0]
    fetches = [
        pltpu.make_async_copy(source, target, sems.at[which])
        for which, (source, target) in enumerate(zip((img_hbm, *olds), (img_ref, *news)))
    ]
    for fetch in fetches:
        fetch.start()
    for which in range(2 * images):
        none = jnp.zeros((HALF, EDGE, 128), F32)
        shifts[which, :, 0:EDGE, :] = none
        shifts[which, :, EDGE + SIDE : 2 * EDGE + SIDE, :] = none
    me = lax.axis_index(AXES) if shards > 1 else 0
    unpack_weights(shards, me, pieces, stage, taps_one, taps_two, taps_three, taps_four)
    for col_tap in range(3):
        lanes = slice(col_tap * 128, (col_tap + 1) * 128)
        more = slice(384 + col_tap * 128, 384 + (col_tap + 1) * 128)
        blocks = tap_blocks(taps_one, C, col_tap)
        fwd_one[0:C, lanes] = blocks[1].astype(BF16)
        fwd_one[C : 2 * C, lanes] = blocks[2].astype(BF16)
        fwd_one[0:C, more] = blocks[3].astype(BF16)
        fwd_one[C : 2 * C, more] = blocks[0].astype(BF16)
        back_one_ref[lanes, 0:C] = (0.5 * blocks[1]).T.astype(BF16)
        back_one_ref[lanes, C : 2 * C] = (0.5 * blocks[2]).T.astype(BF16)
        back_one_ref[more, 0:C] = (0.5 * blocks[3]).T.astype(BF16)
        back_one_ref[more, C : 2 * C] = (0.5 * blocks[0]).T.astype(BF16)
        for taps, fwd, back in (
            (taps_two, fwd_two, back_two),
            (taps_three, fwd_three, back_three),
        ):
            blocks = tap_blocks(taps, HID, col_tap)
            for place, which in enumerate((1, 2, 3, 0)):
                fwd[place * HID : (place + 1) * HID, lanes] = blocks[which].astype(BF16)
            here = jnp.concatenate([blocks[1], blocks[2]], axis=0).T
            around = jnp.concatenate([blocks[3], blocks[0]], axis=0).T
            back[lanes, 0:128] = (0.5 * here).astype(BF16)
            back[lanes, 128:256] = (0.5 * around).astype(BF16)
    four = jnp.concatenate([taps_four[0], taps_four[1]], axis=1)
    both = jnp.concatenate([four, four], axis=0)
    fwd_four_ref[...] = both.astype(BF16)
    back_four[...] = (0.5 * both).T.astype(BF16)

    low = low_lanes((ROWS, 128))
    low_wide = jnp.concatenate([low, low, low], axis=1)

    def rows_before(value):
        return jnp.concatenate([jnp.zeros((PAD, value.shape[1]), value.dtype), value[:-PAD]], axis=0)

    def rows_after(value):
        return jnp.concatenate([value[PAD:], jnp.zeros((PAD, value.shape[1]), value.dtype)], axis=0)

    def add_to(total, value, slot):
        total[...] = value if slot == 0 else total[...] + value

    def image_phases(slot):
        first, second, around_grad = act_one.at[slot], act_two.at[slot], turned.at[slot]
        left, right = shifts.at[2 * slot], shifts.at[2 * slot + 1]

        def by_rows(value):
            return value.reshape(HALF, SIDE, 128)

        def shift_sum(parts):
            left[:, EDGE : EDGE + SIDE, :] = by_rows(parts[:, 0:128])
            right[:, EDGE : EDGE + SIDE, :] = by_rows(parts[:, 256:384])
            before = left[:, EDGE - 1 : EDGE - 1 + SIDE, :]
            after = right[:, EDGE + 1 : EDGE + 1 + SIDE, :]
            return (before + by_rows(parts[:, 128:256]) + after).reshape(ROWS, 128)

        def activate(conv):
            active, slope = silu_and_slope(conv)
            return (active * masks[slot]).astype(BF16), slope * masks[slot]

        def keep_active(act, active):
            act[:, 0:128] = active
            act[:, 128:256] = jnp.where(low, rows_after(active), rows_before(active))

        def turn(grad, row, into):
            add_to(sum_bias.at[row : row + 1, 0:128], jnp.sum(grad, axis=0, keepdims=True), slot)
            left[:, EDGE : EDGE + SIDE, :] = by_rows(grad)
            parts = (
                left[:, EDGE + 1 : EDGE + 1 + SIDE, :].reshape(ROWS, 128),
                grad,
                left[:, EDGE - 1 : EDGE - 1 + SIDE, :].reshape(ROWS, 128),
            )
            value = jnp.concatenate([part.astype(BF16) for part in parts], axis=1)
            into[:, 0:384] = value
            return value

        def back_through(window, kernel):
            parts = dot(window, kernel)
            around = parts[:, 128:256]
            return parts[:, 0:128], around

        def back_sum(pair):
            here, around = pair
            return here + jnp.where(low, rows_before(around), rows_after(around))

        window = jnp.concatenate(
            [even_ref[slot], odd_ref[slot]], axis=1
        )
        parts = dot(window, fwd_one[...])
        yield
        parts = parts[:, 0:384] + jnp.where(
            low_wide, rows_before(parts[:, 384:768]), rows_after(parts[:, 384:768])
        )
        active, slope = activate(shift_sum(parts) + bias_ref[0:1, 0:128])
        keep_active(first, active)
        slope_one[slot] = slope
        yield
        parts = dot(first[...], fwd_two[...])
        yield
        active, slope = activate(shift_sum(parts) + bias_ref[1:2, 0:128])
        keep_active(second, active)
        slope_two[slot] = slope
        yield
        parts = dot(second[...], fwd_three[...])
        back = dot(spread_ref[slot], back_four[...])
        yield
        active, slope = activate(shift_sum(parts) + bias_ref[2:3, 0:128])
        act_three_ref[slot] = active
        turn(back * (GAIN * 0.25) * slope, 2, around_grad)
        yield
        back = back_through(around_grad[:, 0:384], back_three[...])
        add_to(sum_four, dot_rows(spread_ref[slot], act_three_ref[slot]), slot)
        add_to(sum_three, dot_rows(second[...], around_grad[:, 0:384]), slot)
        yield
        turn(back_sum(back) * slope_two[slot], 1, around_grad)
        yield
        back = back_through(around_grad[:, 0:384], back_two[...])
        add_to(sum_two, dot_rows(first[...], around_grad[:, 0:384]), slot)
        yield
        window = turn(back_sum(back) * slope_one[slot], 0, turned_ref.at[slot])
        turned_ref[slot, :, 384:768] = jnp.where(low_wide, rows_after(window), rows_before(window))
        yield
        if slot % MERGE == MERGE - 1 or slot == images - 1:
            first_slot = slot - slot % MERGE
            slots = range(first_slot, slot + 1)
            both = jnp.concatenate(
                [
                    jnp.concatenate(
                        [even_ref[at], odd_ref[at]], axis=1
                    )
                    for at in slots
                ],
                axis=0,
            )
            window = turned_ref[first_slot : slot + 1].reshape(len(slots) * ROWS, 768)
            add_to(sum_one, dot_rows(both, window), first_slot)

    waiting = [image_phases(slot) for slot in range(images)]
    turn_number = 0
    while waiting:
        for place, phases in enumerate(list(waiting)):
            if turn_number >= LAG * place or len(waiting) < images:
                if next(phases, waiting) is waiting:
                    waiting.remove(phases)
        turn_number += 1

    for col_tap in range(3):
        here = slice(col_tap * 128, (col_tap + 1) * 128)
        around = slice(384 + col_tap * 128, 384 + (col_tap + 1) * 128)
        even_here, even_around = sum_one[0:C, here], sum_one[0:C, around]
        odd_here, odd_around = sum_one[C : 2 * C, here], sum_one[C : 2 * C, around]
        for row_tap, value in (
            (0, swap_halves(even_here) + odd_around),
            (1, even_here + swap_halves(odd_here)),
            (2, swap_halves(even_around) + odd_here),
        ):
            at = (row_tap * 3 + col_tap) * C
            taps_one[at : at + C, :] = value
        for total, taps in ((sum_two, taps_two), (sum_three, taps_three)):
            even_here, odd_here, even_next, odd_before = (
                total[part * HID : (part + 1) * HID, here] for part in range(4)
            )
            for row_tap, value in (
                (0, swap_halves(even_here) + odd_before),
                (1, even_here + swap_halves(odd_here)),
                (2, odd_here + swap_halves(even_next)),
            ):
                at = (row_tap * 3 + col_tap) * HID
                taps[at : at + HID, :] = value
    last = sum_four[...].T * (GAIN * 0.25)
    last = last[0:HID, :] + last[HID:128, :]
    taps_four[0] = last[:, 0:128]
    taps_four[1] = last[:, 128:256]
    sums = sum_bias[...]
    tail = sums[:, 0:128]
    tail = tail + swap_halves(tail)
    outer = bias_ref[4:5, :]
    outer = (outer[:, 0:128], outer[:, 128:256])
    bias_high = jnp.concatenate(
        [
            tail[0:3],
            swap_halves(outer[0]),
            outer[0],
            swap_halves(outer[1]),
            outer[1],
            jnp.zeros((1, 128), F32),
        ],
        axis=0,
    )
    one, first, two, four = shard_layout(shards)
    held = shard_held(shards)
    gap = 2 * first - one - 8

    def collect(place, carry):
        start = pl.multiple_of(place * held, 8)
        shard = place
        if shards > 1:
            other, rest = place // (shards // 2), lax.rem(place, shards // 2)
            shard = me ^ (sent_mask(shards, rest) | other)
        at = pl.multiple_of(shard * one, 8)
        high = [swap_halves(taps_one[pl.ds(at + first, one - first), :])]
        if gap:
            high.append(jnp.zeros((gap, 128), F32))
        stage[pl.ds(start, first), :] = jnp.where(
            low_lanes((first, 128)),
            taps_one[pl.ds(at, first), :],
            jnp.concatenate(high + [bias_high], axis=0),
        )
        stage[pl.ds(start + first, two), :] = jnp.where(
            low_lanes((two, 128)),
            taps_two[pl.ds(shard * two, two), :],
            swap_halves(taps_three[pl.ds(shard * two, two), :]),
        )
        at = start + first + two
        for row in range(four // 2):
            row_at = shard * (four // 2) + row
            stage[pl.ds(at + 2 * row, 1), :] = taps_four[0, pl.ds(row_at, 1), :]
            stage[pl.ds(at + 2 * row + 1, 1), :] = taps_four[1, pl.ds(row_at, 1), :]
        return carry

    lax.fori_loop(0, shards, collect, 0, unroll=UNROLL if shards > 1 else 1)
    rows = keep_ref.shape[0] * held
    keep_ref[...] = stage[0:rows, :].reshape(keep_ref.shape).astype(keep_ref.dtype)
    send_ref[...] = stage[shards * held - rows :, :].reshape(send_ref.shape).astype(BF16)
    for fetch in fetches:
        fetch.wait()


BLOCK_SCRATCH = 23


def run_block(shards, bias_rows, even, odd, masks, spread, images, olds, pieces):
    count = even.shape[0]
    held = pieces[0].shape[1]
    part = max(shards // 2, 1)
    inside = pl.BlockSpec(memory_space=pltpu.VMEM)
    vmem = pltpu.VMEM
    hbm = pl.BlockSpec(memory_space=pl.ANY)
    place = pltpu.VMEM if shards > 1 else pltpu.HBM
    return pl.pallas_call(
        functools.partial(block_kernel, shards, len(olds)),
        in_specs=[*[inside] * 5, *[hbm] * (1 + len(olds)), *[inside] * len(pieces)],
        out_specs=[inside] * (7 + len(olds)),
        out_shape=[
            place((part, held, 128), KEEP_TYPE if shards > 1 else F32),
            place((part, held, 128), BF16),
            place((count, ROWS, 768), BF16),
            place((count, ROWS, 128), BF16),
            place((768, 2 * C), BF16),
            place((128, C), BF16),
            place(images.shape, BF16),
            *[place(old.shape, F32) for old in olds],
        ],
        scratch_shapes=[
            pltpu.SemaphoreType.DMA((1 + len(olds),)),
            vmem((shards * held, 128), F32),
            vmem((9 * C, 128), F32),
            vmem((9 * HID, 128), F32),
            vmem((9 * HID, 128), F32),
            vmem((2, HID, 128), F32),
            vmem((2 * C, 768), BF16),
            vmem((4 * HID, 384), BF16),
            vmem((384, 256), BF16),
            vmem((4 * HID, 384), BF16),
            vmem((384, 256), BF16),
            vmem((C, 128), BF16),
            vmem((count, ROWS, 256), BF16),
            vmem((count, ROWS, 256), BF16),
            vmem((count, ROWS, 128), F32),
            vmem((count, ROWS, 128), F32),
            vmem((count, ROWS, 384), BF16),
            vmem((2 * count, HALF, SIDE + 2 * EDGE, 128), F32),
            vmem((2 * C, 768), F32),
            vmem((256, 384), F32),
            vmem((256, 384), F32),
            vmem((C, 128), F32),
            vmem((8, C), F32),
        ],
        compiler_params=pltpu.CompilerParams(vmem_limit_bytes=BLOCK_BYTES),
        cost_estimate=pl.CostEstimate(
            flops=count * 1_200_000_000, bytes_accessed=count * 2_000_000, transcendentals=count * 196608
        ),
        name="block",
    )(
        *(in_vmem if shards > 1 else in_hbm)(bias_rows, even, odd, masks, spread),
        *in_hbm(images, *olds),
        *(in_vmem if shards > 1 else in_hbm)(*pieces),
    )


def finish_kernel(
    first,
    count,
    masks,
    bias_ref,
    img_ref,
    spread_ref,
    turned_ref,
    act_ref,
    back_ref,
    four_ref,
    *refs,
):
    out_hbm, grad_hbm, out_ref, grad_ref, back, sems = refs[-6:]
    stores = []

    def store(source, target):
        copy = pltpu.make_async_copy(source, target, sems.at[len(stores)])
        copy.start()
        stores.append(copy)

    spot = lax.broadcasted_iota(jnp.int32, (128, 256), 0)
    pix = lax.broadcasted_iota(jnp.int32, (128, 256), 1)
    pool_down = jnp.where(pix // 2 == spot, 0.25, 0.0).astype(BF16)
    back[0] = dot(turned_ref[first], back_ref[...])
    for slot in range(count):
        image = first + slot
        if slot + 1 < count:
            back[(slot + 1) % 2] = dot(turned_ref[image + 1], back_ref[...])
        for half in range(2):
            rows = slice(half * 256, (half + 1) * 256)
            base_mean = dot(pool_down, img_ref[image, :, 0].reshape(ROWS, C)[rows]) + dot(
                pool_down, img_ref[image, :, 1].reshape(ROWS, C)[rows]
            )
            act_mean = dot(pool_down, act_ref[image, rows, :]).astype(BF16)
            last = dot(act_mean, four_ref[...]) + bias_ref[3:4, :]
            pooled = 2.0 * dot(pool_down, masks[image, rows, :].astype(BF16))
            value = (base_mean + GAIN * last) * jnp.concatenate([pooled, pooled], axis=1)
            out_ref[slot, half * 8 : (half + 1) * 8] = value.reshape(8, HALF, C).astype(BF16)
        for start in range(0, ROWS, CHUNK):
            rows = slice(start, start + CHUNK)
            pairs = slice(start // SIDE, (start + CHUNK) // SIDE)
            mask = masks[image, rows, :]
            wide_mask = jnp.concatenate([mask, mask], axis=1)
            spread = 0.25 * spread_ref[image, rows, :].astype(F32)
            for parity in range(2):
                base = img_ref[image, pairs, parity].reshape(CHUNK, C).astype(F32)
                _, slope = silu_and_slope(base)
                lanes = slice(parity * C, (parity + 1) * C)
                value = spread + back[slot % 2, rows, lanes] * (slope * wide_mask)
                grad_ref[slot, pairs, parity] = value.reshape(-1, SIDE, C).astype(BF16)
        store(out_ref.at[slot], out_hbm.at[image])
        store(grad_ref.at[slot], grad_hbm.at[image])
    for copy in stores:
        copy.wait()


def run_finish(first, last, before, resident):
    total = resident[0].shape[0]
    count = last - first
    inside = pl.BlockSpec(memory_space=pltpu.VMEM)
    hbm = pl.BlockSpec(memory_space=pl.ANY)
    return pl.pallas_call(
        functools.partial(finish_kernel, first, count),
        in_specs=[*[inside] * len(resident), *[hbm] * len(before)],
        out_specs=[hbm, hbm],
        out_shape=[
            pltpu.HBM((total, HALF, HALF, C), BF16),
            pltpu.HBM((total, HALF, 2, SIDE, C), BF16),
        ],
        input_output_aliases={len(resident) + which: which for which in range(len(before))},
        scratch_shapes=[
            pltpu.VMEM((count, HALF, HALF, C), BF16),
            pltpu.VMEM((count, HALF, 2, SIDE, C), BF16),
            pltpu.VMEM((2, ROWS, 2 * C), F32),
            pltpu.SemaphoreType.DMA((2 * count,)),
        ],
        compiler_params=pltpu.CompilerParams(vmem_limit_bytes=FINISH_BYTES),
        cost_estimate=pl.CostEstimate(
            flops=count * 450_000_000, bytes_accessed=count * 2_500_000, transcendentals=count * 262144
        ),
        name="finish",
    )(*resident, *in_hbm(*before))


def fold_kernel(got, own_ref, *refs):
    outs = refs[got:]
    total = own_ref[...]
    for ref in refs[:got]:
        total = total + ref[...].astype(F32)
    rows = outs[0].shape[0]
    for which, out in enumerate(outs):
        out[...] = total[which * rows : (which + 1) * rows].astype(out.dtype)


def run_fold(own, received, parts):
    shape = (own.shape[0] // parts,) + own.shape[1:]
    inside = pl.BlockSpec(memory_space=pltpu.VMEM)
    return pl.pallas_call(
        functools.partial(fold_kernel, len(received)),
        in_specs=[inside] * (1 + len(received)),
        out_specs=[inside] * parts,
        out_shape=[pltpu.VMEM(shape, F32)] + [pltpu.VMEM(shape, BF16)] * (parts - 1),
        compiler_params=pltpu.CompilerParams(vmem_limit_bytes=FOLD_BYTES),
        cost_estimate=pl.CostEstimate(flops=500_000, bytes_accessed=1_000_000, transcendentals=0),
        name="fold",
    )(*in_vmem(own, *received))


def adamw_update(weight, gradient, first_old, second_old, step_rate):
    first_new = BETA_ONE * first_old + (1.0 - BETA_ONE) * gradient
    second_new = BETA_TWO * second_old + (1.0 - BETA_TWO) * gradient * gradient
    first_hat = first_new / (1.0 - BETA_ONE**STEP)
    second_hat = second_new / (1.0 - BETA_TWO**STEP)
    weight_new = weight - step_rate * (
        first_hat / (jnp.sqrt(second_hat) + EPSILON) + DECAY * weight
    )
    return (first_new, second_new, weight_new, weight_new.astype(BF16))


RATES = ((9.0 * C) ** (-0.5), (9.0 * HID) ** (-0.5), (9.0 * HID) ** (-0.5), 8.0)


def update_kernel(got, own_ref, *refs):
    received, refs = refs[:got], refs[got:]
    olds, news, total, rows_of_64 = refs[:15], refs[15:35], refs[35], refs[36]
    value = own_ref[0]
    for ref in received:
        value = value + ref[0].astype(F32)
    total[...] = value
    one, first, two, four = shard_layout(COMPACT[0] // olds[0].shape[0])

    def joined(rows):
        return jnp.where(
            low_lanes((rows, 128)),
            rows_of_64[pl.ds(0, rows, stride=2), :],
            swap_halves(rows_of_64[pl.ds(1, rows, stride=2), :]),
        )

    rows_of_64[0:first, :] = total[0:first, :]
    rows_of_64[first:one, :] = swap_halves(total[0 : one - first, :])
    gradients = [joined(one // 2)]
    rows_of_64[0:two, :] = total[first : first + two, :]
    gradients.append(joined(two // 2))
    rows_of_64[0:two, :] = swap_halves(total[first : first + two, :])
    gradients.append(joined(two // 2))
    gradients.append(total[first + two : first + two + four, :])
    rows = total[first - 8 : first, :]
    turned = swap_halves(rows)
    low = low_lanes((1, 128))
    parts = [jnp.where(low, turned[row : row + 1], rows[row + 1 : row + 2]) for row in (0, 2, 4)]
    parts.append(turned[6:7])
    gradients.append(jnp.concatenate(parts, axis=1)[:, 0:BIASES])
    rate = jnp.where(lax.broadcasted_iota(jnp.int32, (1, BIASES), 1) < 3 * HID, 0.5, 32.0)
    for which, gradient in enumerate(gradients):
        weight, first_old, second_old = (ref[...] for ref in olds[3 * which : 3 * which + 3])
        values = adamw_update(
            weight, gradient, first_old, second_old, rate if which == 4 else RATES[which]
        )
        for ref, value in zip(news[4 * which : 4 * which + 4], values):
            ref[...] = value.reshape(ref.shape)


def run_update(own, received, olds):
    shapes = []
    for which in range(5):
        shape = olds[3 * which].shape
        low_shape = shape if which < 4 else shape[1:]
        shapes += [jax.ShapeDtypeStruct(shape, F32)] * 3 + [jax.ShapeDtypeStruct(low_shape, BF16)]
    return pl.pallas_call(
        functools.partial(update_kernel, len(received)),
        out_shape=shapes,
        scratch_shapes=[pltpu.VMEM(own.shape[1:], F32), pltpu.VMEM((80, 128), F32)],
        compiler_params=pltpu.CompilerParams(vmem_limit_bytes=FOLD_BYTES),
        cost_estimate=pl.CostEstimate(flops=500_000, bytes_accessed=700_000, transcendentals=8192),
        name="update",
    )(*in_vmem(own, *received, *olds))


def exchange(value, mask, count):
    return lax.ppermute(value, AXES, [(i, i ^ mask) for i in range(count)])


def gather_shards(value, devices, beside):
    groups = bit_groups(devices)
    early, late = beside
    held = value[None]
    for low, top in groups[:-2]:
        parts = [held] + [
            exchange(held, mask << low, devices) for mask in range(1, 1 << (top - low))
        ]
        parts, early = lax.optimization_barrier((parts, early))
        held = jnp.concatenate(parts, axis=0)
    low, top = groups[-2]
    pieces = [exchange(held, mask << low, devices) for mask in range(1, 1 << (top - low))]
    pieces, late = lax.optimization_barrier((pieces, late))
    pieces = [held] + pieces
    return pieces + [exchange(piece, 1, devices) for piece in pieces], early, late


def bit_groups(devices):
    groups = []
    top = devices.bit_length() - 1
    while top > 1:
        low = max(top - 2, 1)
        groups.append((low, top))
        top = low
    groups.append((0, 1))
    return groups


def sent_mask(devices, place):
    mask = 0
    for low, top in bit_groups(devices)[:-1]:
        width = top - low
        mask = mask | ((place & ((1 << width) - 1)) << low)
        place = place >> width
    return mask


def place_mask(devices, place):
    mask = 0
    for low, top in bit_groups(devices):
        width = top - low
        mask = mask | ((place & ((1 << width) - 1)) << low)
        place = place >> width
    return mask


def local(devices, *args):
    (
        images,
        image_sizes,
        out_grad,
        weight_one,
        first_one,
        second_one,
        weight_two,
        first_two,
        second_two,
        weight_three,
        first_three,
        second_three,
        weight_four,
        first_four,
        second_four,
        biases,
        first_bias,
        second_bias,
    ) = args
    weights = (weight_one, weight_two, weight_three, weight_four)
    olds = (
        (weight_one, first_one, second_one),
        (weight_two, first_two, second_two),
        (weight_three, first_three, second_three),
        (weight_four, first_four, second_four),
    )
    count = images.shape[0]
    image_sizes = image_sizes.T
    images = images.reshape(count, HALF, 2, SIDE, C)
    sizes = [weight.shape[0] for weight in weights]
    total = sum(sizes)
    packed = (
        all(size % 128 == 0 for size in sizes)
        and sizes[3] % 256 == 0
        and devices >= 8
        and devices & (devices - 1) == 0
    )
    shards = devices if packed else 1
    held = shard_held(shards)
    beside = (
        run_spread(image_sizes, biases.reshape(1, BIASES), out_grad),
        run_active(image_sizes, images),
    )
    if packed:
        mine = run_pack(held, [weight.reshape(-1, 128) for weight in weights])
        pieces, *beside = gather_shards(mine, devices, beside)
    else:
        low = jnp.concatenate([weight.astype(BF16) for weight in weights])
        full = lax.all_gather(low, AXES, axis=0, tiled=False)
        parts = []
        at = 0
        for size in sizes:
            parts.append(full[:, at : at + size].reshape(-1))
            at += size
        one, first, two, four = shard_layout(1)
        rows = parts[0].reshape(one, HID)
        rows = jnp.concatenate(
            [rows[:first], jnp.pad(rows[first:], ((0, 2 * first - one), (0, 0)))], axis=1
        )
        both = jnp.concatenate([part.reshape(two, HID) for part in parts[1:3]], axis=1)
        full = jnp.concatenate([rows, both, parts[3].reshape(four, 128)], axis=0)
        pieces = [jnp.pad(full, ((0, held - full.shape[0]), (0, 0)))[None]]
    (spread, bias_rows), (even, odd, masks) = beside
    flat = []
    if packed:
        flat = [array.reshape(-1, 128) for three in olds for array in three]
        flat += [array.reshape(1, BIASES) for array in (biases, first_bias, second_bias)]
    keep, send, turned, act_three, back_one, fwd_four, base, *flat = run_block(
        shards, bias_rows, even, odd, masks, spread, images, flat, pieces
    )
    resident = [masks, bias_rows, base, spread, turned, act_three, back_one, fwd_four]
    outs = ()
    if packed:
        own, received = keep, [exchange(send, 1, devices)]
        groups = bit_groups(devices)[:-1][::-1]
        cuts = [0] + [FINISH_SPLIT] * (len(groups) - 1) + [count]
        for which, (low, top) in enumerate(groups):
            own, *sent = run_fold(own, received, 1 << (top - low))
            sent, resident, outs = lax.optimization_barrier((sent, resident, outs))
            received = [exchange(part, (at + 1) << low, devices) for at, part in enumerate(sent)]
            if cuts[which] < cuts[which + 1]:
                outs = run_finish(cuts[which], cuts[which + 1], outs, in_vmem(*resident))
            received, outs = lax.optimization_barrier((received, outs))
    else:
        outs = run_finish(0, count, outs, in_hbm(*resident))
    block_out, image_grad = outs
    image_grad = image_grad.reshape(count, SIDE, SIDE, C)
    if packed:
        updates = [array.reshape(-1) for array in run_update(own, received, flat)]
        return (block_out, image_grad, *updates)
    rows = keep[0]
    one, first, two, four = shard_layout(1)
    parts = [
        jnp.concatenate([rows[:first, :HID], rows[: one - first, HID:]], axis=0),
        rows[first : first + two, :HID],
        rows[first : first + two, HID:],
        rows[first + two : first + two + four],
    ]
    parts = [part.reshape(devices, -1) for part in parts]
    bias_part = rows[first - 8 : first - 1, HID:].reshape(-1)
    bias_total = lax.psum(bias_part, AXES)
    summed = lax.psum_scatter(
        jnp.concatenate(parts, axis=1).reshape(-1), AXES, scatter_dimension=0, tiled=True
    )
    updates = []
    at = 0
    for (weight, first, second), rate, size in zip(olds, RATES, sizes):
        updates += list(adamw_update(weight, summed[at : at + size], first, second, rate))
        at += size
    bias_rates = jnp.where(jnp.arange(BIASES) < 3 * HID, 0.5, 32.0)
    updates += list(adamw_update(biases, bias_total, first_bias, second_bias, bias_rates))
    return (block_out, image_grad, *updates)


def solution(mesh):
    devices = mesh.shape["dp"] * mesh.shape["fsdp"]
    split = P(AXES)
    return jax.shard_map(
        functools.partial(local, devices),
        mesh=mesh,
        in_specs=(
            P(AXES, None, None, None),
            P(AXES, None),
            P(AXES, None, None, None),
            *([split] * 12),
            P(),
            P(),
            P(),
        ),
        out_specs=(
            P(AXES, None, None, None),
            P(AXES, None, None, None),
            *([split] * 16),
            P(),
            P(),
            P(),
            P(),
        ),
        check_vma=False,
    )
```

```python
import functools

import jax
import jax.numpy as jnp
from jax import lax
from jax.experimental import pallas as pl
from jax.experimental.pallas import tpu as pltpu
from jax.sharding import PartitionSpec as P

C = 256
HID = 64
STEP = 10
SIDE = 32
HALF = SIDE // 2
ROWS = HALF * SIDE
PAD = SIDE

GAIN = 1.0 / 64.0
BETA_ONE = 0.9
BETA_TWO = 0.999
DECAY = 0.01
EPSILON = 1e-08
AXES = ("dp", "fsdp")
UNROLL = 16
SPARE = 8
SPREAD_BYTES = 58 * 1024 * 1024
ACTIVE_BYTES = 56 * 1024 * 1024
BLOCK_BYTES = 40 * 1024 * 1024
FINISH_BYTES = 24 * 1024 * 1024
FOLD_BYTES = 24 * 1024 * 1024
FINISH_SPLIT = 3
CHUNK = 64
LAG = 1
MERGE = 2
EDGE = 8
KEEP_TYPE = jnp.float32

COMPACT = (9 * C * HID // 128, 9 * HID * HID // 128, 9 * HID * HID // 128, HID * C // 128)
BIASES = 3 * HID + C

F32 = jnp.float32
BF16 = jnp.bfloat16


def silu(value):
    half = 0.5 * value
    return half * (1.0 + jnp.tanh(half))


def silu_and_slope(value):
    half = 0.5 * value
    turn = jnp.tanh(half)
    above = 1.0 + turn
    return half * above, above + half * (1.0 - turn * turn)


def dot(left, right):
    return jnp.dot(left, right, preferred_element_type=F32)


def dot_rows(left, right):
    return lax.dot_general(left, right, (((0,), (0,)), ((), ())), preferred_element_type=F32)


def swap_halves(value):
    return pltpu.roll(value, HID, 1)


def low_lanes(shape):
    return lax.broadcasted_iota(jnp.int32, shape, 1) < HID


def shard_layout(shards):
    one, two, three, four = (rows // shards for rows in COMPACT)
    first = -(-(one + 4) // 8) * 8
    return 2 * one, first, 2 * two, four


def shard_held(shards):
    _, first, two, four = shard_layout(shards)
    return -(-(first + two + four) // 16) * 16


def pack_kernel(one_ref, two_ref, three_ref, four_ref, out_ref, stage, rows_of_64):
    _, first, two, four = shard_layout(COMPACT[0] // one_ref.shape[0])
    stage[...] = jnp.zeros(stage.shape, F32)

    def spread_rows(ref):
        value = ref[...]
        rows = value.shape[0]
        rows_of_64[pl.ds(0, rows, stride=2), :] = value
        rows_of_64[pl.ds(1, rows, stride=2), :] = swap_halves(value)

    spread_rows(one_ref)
    rest = 2 * one_ref.shape[0] - first
    low = low_lanes((rest, 128))
    stage[0:rest, :] = jnp.where(
        low, rows_of_64[0:rest, :], swap_halves(rows_of_64[first : first + rest, :])
    )
    stage[rest:first, :] = rows_of_64[rest:first, :]
    spread_rows(two_ref)
    value = rows_of_64[0:two, :]
    spread_rows(three_ref)
    stage[first : first + two, :] = jnp.where(
        low_lanes((two, 128)), value, swap_halves(rows_of_64[0:two, :])
    )
    stage[first + two : first + two + four, :] = four_ref[...]
    out_ref[...] = stage[...].astype(BF16)


def run_pack(held, weights):
    return pl.pallas_call(
        pack_kernel,
        out_shape=pltpu.VMEM((held, 128), BF16),
        scratch_shapes=[pltpu.VMEM((held, 128), F32), pltpu.VMEM((80, 128), F32)],
        cost_estimate=pl.CostEstimate(flops=8192, bytes_accessed=48 * 1024, transcendentals=0),
        name="pack",
    )(*in_hbm(*weights))


def pair_inside(sizes_ref, image):
    shape = (HALF, SIDE, 128)
    row = lax.broadcasted_iota(jnp.int32, shape, 0)
    col = lax.broadcasted_iota(jnp.int32, shape, 1)
    inside = (row < sizes_ref[0, image] // 2) & (col < sizes_ref[1, image])
    return jnp.where(inside, 1.0, 0.0).reshape(ROWS, 128)


def pooled_inside(sizes_ref, step):
    spot = lax.broadcasted_iota(jnp.int32, (HALF * HALF, C), 0)
    return (spot < sizes_ref[0, step] * (HALF // 2)) & (
        jnp.bitwise_and(spot, HALF - 1) < sizes_ref[1, step] // 2
    )


def spread_kernel(sizes_ref, bias_ref, og_ref, spread_ref, bias_rows_ref):
    parts = [bias_ref[:, at : at + 128] for at in (0, 128, 256)]
    last = jnp.concatenate([bias_ref[:, 384:448], jnp.zeros((1, HID), F32)], axis=1)
    parts.append(last)
    turned = [swap_halves(part) for part in parts]
    low = low_lanes((1, 128))
    zero = jnp.zeros((1, 128), F32)
    rows = [
        (jnp.where(low, parts[0], turned[0]), zero),
        (jnp.where(low, turned[0], parts[0]), zero),
        (jnp.where(low, parts[1], turned[1]), zero),
        (jnp.where(low, turned[1], turned[2]), jnp.where(low, turned[2], turned[3])),
    ]
    for row, pair in enumerate(rows):
        bias_rows_ref[row : row + 1, :] = jnp.concatenate(pair, axis=1)
    total = jnp.zeros((1, C), F32)
    pix = lax.broadcasted_iota(jnp.int32, (256, 128), 0)
    spot = lax.broadcasted_iota(jnp.int32, (256, 128), 1)
    spread_up = jnp.where(pix // 2 == spot, 1.0, 0.0).astype(BF16)
    for image in range(og_ref.shape[0]):
        cot = jnp.where(
            pooled_inside(sizes_ref, image),
            og_ref[image].reshape(HALF * HALF, C).astype(F32),
            0.0,
        )
        total = total + jnp.sum(cot, axis=0, keepdims=True)
        cot = cot.astype(BF16)
        for half in range(2):
            value = dot(spread_up, cot[half * 128 : (half + 1) * 128])
            spread_ref[image, half * 256 : (half + 1) * 256, :] = value.astype(BF16)
    bias_rows_ref[4:8, :] = jnp.concatenate([total * GAIN, jnp.zeros((3, C), F32)], axis=0)


def active_kernel(sizes_ref, img_ref, even_ref, odd_ref, mask_ref):
    step = pl.program_id(0)
    mask = pair_inside(sizes_ref, step)
    mask_ref[step] = mask
    wide_mask = jnp.concatenate([mask, mask], axis=1)
    for parity, act in ((0, even_ref), (1, odd_ref)):
        base = img_ref[0, :, parity].reshape(ROWS, C).astype(F32)
        act[step] = (silu(base) * wide_mask).astype(BF16)


def in_vmem(*arrays):
    return [pltpu.with_memory_space_constraint(array, pltpu.VMEM) for array in arrays]


def in_hbm(*arrays):
    return [pltpu.with_memory_space_constraint(array, pltpu.HBM) for array in arrays]


def block_of(shape):
    rest = (0,) * (len(shape) - 1)
    return pl.BlockSpec(shape, lambda i: (i,) + rest)


def whole(shape):
    return pl.BlockSpec(shape, lambda i: (0,) * len(shape))


def run_spread(sizes, biases, out_grad):
    count = out_grad.shape[0]
    vmem = pl.BlockSpec(memory_space=pltpu.VMEM)
    return pl.pallas_call(
        spread_kernel,
        in_specs=[pl.BlockSpec(memory_space=pltpu.SMEM), vmem, vmem],
        out_specs=[vmem, vmem],
        out_shape=[
            pltpu.VMEM((count, ROWS, C), BF16),
            pltpu.VMEM((8, C), F32),
        ],
        compiler_params=pltpu.CompilerParams(vmem_limit_bytes=SPREAD_BYTES),
        cost_estimate=pl.CostEstimate(
            flops=count * 2 * 512 * 128 * 256, bytes_accessed=count * 400_000, transcendentals=0
        ),
        name="spread",
    )(sizes, *in_hbm(biases, out_grad))


def run_active(sizes, images):
    count = images.shape[0]
    return pl.pallas_call(
        active_kernel,
        grid=(count,),
        in_specs=[
            pl.BlockSpec(memory_space=pltpu.SMEM),
            block_of((1, HALF, 2, SIDE, C)),
        ],
        out_specs=[pl.BlockSpec(memory_space=pltpu.VMEM)] * 3,
        out_shape=[
            pltpu.VMEM((count, ROWS, C), BF16),
            pltpu.VMEM((count, ROWS, C), BF16),
            pltpu.VMEM((count, ROWS, 128), F32),
        ],
        compiler_params=pltpu.CompilerParams(
            dimension_semantics=("arbitrary",), vmem_limit_bytes=ACTIVE_BYTES
        ),
        cost_estimate=pl.CostEstimate(
            flops=count * 3_000_000, bytes_accessed=count * 1_100_000, transcendentals=count * 262144
        ),
        name="active",
    )(sizes, *in_hbm(images))


def unpack_weights(shards, me, pieces, stage, taps_one, taps_two, taps_three, taps_four):
    one, first, two, four = shard_layout(shards)
    held = pieces[0].shape[1]
    for which, piece in enumerate(pieces):
        group = piece.shape[0]
        stage[which * group * held : (which + 1) * group * held, :] = (
            piece[...].reshape(group * held, 128).astype(F32)
        )

    def place(shard, carry):
        owner = me ^ place_mask(shards, shard) if shards > 1 else shard
        start = pl.multiple_of(shard * held, 8)
        value = stage[pl.ds(start, first), :]
        at = pl.multiple_of(owner * one, 8)
        taps_one[pl.ds(at, first), :] = value
        taps_one[pl.ds(at + first, one - first), :] = swap_halves(value[0 : one - first])
        value = stage[pl.ds(start + first, two), :]
        taps_two[pl.ds(owner * two, two), :] = value
        taps_three[pl.ds(owner * two, two), :] = swap_halves(value)
        at = start + first + two
        for row in range(four // 2):
            row_at = owner * (four // 2) + row
            taps_four[0, pl.ds(row_at, 1), :] = stage[pl.ds(at + 2 * row, 1), :]
            taps_four[1, pl.ds(row_at, 1), :] = stage[pl.ds(at + 2 * row + 1, 1), :]
        return carry

    lax.fori_loop(0, shards, place, 0, unroll=UNROLL if shards > 1 else 1)


def tap_blocks(taps, width, col_tap):
    rows = [
        taps[(row_tap * 3 + col_tap) * width : (row_tap * 3 + col_tap + 1) * width, :]
        for row_tap in range(3)
    ]
    low = low_lanes((width, 128))
    zero = jnp.zeros((width, 128), F32)
    turned = [swap_halves(value) for value in rows]
    return (
        jnp.where(low, rows[0], zero),
        jnp.where(low, rows[1], turned[0]),
        jnp.where(low, rows[2], turned[1]),
        jnp.where(low, zero, turned[2]),
    )


def block_kernel(
    shards,
    fetched,
    bias_ref,
    even_ref,
    odd_ref,
    masks,
    spread_ref,
    img_hbm,
    *refs,
):
    olds, refs = refs[:fetched], refs[fetched:]
    outs = 7 + fetched
    cut = len(refs) - BLOCK_SCRATCH - outs
    pieces, refs = refs[:cut], refs[cut:]
    keep_ref, send_ref, turned_ref, act_three_ref, back_one_ref, fwd_four_ref, img_ref = refs[:7]
    news = refs[7:outs]
    (
        sems,
        stage,
        taps_one,
        taps_two,
        taps_three,
        taps_four,
        fwd_one,
        fwd_two,
        back_two,
        fwd_three,
        back_three,
        back_four,
        act_one,
        act_two,
        slope_one,
        slope_two,
        turned,
        shifts,
        sum_one,
        sum_two,
        sum_three,
        sum_four,
        sum_bias,
    ) = refs[outs:]
    images = even_ref.shape[0]
    fetches = [
        pltpu.make_async_copy(source, target, sems.at[which])
        for which, (source, target) in enumerate(zip((img_hbm, *olds), (img_ref, *news)))
    ]
    for fetch in fetches:
        fetch.start()
    for which in range(2 * images):
        none = jnp.zeros((HALF, EDGE, 128), F32)
        shifts[which, :, 0:EDGE, :] = none
        shifts[which, :, EDGE + SIDE : 2 * EDGE + SIDE, :] = none
    me = lax.axis_index(AXES) if shards > 1 else 0
    unpack_weights(shards, me, pieces, stage, taps_one, taps_two, taps_three, taps_four)
    for col_tap in range(3):
        lanes = slice(col_tap * 128, (col_tap + 1) * 128)
        more = slice(384 + col_tap * 128, 384 + (col_tap + 1) * 128)
        blocks = tap_blocks(taps_one, C, col_tap)
        fwd_one[0:C, lanes] = blocks[1].astype(BF16)
        fwd_one[C : 2 * C, lanes] = blocks[2].astype(BF16)
        fwd_one[0:C, more] = blocks[3].astype(BF16)
        fwd_one[C : 2 * C, more] = blocks[0].astype(BF16)
        back_one_ref[lanes, 0:C] = (0.5 * blocks[1]).T.astype(BF16)
        back_one_ref[lanes, C : 2 * C] = (0.5 * blocks[2]).T.astype(BF16)
        back_one_ref[more, 0:C] = (0.5 * blocks[3]).T.astype(BF16)
        back_one_ref[more, C : 2 * C] = (0.5 * blocks[0]).T.astype(BF16)
        for taps, fwd, back in (
            (taps_two, fwd_two, back_two),
            (taps_three, fwd_three, back_three),
        ):
            blocks = tap_blocks(taps, HID, col_tap)
            for place, which in enumerate((1, 2, 3, 0)):
                fwd[place * HID : (place + 1) * HID, lanes] = blocks[which].astype(BF16)
            here = jnp.concatenate([blocks[1], blocks[2]], axis=0).T
            around = jnp.concatenate([blocks[3], blocks[0]], axis=0).T
            back[lanes, 0:128] = (0.5 * here).astype(BF16)
            back[lanes, 128:256] = (0.5 * around).astype(BF16)
    four = jnp.concatenate([taps_four[0, 0:HID], taps_four[1, 0:HID]], axis=1)
    both = jnp.concatenate([four, four], axis=0)
    fwd_four_ref[...] = both.astype(BF16)
    back_four[...] = (0.5 * both).T.astype(BF16)

    low = low_lanes((ROWS, 128))
    low_wide = jnp.concatenate([low, low, low], axis=1)

    def rows_before(value):
        return jnp.concatenate([jnp.zeros((PAD, value.shape[1]), value.dtype), value[:-PAD]], axis=0)

    def rows_after(value):
        return jnp.concatenate([value[PAD:], jnp.zeros((PAD, value.shape[1]), value.dtype)], axis=0)

    def add_to(total, value, slot):
        total[...] = value if slot == 0 else total[...] + value

    def image_phases(slot):
        first, second, around_grad = act_one.at[slot], act_two.at[slot], turned.at[slot]
        left, right = shifts.at[2 * slot], shifts.at[2 * slot + 1]

        def by_rows(value):
            return value.reshape(HALF, SIDE, 128)

        def shift_sum(parts):
            left[:, EDGE : EDGE + SIDE, :] = by_rows(parts[:, 0:128])
            right[:, EDGE : EDGE + SIDE, :] = by_rows(parts[:, 256:384])
            before = left[:, EDGE - 1 : EDGE - 1 + SIDE, :]
            after = right[:, EDGE + 1 : EDGE + 1 + SIDE, :]
            return (before + by_rows(parts[:, 128:256]) + after).reshape(ROWS, 128)

        def activate(conv):
            active, slope = silu_and_slope(conv)
            return (active * masks[slot]).astype(BF16), slope * masks[slot]

        def keep_active(act, active):
            act[:, 0:128] = active
            act[:, 128:256] = jnp.where(low, rows_after(active), rows_before(active))

        def turn(grad, row, into):
            add_to(sum_bias.at[row : row + 1, 0:128], jnp.sum(grad, axis=0, keepdims=True), slot)
            left[:, EDGE : EDGE + SIDE, :] = by_rows(grad)
            parts = (
                left[:, EDGE + 1 : EDGE + 1 + SIDE, :].reshape(ROWS, 128),
                grad,
                left[:, EDGE - 1 : EDGE - 1 + SIDE, :].reshape(ROWS, 128),
            )
            value = jnp.concatenate([part.astype(BF16) for part in parts], axis=1)
            into[:, 0:384] = value
            return value

        def back_through(window, kernel):
            parts = dot(window, kernel)
            around = parts[:, 128:256]
            return parts[:, 0:128], around

        def back_sum(pair):
            here, around = pair
            return here + jnp.where(low, rows_before(around), rows_after(around))

        window = jnp.concatenate(
            [even_ref[slot], odd_ref[slot]], axis=1
        )
        parts = dot(window, fwd_one[...])
        yield
        parts = parts[:, 0:384] + jnp.where(
            low_wide, rows_before(parts[:, 384:768]), rows_after(parts[:, 384:768])
        )
        active, slope = activate(shift_sum(parts) + bias_ref[0:1, 0:128])
        keep_active(first, active)
        slope_one[slot] = slope
        yield
        parts = dot(first[...], fwd_two[...])
        yield
        active, slope = activate(shift_sum(parts) + bias_ref[1:2, 0:128])
        keep_active(second, active)
        slope_two[slot] = slope
        yield
        parts = dot(second[...], fwd_three[...])
        back = dot(spread_ref[slot], back_four[...])
        yield
        active, slope = activate(shift_sum(parts) + bias_ref[2:3, 0:128])
        act_three_ref[slot] = active
        turn(back * (GAIN * 0.25) * slope, 2, around_grad)
        yield
        back = back_through(around_grad[:, 0:384], back_three[...])
        part = dot_rows(act_three_ref[slot], spread_ref[slot])
        for half in (slice(0, HID), slice(HID, 2 * HID)):
            add_to(sum_four.at[half, :], part[half, :], slot)
        add_to(sum_three, dot_rows(second[...], around_grad[:, 0:384]), slot)
        yield
        turn(back_sum(back) * slope_two[slot], 1, around_grad)
        yield
        back = back_through(around_grad[:, 0:384], back_two[...])
        add_to(sum_two, dot_rows(first[...], around_grad[:, 0:384]), slot)
        yield
        window = turn(back_sum(back) * slope_one[slot], 0, turned_ref.at[slot])
        turned_ref[slot, :, 384:768] = jnp.where(low_wide, rows_after(window), rows_before(window))
        yield
        if slot % MERGE == MERGE - 1 or slot == images - 1:
            first_slot = slot - slot % MERGE
            slots = range(first_slot, slot + 1)
            both = jnp.concatenate(
                [
                    jnp.concatenate(
                        [even_ref[at], odd_ref[at]], axis=1
                    )
                    for at in slots
                ],
                axis=0,
            )
            window = turned_ref[first_slot : slot + 1].reshape(len(slots) * ROWS, 768)
            add_to(sum_one, dot_rows(both, window), first_slot)

    waiting = [image_phases(slot) for slot in range(images)]
    turn_number = 0
    while waiting:
        for place, phases in enumerate(list(waiting)):
            if turn_number >= LAG * place or len(waiting) < images:
                if next(phases, waiting) is waiting:
                    waiting.remove(phases)
        turn_number += 1

    for col_tap in range(3):
        here = slice(col_tap * 128, (col_tap + 1) * 128)
        around = slice(384 + col_tap * 128, 384 + (col_tap + 1) * 128)
        even_here, even_around = sum_one[0:C, here], sum_one[0:C, around]
        odd_here, odd_around = sum_one[C : 2 * C, here], sum_one[C : 2 * C, around]
        for row_tap, value in (
            (0, swap_halves(even_here) + odd_around),
            (1, even_here + swap_halves(odd_here)),
            (2, swap_halves(even_around) + odd_here),
        ):
            at = (row_tap * 3 + col_tap) * C
            taps_one[at : at + C, :] = value
        for total, taps in ((sum_two, taps_two), (sum_three, taps_three)):
            even_here, odd_here, even_next, odd_before = (
                total[part * HID : (part + 1) * HID, here] for part in range(4)
            )
            for row_tap, value in (
                (0, swap_halves(even_here) + odd_before),
                (1, even_here + swap_halves(odd_here)),
                (2, odd_here + swap_halves(even_next)),
            ):
                at = (row_tap * 3 + col_tap) * HID
                taps[at : at + HID, :] = value
    last = (sum_four[0:HID, :] + sum_four[HID:128, :]) * (GAIN * 0.25)
    taps_four[0, 0:HID] = last[:, 0:128]
    taps_four[1, 0:HID] = last[:, 128:256]
    sums = sum_bias[...]
    tail = sums[:, 0:128]
    tail = tail + swap_halves(tail)
    outer = bias_ref[4:5, :]
    outer = (outer[:, 0:128], outer[:, 128:256])
    bias_high = jnp.concatenate(
        [
            tail[0:3],
            swap_halves(outer[0]),
            outer[0],
            swap_halves(outer[1]),
            outer[1],
            jnp.zeros((1, 128), F32),
        ],
        axis=0,
    )
    one, first, two, four = shard_layout(shards)
    held = shard_held(shards)
    gap = 2 * first - one - 8

    def collect(place, carry):
        start = pl.multiple_of(place * held, 8)
        shard = place
        if shards > 1:
            other, rest = place // (shards // 2), lax.rem(place, shards // 2)
            shard = me ^ (sent_mask(shards, rest) | other)
        at = pl.multiple_of(shard * one, 8)
        high = [swap_halves(taps_one[pl.ds(at + first, one - first), :])]
        if gap:
            high.append(jnp.zeros((gap, 128), F32))
        stage[pl.ds(start, first), :] = jnp.where(
            low_lanes((first, 128)),
            taps_one[pl.ds(at, first), :],
            jnp.concatenate(high + [bias_high], axis=0),
        )
        stage[pl.ds(start + first, two), :] = jnp.where(
            low_lanes((two, 128)),
            taps_two[pl.ds(shard * two, two), :],
            swap_halves(taps_three[pl.ds(shard * two, two), :]),
        )
        at = start + first + two
        for row in range(four // 2):
            row_at = shard * (four // 2) + row
            stage[pl.ds(at + 2 * row, 1), :] = taps_four[0, pl.ds(row_at, 1), :]
            stage[pl.ds(at + 2 * row + 1, 1), :] = taps_four[1, pl.ds(row_at, 1), :]
        return carry

    lax.fori_loop(0, shards, collect, 0, unroll=UNROLL if shards > 1 else 1)
    rows = keep_ref.shape[0] * held
    keep_ref[...] = stage[0:rows, :].reshape(keep_ref.shape).astype(keep_ref.dtype)
    sent = stage[shards * held - rows : shards * held, :]
    send_ref[...] = sent.reshape(send_ref.shape).astype(BF16)
    for fetch in fetches:
        fetch.wait()


BLOCK_SCRATCH = 23


def run_block(shards, bias_rows, even, odd, masks, spread, images, olds, pieces):
    count = even.shape[0]
    held = pieces[0].shape[1]
    part = max(shards // 2, 1)
    inside = pl.BlockSpec(memory_space=pltpu.VMEM)
    vmem = pltpu.VMEM
    hbm = pl.BlockSpec(memory_space=pl.ANY)
    place = pltpu.VMEM if shards > 1 else pltpu.HBM
    return pl.pallas_call(
        functools.partial(block_kernel, shards, len(olds)),
        in_specs=[*[inside] * 5, *[hbm] * (1 + len(olds)), *[inside] * len(pieces)],
        out_specs=[inside] * (7 + len(olds)),
        out_shape=[
            place((part, held, 128), KEEP_TYPE if shards > 1 else F32),
            place((part, held, 128), BF16),
            place((count, ROWS, 768), BF16),
            place((count, ROWS, 128), BF16),
            place((768, 2 * C), BF16),
            place((128, C), BF16),
            place(images.shape, BF16),
            *[place(old.shape, F32) for old in olds],
        ],
        scratch_shapes=[
            pltpu.SemaphoreType.DMA((1 + len(olds),)),
            vmem((shards * held + SPARE, 128), F32),
            vmem((9 * C + SPARE, 128), F32),
            vmem((9 * HID + SPARE, 128), F32),
            vmem((9 * HID + SPARE, 128), F32),
            vmem((2, HID + SPARE, 128), F32),
            vmem((2 * C, 768), BF16),
            vmem((4 * HID, 384), BF16),
            vmem((384, 256), BF16),
            vmem((4 * HID, 384), BF16),
            vmem((384, 256), BF16),
            vmem((C, 128), BF16),
            vmem((count, ROWS, 256), BF16),
            vmem((count, ROWS, 256), BF16),
            vmem((count, ROWS, 128), F32),
            vmem((count, ROWS, 128), F32),
            vmem((count, ROWS, 384), BF16),
            vmem((2 * count, HALF, SIDE + 2 * EDGE, 128), F32),
            vmem((2 * C, 768), F32),
            vmem((256, 384), F32),
            vmem((256, 384), F32),
            vmem((128, C), F32),
            vmem((8, C), F32),
        ],
        compiler_params=pltpu.CompilerParams(vmem_limit_bytes=BLOCK_BYTES),
        cost_estimate=pl.CostEstimate(
            flops=count * 1_200_000_000, bytes_accessed=count * 2_000_000, transcendentals=count * 196608
        ),
        name="block",
    )(
        *(in_vmem if shards > 1 else in_hbm)(bias_rows, even, odd, masks, spread),
        *in_hbm(images, *olds),
        *(in_vmem if shards > 1 else in_hbm)(*pieces),
    )


def finish_kernel(
    first,
    count,
    masks,
    bias_ref,
    img_ref,
    spread_ref,
    turned_ref,
    act_ref,
    back_ref,
    four_ref,
    *refs,
):
    out_hbm, grad_hbm, out_ref, grad_ref, back, sems = refs[-6:]
    stores = []

    def store(source, target):
        copy = pltpu.make_async_copy(source, target, sems.at[len(stores)])
        copy.start()
        stores.append(copy)

    spot = lax.broadcasted_iota(jnp.int32, (128, 256), 0)
    pix = lax.broadcasted_iota(jnp.int32, (128, 256), 1)
    pool_down = jnp.where(pix // 2 == spot, 0.25, 0.0).astype(BF16)
    back[0] = dot(turned_ref[first], back_ref[...])
    for slot in range(count):
        image = first + slot
        if slot + 1 < count:
            back[(slot + 1) % 2] = dot(turned_ref[image + 1], back_ref[...])
        for half in range(2):
            rows = slice(half * 256, (half + 1) * 256)
            base_mean = dot(pool_down, img_ref[image, :, 0].reshape(ROWS, C)[rows]) + dot(
                pool_down, img_ref[image, :, 1].reshape(ROWS, C)[rows]
            )
            act_mean = dot(pool_down, act_ref[image, rows, :]).astype(BF16)
            last = dot(act_mean, four_ref[...]) + bias_ref[3:4, :]
            pooled = 2.0 * dot(pool_down, masks[image, rows, :].astype(BF16))
            value = (base_mean + GAIN * last) * jnp.concatenate([pooled, pooled], axis=1)
            out_ref[slot, half * 8 : (half + 1) * 8] = value.reshape(8, HALF, C).astype(BF16)
        for start in range(0, ROWS, CHUNK):
            rows = slice(start, start + CHUNK)
            pairs = slice(start // SIDE, (start + CHUNK) // SIDE)
            mask = masks[image, rows, :]
            wide_mask = jnp.concatenate([mask, mask], axis=1)
            spread = 0.25 * spread_ref[image, rows, :].astype(F32)
            for parity in range(2):
                base = img_ref[image, pairs, parity].reshape(CHUNK, C).astype(F32)
                _, slope = silu_and_slope(base)
                lanes = slice(parity * C, (parity + 1) * C)
                value = spread + back[slot % 2, rows, lanes] * (slope * wide_mask)
                grad_ref[slot, pairs, parity] = value.reshape(-1, SIDE, C).astype(BF16)
        store(out_ref.at[slot], out_hbm.at[image])
        store(grad_ref.at[slot], grad_hbm.at[image])
    for copy in stores:
        copy.wait()


def run_finish(first, last, before, resident):
    total = resident[0].shape[0]
    count = last - first
    inside = pl.BlockSpec(memory_space=pltpu.VMEM)
    hbm = pl.BlockSpec(memory_space=pl.ANY)
    return pl.pallas_call(
        functools.partial(finish_kernel, first, count),
        in_specs=[*[inside] * len(resident), *[hbm] * len(before)],
        out_specs=[hbm, hbm],
        out_shape=[
            pltpu.HBM((total, HALF, HALF, C), BF16),
            pltpu.HBM((total, HALF, 2, SIDE, C), BF16),
        ],
        input_output_aliases={len(resident) + which: which for which in range(len(before))},
        scratch_shapes=[
            pltpu.VMEM((count, HALF, HALF, C), BF16),
            pltpu.VMEM((count, HALF, 2, SIDE, C), BF16),
            pltpu.VMEM((2, ROWS, 2 * C), F32),
            pltpu.SemaphoreType.DMA((2 * count,)),
        ],
        compiler_params=pltpu.CompilerParams(vmem_limit_bytes=FINISH_BYTES),
        cost_estimate=pl.CostEstimate(
            flops=count * 450_000_000, bytes_accessed=count * 2_500_000, transcendentals=count * 262144
        ),
        name="finish",
    )(*resident, *in_hbm(*before))


def fold_kernel(got, own_ref, *refs):
    outs = refs[got:]
    total = own_ref[...]
    for ref in refs[:got]:
        total = total + ref[...].astype(F32)
    rows = outs[0].shape[0]
    for which, out in enumerate(outs):
        out[...] = total[which * rows : (which + 1) * rows].astype(out.dtype)


def run_fold(own, received, parts):
    shape = (own.shape[0] // parts,) + own.shape[1:]
    inside = pl.BlockSpec(memory_space=pltpu.VMEM)
    return pl.pallas_call(
        functools.partial(fold_kernel, len(received)),
        in_specs=[inside] * (1 + len(received)),
        out_specs=[inside] * parts,
        out_shape=[pltpu.VMEM(shape, F32)] + [pltpu.VMEM(shape, BF16)] * (parts - 1),
        compiler_params=pltpu.CompilerParams(vmem_limit_bytes=FOLD_BYTES),
        cost_estimate=pl.CostEstimate(flops=500_000, bytes_accessed=1_000_000, transcendentals=0),
        name="fold",
    )(*in_vmem(own, *received))


def adamw_update(weight, gradient, first_old, second_old, step_rate):
    first_new = BETA_ONE * first_old + (1.0 - BETA_ONE) * gradient
    second_new = BETA_TWO * second_old + (1.0 - BETA_TWO) * gradient * gradient
    first_hat = first_new / (1.0 - BETA_ONE**STEP)
    second_hat = second_new / (1.0 - BETA_TWO**STEP)
    weight_new = weight - step_rate * (
        first_hat / (jnp.sqrt(second_hat) + EPSILON) + DECAY * weight
    )
    return (first_new, second_new, weight_new, weight_new.astype(BF16))


RATES = ((9.0 * C) ** (-0.5), (9.0 * HID) ** (-0.5), (9.0 * HID) ** (-0.5), 8.0)


def update_kernel(got, own_ref, *refs):
    received, refs = refs[:got], refs[got:]
    olds, news, total, rows_of_64 = refs[:15], refs[15:35], refs[35], refs[36]
    value = own_ref[0]
    for ref in received:
        value = value + ref[0].astype(F32)
    total[...] = value
    one, first, two, four = shard_layout(COMPACT[0] // olds[0].shape[0])

    def joined(rows):
        return jnp.where(
            low_lanes((rows, 128)),
            rows_of_64[pl.ds(0, rows, stride=2), :],
            swap_halves(rows_of_64[pl.ds(1, rows, stride=2), :]),
        )

    rows_of_64[0:first, :] = total[0:first, :]
    rows_of_64[first:one, :] = swap_halves(total[0 : one - first, :])
    gradients = [joined(one // 2)]
    rows_of_64[0:two, :] = total[first : first + two, :]
    gradients.append(joined(two // 2))
    rows_of_64[0:two, :] = swap_halves(total[first : first + two, :])
    gradients.append(joined(two // 2))
    gradients.append(total[first + two : first + two + four, :])
    rows = total[first - 8 : first, :]
    turned = swap_halves(rows)
    low = low_lanes((1, 128))
    parts = [jnp.where(low, turned[row : row + 1], rows[row + 1 : row + 2]) for row in (0, 2, 4)]
    parts.append(turned[6:7])
    gradients.append(jnp.concatenate(parts, axis=1)[:, 0:BIASES])
    rate = jnp.where(lax.broadcasted_iota(jnp.int32, (1, BIASES), 1) < 3 * HID, 0.5, 32.0)
    for which, gradient in enumerate(gradients):
        weight, first_old, second_old = (ref[...] for ref in olds[3 * which : 3 * which + 3])
        values = adamw_update(
            weight, gradient, first_old, second_old, rate if which == 4 else RATES[which]
        )
        for ref, value in zip(news[4 * which : 4 * which + 4], values):
            ref[...] = value.reshape(ref.shape)


def run_update(own, received, olds):
    shapes = []
    for which in range(5):
        shape = olds[3 * which].shape
        low_shape = shape if which < 4 else shape[1:]
        shapes += [jax.ShapeDtypeStruct(shape, F32)] * 3 + [jax.ShapeDtypeStruct(low_shape, BF16)]
    return pl.pallas_call(
        functools.partial(update_kernel, len(received)),
        out_shape=shapes,
        scratch_shapes=[pltpu.VMEM(own.shape[1:], F32), pltpu.VMEM((80, 128), F32)],
        compiler_params=pltpu.CompilerParams(vmem_limit_bytes=FOLD_BYTES),
        cost_estimate=pl.CostEstimate(flops=500_000, bytes_accessed=700_000, transcendentals=8192),
        name="update",
    )(*in_vmem(own, *received, *olds))


def exchange(value, mask, count):
    return lax.ppermute(value, AXES, [(i, i ^ mask) for i in range(count)])


def gather_shards(value, devices, beside):
    groups = bit_groups(devices)
    early, late = beside
    held = value[None]
    for low, top in groups[:-2]:
        parts = [held] + [
            exchange(held, mask << low, devices) for mask in range(1, 1 << (top - low))
        ]
        parts, early = lax.optimization_barrier((parts, early))
        held = jnp.concatenate(parts, axis=0)
    low, top = groups[-2]
    pieces = [exchange(held, mask << low, devices) for mask in range(1, 1 << (top - low))]
    pieces, late = lax.optimization_barrier((pieces, late))
    pieces = [held] + pieces
    return pieces + [exchange(piece, 1, devices) for piece in pieces], early, late


def bit_groups(devices):
    groups = []
    top = devices.bit_length() - 1
    while top > 1:
        low = max(top - 2, 1)
        groups.append((low, top))
        top = low
    groups.append((0, 1))
    return groups


def sent_mask(devices, place):
    mask = 0
    for low, top in bit_groups(devices)[:-1]:
        width = top - low
        mask = mask | ((place & ((1 << width) - 1)) << low)
        place = place >> width
    return mask


def place_mask(devices, place):
    mask = 0
    for low, top in bit_groups(devices):
        width = top - low
        mask = mask | ((place & ((1 << width) - 1)) << low)
        place = place >> width
    return mask


def local(devices, *args):
    (
        images,
        image_sizes,
        out_grad,
        weight_one,
        first_one,
        second_one,
        weight_two,
        first_two,
        second_two,
        weight_three,
        first_three,
        second_three,
        weight_four,
        first_four,
        second_four,
        biases,
        first_bias,
        second_bias,
    ) = args
    weights = (weight_one, weight_two, weight_three, weight_four)
    olds = (
        (weight_one, first_one, second_one),
        (weight_two, first_two, second_two),
        (weight_three, first_three, second_three),
        (weight_four, first_four, second_four),
    )
    count = images.shape[0]
    image_sizes = image_sizes.T
    images = images.reshape(count, HALF, 2, SIDE, C)
    sizes = [weight.shape[0] for weight in weights]
    total = sum(sizes)
    packed = (
        all(size % 128 == 0 for size in sizes)
        and sizes[3] % 256 == 0
        and devices >= 8
        and devices & (devices - 1) == 0
    )
    shards = devices if packed else 1
    held = shard_held(shards)
    beside = (
        run_spread(image_sizes, biases.reshape(1, BIASES), out_grad),
        run_active(image_sizes, images),
    )
    if packed:
        mine = run_pack(held, [weight.reshape(-1, 128) for weight in weights])
        pieces, *beside = gather_shards(mine, devices, beside)
    else:
        low = jnp.concatenate([weight.astype(BF16) for weight in weights])
        full = lax.all_gather(low, AXES, axis=0, tiled=False)
        parts = []
        at = 0
        for size in sizes:
            parts.append(full[:, at : at + size].reshape(-1))
            at += size
        one, first, two, four = shard_layout(1)
        rows = parts[0].reshape(one, HID)
        rows = jnp.concatenate(
            [rows[:first], jnp.pad(rows[first:], ((0, 2 * first - one), (0, 0)))], axis=1
        )
        both = jnp.concatenate([part.reshape(two, HID) for part in parts[1:3]], axis=1)
        full = jnp.concatenate([rows, both, parts[3].reshape(four, 128)], axis=0)
        pieces = [jnp.pad(full, ((0, held - full.shape[0]), (0, 0)))[None]]
    (spread, bias_rows), (even, odd, masks) = beside
    flat = []
    if packed:
        flat = [array.reshape(-1, 128) for three in olds for array in three]
        flat += [array.reshape(1, BIASES) for array in (biases, first_bias, second_bias)]
    keep, send, turned, act_three, back_one, fwd_four, base, *flat = run_block(
        shards, bias_rows, even, odd, masks, spread, images, flat, pieces
    )
    resident = [masks, bias_rows, base, spread, turned, act_three, back_one, fwd_four]
    outs = ()
    if packed:
        own, received = keep, [exchange(send, 1, devices)]
        groups = bit_groups(devices)[:-1][::-1]
        cuts = [0] + [FINISH_SPLIT] * (len(groups) - 1) + [count]
        for which, (low, top) in enumerate(groups):
            own, *sent = run_fold(own, received, 1 << (top - low))
            sent, resident, outs = lax.optimization_barrier((sent, resident, outs))
            received = [exchange(part, (at + 1) << low, devices) for at, part in enumerate(sent)]
            if cuts[which] < cuts[which + 1]:
                outs = run_finish(cuts[which], cuts[which + 1], outs, in_vmem(*resident))
            received, outs = lax.optimization_barrier((received, outs))
    else:
        outs = run_finish(0, count, outs, in_hbm(*resident))
    block_out, image_grad = outs
    image_grad = image_grad.reshape(count, SIDE, SIDE, C)
    if packed:
        updates = [array.reshape(-1) for array in run_update(own, received, flat)]
        return (block_out, image_grad, *updates)
    rows = keep[0]
    one, first, two, four = shard_layout(1)
    parts = [
        jnp.concatenate([rows[:first, :HID], rows[: one - first, HID:]], axis=0),
        rows[first : first + two, :HID],
        rows[first : first + two, HID:],
        rows[first + two : first + two + four],
    ]
    parts = [part.reshape(devices, -1) for part in parts]
    bias_part = rows[first - 8 : first - 1, HID:].reshape(-1)
    bias_total = lax.psum(bias_part, AXES)
    summed = lax.psum_scatter(
        jnp.concatenate(parts, axis=1).reshape(-1), AXES, scatter_dimension=0, tiled=True
    )
    updates = []
    at = 0
    for (weight, first, second), rate, size in zip(olds, RATES, sizes):
        updates += list(adamw_update(weight, summed[at : at + size], first, second, rate))
        at += size
    bias_rates = jnp.where(jnp.arange(BIASES) < 3 * HID, 0.5, 32.0)
    updates += list(adamw_update(biases, bias_total, first_bias, second_bias, bias_rates))
    return (block_out, image_grad, *updates)


def solution(mesh):
    devices = mesh.shape["dp"] * mesh.shape["fsdp"]
    split = P(AXES)
    return jax.shard_map(
        functools.partial(local, devices),
        mesh=mesh,
        in_specs=(
            P(AXES, None, None, None),
            P(AXES, None),
            P(AXES, None, None, None),
            *([split] * 12),
            P(),
            P(),
            P(),
        ),
        out_specs=(
            P(AXES, None, None, None),
            P(AXES, None, None, None),
            *([split] * 16),
            P(),
            P(),
            P(),
            P(),
        ),
        check_vma=False,
    )
```

```python
import functools

import jax
import jax.numpy as jnp
from jax import lax
from jax.experimental import pallas as pl
from jax.experimental.pallas import tpu as pltpu
from jax.sharding import PartitionSpec as P

C = 256
HID = 64
STEP = 10
SIDE = 32
HALF = SIDE // 2
ROWS = HALF * SIDE
PAD = SIDE

GAIN = 1.0 / 64.0
BETA_ONE = 0.9
BETA_TWO = 0.999
DECAY = 0.01
EPSILON = 1e-08
AXES = ("dp", "fsdp")
UNROLL = 16
SPARE = 8
SPREAD_BYTES = 58 * 1024 * 1024
ACTIVE_BYTES = 56 * 1024 * 1024
BLOCK_BYTES = 40 * 1024 * 1024
FINISH_BYTES = 24 * 1024 * 1024
FOLD_BYTES = 24 * 1024 * 1024
FINISH_SPLIT = 3
CHUNK = 64
LAG = 1
MERGE = 1
EDGE = 8
KEEP_TYPE = jnp.float32

COMPACT = (9 * C * HID // 128, 9 * HID * HID // 128, 9 * HID * HID // 128, HID * C // 128)
BIASES = 3 * HID + C

F32 = jnp.float32
BF16 = jnp.bfloat16


def silu(value):
    half = 0.5 * value
    return half * (1.0 + jnp.tanh(half))


def silu_and_slope(value):
    half = 0.5 * value
    turn = jnp.tanh(half)
    above = 1.0 + turn
    return half * above, above + half * (1.0 - turn * turn)


def dot(left, right):
    return jnp.dot(left, right, preferred_element_type=F32)


def dot_rows(left, right):
    return lax.dot_general(left, right, (((0,), (0,)), ((), ())), preferred_element_type=F32)


def swap_halves(value):
    return pltpu.roll(value, HID, 1)


def low_lanes(shape):
    return lax.broadcasted_iota(jnp.int32, shape, 1) < HID


def shard_layout(shards):
    one, two, three, four = (rows // shards for rows in COMPACT)
    first = -(-(one + 4) // 8) * 8
    return 2 * one, first, 2 * two, four


def shard_held(shards):
    _, first, two, four = shard_layout(shards)
    return -(-(first + two + four) // 16) * 16


def pack_kernel(one_ref, two_ref, three_ref, four_ref, out_ref, stage, rows_of_64):
    _, first, two, four = shard_layout(COMPACT[0] // one_ref.shape[0])
    stage[...] = jnp.zeros(stage.shape, F32)

    def spread_rows(ref):
        value = ref[...]
        rows = value.shape[0]
        rows_of_64[pl.ds(0, rows, stride=2), :] = value
        rows_of_64[pl.ds(1, rows, stride=2), :] = swap_halves(value)

    spread_rows(one_ref)
    rest = 2 * one_ref.shape[0] - first
    low = low_lanes((rest, 128))
    stage[0:rest, :] = jnp.where(
        low, rows_of_64[0:rest, :], swap_halves(rows_of_64[first : first + rest, :])
    )
    stage[rest:first, :] = rows_of_64[rest:first, :]
    spread_rows(two_ref)
    value = rows_of_64[0:two, :]
    spread_rows(three_ref)
    stage[first : first + two, :] = jnp.where(
        low_lanes((two, 128)), value, swap_halves(rows_of_64[0:two, :])
    )
    stage[first + two : first + two + four, :] = four_ref[...]
    out_ref[...] = stage[...].astype(BF16)


def run_pack(held, weights):
    return pl.pallas_call(
        pack_kernel,
        out_shape=pltpu.VMEM((held, 128), BF16),
        scratch_shapes=[pltpu.VMEM((held, 128), F32), pltpu.VMEM((80, 128), F32)],
        cost_estimate=pl.CostEstimate(flops=8192, bytes_accessed=48 * 1024, transcendentals=0),
        name="pack",
    )(*in_hbm(*weights))


def pair_inside(sizes_ref, image):
    shape = (HALF, SIDE, 128)
    row = lax.broadcasted_iota(jnp.int32, shape, 0)
    col = lax.broadcasted_iota(jnp.int32, shape, 1)
    inside = (row < sizes_ref[0, image] // 2) & (col < sizes_ref[1, image])
    return jnp.where(inside, 1.0, 0.0).reshape(ROWS, 128)


def pooled_inside(sizes_ref, step):
    spot = lax.broadcasted_iota(jnp.int32, (HALF * HALF, C), 0)
    return (spot < sizes_ref[0, step] * (HALF // 2)) & (
        jnp.bitwise_and(spot, HALF - 1) < sizes_ref[1, step] // 2
    )


def spread_kernel(sizes_ref, bias_ref, og_ref, spread_ref, bias_rows_ref):
    parts = [bias_ref[:, at : at + 128] for at in (0, 128, 256)]
    last = jnp.concatenate([bias_ref[:, 384:448], jnp.zeros((1, HID), F32)], axis=1)
    parts.append(last)
    turned = [swap_halves(part) for part in parts]
    low = low_lanes((1, 128))
    zero = jnp.zeros((1, 128), F32)
    rows = [
        (jnp.where(low, parts[0], turned[0]), zero),
        (jnp.where(low, turned[0], parts[0]), zero),
        (jnp.where(low, parts[1], turned[1]), zero),
        (jnp.where(low, turned[1], turned[2]), jnp.where(low, turned[2], turned[3])),
    ]
    for row, pair in enumerate(rows):
        bias_rows_ref[row : row + 1, :] = jnp.concatenate(pair, axis=1)
    total = jnp.zeros((1, C), F32)
    pix = lax.broadcasted_iota(jnp.int32, (256, 128), 0)
    spot = lax.broadcasted_iota(jnp.int32, (256, 128), 1)
    spread_up = jnp.where(pix // 2 == spot, 1.0, 0.0).astype(BF16)
    for image in range(og_ref.shape[0]):
        cot = jnp.where(
            pooled_inside(sizes_ref, image),
            og_ref[image].reshape(HALF * HALF, C).astype(F32),
            0.0,
        )
        total = total + jnp.sum(cot, axis=0, keepdims=True)
        cot = cot.astype(BF16)
        for half in range(2):
            value = dot(spread_up, cot[half * 128 : (half + 1) * 128])
            spread_ref[image, half * 256 : (half + 1) * 256, :] = value.astype(BF16)
    bias_rows_ref[4:8, :] = jnp.concatenate([total * GAIN, jnp.zeros((3, C), F32)], axis=0)


def active_kernel(sizes_ref, img_ref, even_ref, odd_ref, mask_ref):
    step = pl.program_id(0)
    mask = pair_inside(sizes_ref, step)
    mask_ref[step] = mask
    wide_mask = jnp.concatenate([mask, mask], axis=1)
    for parity, act in ((0, even_ref), (1, odd_ref)):
        base = img_ref[0, :, parity].reshape(ROWS, C).astype(F32)
        act[step] = (silu(base) * wide_mask).astype(BF16)


def in_vmem(*arrays):
    return [pltpu.with_memory_space_constraint(array, pltpu.VMEM) for array in arrays]


def in_hbm(*arrays):
    return [pltpu.with_memory_space_constraint(array, pltpu.HBM) for array in arrays]


def block_of(shape):
    rest = (0,) * (len(shape) - 1)
    return pl.BlockSpec(shape, lambda i: (i,) + rest)


def whole(shape):
    return pl.BlockSpec(shape, lambda i: (0,) * len(shape))


def run_spread(sizes, biases, out_grad):
    count = out_grad.shape[0]
    vmem = pl.BlockSpec(memory_space=pltpu.VMEM)
    return pl.pallas_call(
        spread_kernel,
        in_specs=[pl.BlockSpec(memory_space=pltpu.SMEM), vmem, vmem],
        out_specs=[vmem, vmem],
        out_shape=[
            pltpu.VMEM((count, ROWS, C), BF16),
            pltpu.VMEM((8, C), F32),
        ],
        compiler_params=pltpu.CompilerParams(vmem_limit_bytes=SPREAD_BYTES),
        cost_estimate=pl.CostEstimate(
            flops=count * 2 * 512 * 128 * 256, bytes_accessed=count * 400_000, transcendentals=0
        ),
        name="spread",
    )(sizes, *in_hbm(biases, out_grad))


def run_active(sizes, images):
    count = images.shape[0]
    return pl.pallas_call(
        active_kernel,
        grid=(count,),
        in_specs=[
            pl.BlockSpec(memory_space=pltpu.SMEM),
            block_of((1, HALF, 2, SIDE, C)),
        ],
        out_specs=[pl.BlockSpec(memory_space=pltpu.VMEM)] * 3,
        out_shape=[
            pltpu.VMEM((count, ROWS, C), BF16),
            pltpu.VMEM((count, ROWS, C), BF16),
            pltpu.VMEM((count, ROWS, 128), F32),
        ],
        compiler_params=pltpu.CompilerParams(
            dimension_semantics=("arbitrary",), vmem_limit_bytes=ACTIVE_BYTES
        ),
        cost_estimate=pl.CostEstimate(
            flops=count * 3_000_000, bytes_accessed=count * 1_100_000, transcendentals=count * 262144
        ),
        name="active",
    )(sizes, *in_hbm(images))


def unpack_weights(shards, me, pieces, stage, taps_one, taps_two, taps_three, taps_four):
    one, first, two, four = shard_layout(shards)
    held = pieces[0].shape[1]
    for which, piece in enumerate(pieces):
        group = piece.shape[0]
        stage[which * group * held : (which + 1) * group * held, :] = (
            piece[...].reshape(group * held, 128).astype(F32)
        )

    def place(shard, carry):
        owner = me ^ place_mask(shards, shard) if shards > 1 else shard
        start = pl.multiple_of(shard * held, 8)
        value = stage[pl.ds(start, first), :]
        at = pl.multiple_of(owner * one, 8)
        taps_one[pl.ds(at, first), :] = value
        taps_one[pl.ds(at + first, one - first), :] = swap_halves(value[0 : one - first])
        value = stage[pl.ds(start + first, two), :]
        taps_two[pl.ds(owner * two, two), :] = value
        taps_three[pl.ds(owner * two, two), :] = swap_halves(value)
        at = start + first + two
        for row in range(four // 2):
            row_at = owner * (four // 2) + row
            taps_four[0, pl.ds(row_at, 1), :] = stage[pl.ds(at + 2 * row, 1), :]
            taps_four[1, pl.ds(row_at, 1), :] = stage[pl.ds(at + 2 * row + 1, 1), :]
        return carry

    lax.fori_loop(0, shards, place, 0, unroll=UNROLL if shards > 1 else 1)


def tap_blocks(taps, width, col_tap):
    rows = [
        taps[(row_tap * 3 + col_tap) * width : (row_tap * 3 + col_tap + 1) * width, :]
        for row_tap in range(3)
    ]
    low = low_lanes((width, 128))
    zero = jnp.zeros((width, 128), F32)
    turned = [swap_halves(value) for value in rows]
    return (
        jnp.where(low, rows[0], zero),
        jnp.where(low, rows[1], turned[0]),
        jnp.where(low, rows[2], turned[1]),
        jnp.where(low, zero, turned[2]),
    )


def block_kernel(
    shards,
    fetched,
    bias_ref,
    even_ref,
    odd_ref,
    masks,
    spread_ref,
    img_hbm,
    *refs,
):
    olds, refs = refs[:fetched], refs[fetched:]
    outs = 7 + fetched
    cut = len(refs) - BLOCK_SCRATCH - outs
    pieces, refs = refs[:cut], refs[cut:]
    keep_ref, send_ref, turned_ref, act_three_ref, back_one_ref, fwd_four_ref, img_ref = refs[:7]
    news = refs[7:outs]
    (
        sems,
        stage,
        taps_one,
        taps_two,
        taps_three,
        taps_four,
        fwd_one,
        fwd_two,
        back_two,
        fwd_three,
        back_three,
        back_four,
        act_one,
        act_two,
        slope_one,
        slope_two,
        turned,
        shifts,
        sum_one,
        sum_two,
        sum_three,
        sum_four,
        sum_bias,
    ) = refs[outs:]
    images = even_ref.shape[0]
    fetches = [
        pltpu.make_async_copy(source, target, sems.at[which])
        for which, (source, target) in enumerate(zip((img_hbm, *olds), (img_ref, *news)))
    ]
    for fetch in fetches:
        fetch.start()
    for which in range(2 * images):
        none = jnp.zeros((HALF, EDGE, 128), F32)
        shifts[which, :, 0:EDGE, :] = none
        shifts[which, :, EDGE + SIDE : 2 * EDGE + SIDE, :] = none
    me = lax.axis_index(AXES) if shards > 1 else 0
    unpack_weights(shards, me, pieces, stage, taps_one, taps_two, taps_three, taps_four)
    for col_tap in range(3):
        lanes = slice(col_tap * 128, (col_tap + 1) * 128)
        more = slice(384 + col_tap * 128, 384 + (col_tap + 1) * 128)
        blocks = tap_blocks(taps_one, C, col_tap)
        fwd_one[0:C, lanes] = blocks[1].astype(BF16)
        fwd_one[C : 2 * C, lanes] = blocks[2].astype(BF16)
        fwd_one[0:C, more] = blocks[3].astype(BF16)
        fwd_one[C : 2 * C, more] = blocks[0].astype(BF16)
        back_one_ref[lanes, 0:C] = (0.5 * blocks[1]).T.astype(BF16)
        back_one_ref[lanes, C : 2 * C] = (0.5 * blocks[2]).T.astype(BF16)
        back_one_ref[more, 0:C] = (0.5 * blocks[3]).T.astype(BF16)
        back_one_ref[more, C : 2 * C] = (0.5 * blocks[0]).T.astype(BF16)
        for taps, fwd, back in (
            (taps_two, fwd_two, back_two),
            (taps_three, fwd_three, back_three),
        ):
            blocks = tap_blocks(taps, HID, col_tap)
            for place, which in enumerate((1, 2, 3, 0)):
                fwd[place * HID : (place + 1) * HID, lanes] = blocks[which].astype(BF16)
            here = jnp.concatenate([blocks[1], blocks[2]], axis=0).T
            around = jnp.concatenate([blocks[3], blocks[0]], axis=0).T
            back[lanes, 0:128] = (0.5 * here).astype(BF16)
            back[lanes, 128:256] = (0.5 * around).astype(BF16)
    four = jnp.concatenate([taps_four[0, 0:HID], taps_four[1, 0:HID]], axis=1)
    both = jnp.concatenate([four, four], axis=0)
    fwd_four_ref[...] = both.astype(BF16)
    back_four[...] = (0.5 * both).T.astype(BF16)

    low = low_lanes((ROWS, 128))
    low_wide = jnp.concatenate([low, low, low], axis=1)

    def rows_before(value):
        return jnp.concatenate([jnp.zeros((PAD, value.shape[1]), value.dtype), value[:-PAD]], axis=0)

    def rows_after(value):
        return jnp.concatenate([value[PAD:], jnp.zeros((PAD, value.shape[1]), value.dtype)], axis=0)

    def add_to(total, value, slot):
        total[...] = value if slot == 0 else total[...] + value

    def image_phases(slot):
        first, second, around_grad = act_one.at[slot], act_two.at[slot], turned.at[slot]
        left, right = shifts.at[2 * slot], shifts.at[2 * slot + 1]

        def by_rows(value):
            return value.reshape(HALF, SIDE, 128)

        def shift_sum(parts):
            left[:, EDGE : EDGE + SIDE, :] = by_rows(parts[:, 0:128])
            right[:, EDGE : EDGE + SIDE, :] = by_rows(parts[:, 256:384])
            before = left[:, EDGE - 1 : EDGE - 1 + SIDE, :]
            after = right[:, EDGE + 1 : EDGE + 1 + SIDE, :]
            return (before + by_rows(parts[:, 128:256]) + after).reshape(ROWS, 128)

        def activate(conv):
            active, slope = silu_and_slope(conv)
            return (active * masks[slot]).astype(BF16), slope * masks[slot]

        def keep_active(act, active):
            act[:, 0:128] = active
            act[:, 128:256] = jnp.where(low, rows_after(active), rows_before(active))

        def turn(grad, row, into):
            add_to(sum_bias.at[row : row + 1, 0:128], jnp.sum(grad, axis=0, keepdims=True), slot)
            left[:, EDGE : EDGE + SIDE, :] = by_rows(grad)
            parts = (
                left[:, EDGE + 1 : EDGE + 1 + SIDE, :].reshape(ROWS, 128),
                grad,
                left[:, EDGE - 1 : EDGE - 1 + SIDE, :].reshape(ROWS, 128),
            )
            value = jnp.concatenate([part.astype(BF16) for part in parts], axis=1)
            into[:, 0:384] = value
            return value

        def back_through(window, kernel):
            parts = dot(window, kernel)
            around = parts[:, 128:256]
            return parts[:, 0:128], around

        def back_sum(pair):
            here, around = pair
            return here + jnp.where(low, rows_before(around), rows_after(around))

        window = jnp.concatenate(
            [even_ref[slot], odd_ref[slot]], axis=1
        )
        parts = dot(window, fwd_one[...])
        yield
        parts = parts[:, 0:384] + jnp.where(
            low_wide, rows_before(parts[:, 384:768]), rows_after(parts[:, 384:768])
        )
        active, slope = activate(shift_sum(parts) + bias_ref[0:1, 0:128])
        keep_active(first, active)
        slope_one[slot] = slope
        yield
        parts = dot(first[...], fwd_two[...])
        yield
        active, slope = activate(shift_sum(parts) + bias_ref[1:2, 0:128])
        keep_active(second, active)
        slope_two[slot] = slope
        yield
        parts = dot(second[...], fwd_three[...])
        back = dot(spread_ref[slot], back_four[...])
        yield
        active, slope = activate(shift_sum(parts) + bias_ref[2:3, 0:128])
        act_three_ref[slot] = active
        turn(back * (GAIN * 0.25) * slope, 2, around_grad)
        yield
        back = back_through(around_grad[:, 0:384], back_three[...])
        part = dot_rows(act_three_ref[slot], spread_ref[slot])
        for half in (slice(0, HID), slice(HID, 2 * HID)):
            add_to(sum_four.at[half, :], part[half, :], slot)
        add_to(sum_three, dot_rows(second[...], around_grad[:, 0:384]), slot)
        yield
        turn(back_sum(back) * slope_two[slot], 1, around_grad)
        yield
        back = back_through(around_grad[:, 0:384], back_two[...])
        add_to(sum_two, dot_rows(first[...], around_grad[:, 0:384]), slot)
        yield
        window = turn(back_sum(back) * slope_one[slot], 0, turned_ref.at[slot])
        turned_ref[slot, :, 384:768] = jnp.where(low_wide, rows_after(window), rows_before(window))
        yield
        if slot % MERGE == MERGE - 1 or slot == images - 1:
            first_slot = slot - slot % MERGE
            slots = range(first_slot, slot + 1)
            both = jnp.concatenate(
                [
                    jnp.concatenate(
                        [even_ref[at], odd_ref[at]], axis=1
                    )
                    for at in slots
                ],
                axis=0,
            )
            window = turned_ref[first_slot : slot + 1].reshape(len(slots) * ROWS, 768)
            add_to(sum_one, dot_rows(both, window), first_slot)

    waiting = [image_phases(slot) for slot in range(images)]
    turn_number = 0
    while waiting:
        for place, phases in enumerate(list(waiting)):
            if turn_number >= LAG * place or len(waiting) < images:
                if next(phases, waiting) is waiting:
                    waiting.remove(phases)
        turn_number += 1

    for col_tap in range(3):
        here = slice(col_tap * 128, (col_tap + 1) * 128)
        around = slice(384 + col_tap * 128, 384 + (col_tap + 1) * 128)
        even_here, even_around = sum_one[0:C, here], sum_one[0:C, around]
        odd_here, odd_around = sum_one[C : 2 * C, here], sum_one[C : 2 * C, around]
        for row_tap, value in (
            (0, swap_halves(even_here) + odd_around),
            (1, even_here + swap_halves(odd_here)),
            (2, swap_halves(even_around) + odd_here),
        ):
            at = (row_tap * 3 + col_tap) * C
            taps_one[at : at + C, :] = value
        for total, taps in ((sum_two, taps_two), (sum_three, taps_three)):
            even_here, odd_here, even_next, odd_before = (
                total[part * HID : (part + 1) * HID, here] for part in range(4)
            )
            for row_tap, value in (
                (0, swap_halves(even_here) + odd_before),
                (1, even_here + swap_halves(odd_here)),
                (2, odd_here + swap_halves(even_next)),
            ):
                at = (row_tap * 3 + col_tap) * HID
                taps[at : at + HID, :] = value
    last = (sum_four[0:HID, :] + sum_four[HID:128, :]) * (GAIN * 0.25)
    taps_four[0, 0:HID] = last[:, 0:128]
    taps_four[1, 0:HID] = last[:, 128:256]
    sums = sum_bias[...]
    tail = sums[:, 0:128]
    tail = tail + swap_halves(tail)
    outer = bias_ref[4:5, :]
    outer = (outer[:, 0:128], outer[:, 128:256])
    bias_high = jnp.concatenate(
        [
            tail[0:3],
            swap_halves(outer[0]),
            outer[0],
            swap_halves(outer[1]),
            outer[1],
            jnp.zeros((1, 128), F32),
        ],
        axis=0,
    )
    one, first, two, four = shard_layout(shards)
    held = shard_held(shards)
    gap = 2 * first - one - 8

    def collect(place, carry):
        start = pl.multiple_of(place * held, 8)
        shard = place
        if shards > 1:
            other, rest = place // (shards // 2), lax.rem(place, shards // 2)
            shard = me ^ (sent_mask(shards, rest) | other)
        at = pl.multiple_of(shard * one, 8)
        high = [swap_halves(taps_one[pl.ds(at + first, one - first), :])]
        if gap:
            high.append(jnp.zeros((gap, 128), F32))
        stage[pl.ds(start, first), :] = jnp.where(
            low_lanes((first, 128)),
            taps_one[pl.ds(at, first), :],
            jnp.concatenate(high + [bias_high], axis=0),
        )
        stage[pl.ds(start + first, two), :] = jnp.where(
            low_lanes((two, 128)),
            taps_two[pl.ds(shard * two, two), :],
            swap_halves(taps_three[pl.ds(shard * two, two), :]),
        )
        at = start + first + two
        for row in range(four // 2):
            row_at = shard * (four // 2) + row
            stage[pl.ds(at + 2 * row, 1), :] = taps_four[0, pl.ds(row_at, 1), :]
            stage[pl.ds(at + 2 * row + 1, 1), :] = taps_four[1, pl.ds(row_at, 1), :]
        return carry

    lax.fori_loop(0, shards, collect, 0, unroll=UNROLL if shards > 1 else 1)
    rows = keep_ref.shape[0] * held
    keep_ref[...] = stage[0:rows, :].reshape(keep_ref.shape).astype(keep_ref.dtype)
    sent = stage[shards * held - rows : shards * held, :]
    send_ref[...] = sent.reshape(send_ref.shape).astype(BF16)
    for fetch in fetches:
        fetch.wait()


BLOCK_SCRATCH = 23


def run_block(shards, bias_rows, even, odd, masks, spread, images, olds, pieces):
    count = even.shape[0]
    held = pieces[0].shape[1]
    part = max(shards // 2, 1)
    inside = pl.BlockSpec(memory_space=pltpu.VMEM)
    vmem = pltpu.VMEM
    hbm = pl.BlockSpec(memory_space=pl.ANY)
    place = pltpu.VMEM if shards > 1 else pltpu.HBM
    return pl.pallas_call(
        functools.partial(block_kernel, shards, len(olds)),
        in_specs=[*[inside] * 5, *[hbm] * (1 + len(olds)), *[inside] * len(pieces)],
        out_specs=[inside] * (7 + len(olds)),
        out_shape=[
            place((part, held, 128), KEEP_TYPE if shards > 1 else F32),
            place((part, held, 128), BF16),
            place((count, ROWS, 768), BF16),
            place((count, ROWS, 128), BF16),
            place((768, 2 * C), BF16),
            place((128, C), BF16),
            place(images.shape, BF16),
            *[place(old.shape, F32) for old in olds],
        ],
        scratch_shapes=[
            pltpu.SemaphoreType.DMA((1 + len(olds),)),
            vmem((shards * held + SPARE, 128), F32),
            vmem((9 * C + SPARE, 128), F32),
            vmem((9 * HID + SPARE, 128), F32),
            vmem((9 * HID + SPARE, 128), F32),
            vmem((2, HID + SPARE, 128), F32),
            vmem((2 * C, 768), BF16),
            vmem((4 * HID, 384), BF16),
            vmem((384, 256), BF16),
            vmem((4 * HID, 384), BF16),
            vmem((384, 256), BF16),
            vmem((C, 128), BF16),
            vmem((count, ROWS, 256), BF16),
            vmem((count, ROWS, 256), BF16),
            vmem((count, ROWS, 128), F32),
            vmem((count, ROWS, 128), F32),
            vmem((count, ROWS, 384), BF16),
            vmem((2 * count, HALF, SIDE + 2 * EDGE, 128), F32),
            vmem((2 * C, 768), F32),
            vmem((256, 384), F32),
            vmem((256, 384), F32),
            vmem((128, C), F32),
            vmem((8, C), F32),
        ],
        compiler_params=pltpu.CompilerParams(vmem_limit_bytes=BLOCK_BYTES),
        cost_estimate=pl.CostEstimate(
            flops=count * 1_200_000_000, bytes_accessed=count * 2_000_000, transcendentals=count * 196608
        ),
        name="block",
    )(
        *(in_vmem if shards > 1 else in_hbm)(bias_rows, even, odd, masks, spread),
        *in_hbm(images, *olds),
        *(in_vmem if shards > 1 else in_hbm)(*pieces),
    )


def finish_kernel(
    first,
    count,
    masks,
    bias_ref,
    img_ref,
    spread_ref,
    turned_ref,
    act_ref,
    back_ref,
    four_ref,
    *refs,
):
    out_hbm, grad_hbm, out_ref, grad_ref, back, sems = refs[-6:]
    stores = []

    def store(source, target):
        copy = pltpu.make_async_copy(source, target, sems.at[len(stores)])
        copy.start()
        stores.append(copy)

    spot = lax.broadcasted_iota(jnp.int32, (128, 256), 0)
    pix = lax.broadcasted_iota(jnp.int32, (128, 256), 1)
    pool_down = jnp.where(pix // 2 == spot, 0.25, 0.0).astype(BF16)
    back[0] = dot(turned_ref[first], back_ref[...])
    for slot in range(count):
        image = first + slot
        if slot + 1 < count:
            back[(slot + 1) % 2] = dot(turned_ref[image + 1], back_ref[...])
        for half in range(2):
            rows = slice(half * 256, (half + 1) * 256)
            base_mean = dot(pool_down, img_ref[image, :, 0].reshape(ROWS, C)[rows]) + dot(
                pool_down, img_ref[image, :, 1].reshape(ROWS, C)[rows]
            )
            act_mean = dot(pool_down, act_ref[image, rows, :]).astype(BF16)
            last = dot(act_mean, four_ref[...]) + bias_ref[3:4, :]
            pooled = 2.0 * dot(pool_down, masks[image, rows, :].astype(BF16))
            value = (base_mean + GAIN * last) * jnp.concatenate([pooled, pooled], axis=1)
            out_ref[slot, half * 8 : (half + 1) * 8] = value.reshape(8, HALF, C).astype(BF16)
        for start in range(0, ROWS, CHUNK):
            rows = slice(start, start + CHUNK)
            pairs = slice(start // SIDE, (start + CHUNK) // SIDE)
            mask = masks[image, rows, :]
            wide_mask = jnp.concatenate([mask, mask], axis=1)
            spread = 0.25 * spread_ref[image, rows, :].astype(F32)
            for parity in range(2):
                base = img_ref[image, pairs, parity].reshape(CHUNK, C).astype(F32)
                _, slope = silu_and_slope(base)
                lanes = slice(parity * C, (parity + 1) * C)
                value = spread + back[slot % 2, rows, lanes] * (slope * wide_mask)
                grad_ref[slot, pairs, parity] = value.reshape(-1, SIDE, C).astype(BF16)
        store(out_ref.at[slot], out_hbm.at[image])
        store(grad_ref.at[slot], grad_hbm.at[image])
    for copy in stores:
        copy.wait()


def run_finish(first, last, before, resident):
    total = resident[0].shape[0]
    count = last - first
    inside = pl.BlockSpec(memory_space=pltpu.VMEM)
    hbm = pl.BlockSpec(memory_space=pl.ANY)
    return pl.pallas_call(
        functools.partial(finish_kernel, first, count),
        in_specs=[*[inside] * len(resident), *[hbm] * len(before)],
        out_specs=[hbm, hbm],
        out_shape=[
            pltpu.HBM((total, HALF, HALF, C), BF16),
            pltpu.HBM((total, HALF, 2, SIDE, C), BF16),
        ],
        input_output_aliases={len(resident) + which: which for which in range(len(before))},
        scratch_shapes=[
            pltpu.VMEM((count, HALF, HALF, C), BF16),
            pltpu.VMEM((count, HALF, 2, SIDE, C), BF16),
            pltpu.VMEM((2, ROWS, 2 * C), F32),
            pltpu.SemaphoreType.DMA((2 * count,)),
        ],
        compiler_params=pltpu.CompilerParams(vmem_limit_bytes=FINISH_BYTES),
        cost_estimate=pl.CostEstimate(
            flops=count * 450_000_000, bytes_accessed=count * 2_500_000, transcendentals=count * 262144
        ),
        name="finish",
    )(*resident, *in_hbm(*before))


def fold_kernel(got, own_ref, *refs):
    outs = refs[got:]
    total = own_ref[...]
    for ref in refs[:got]:
        total = total + ref[...].astype(F32)
    rows = outs[0].shape[0]
    for which, out in enumerate(outs):
        out[...] = total[which * rows : (which + 1) * rows].astype(out.dtype)


def run_fold(own, received, parts):
    shape = (own.shape[0] // parts,) + own.shape[1:]
    inside = pl.BlockSpec(memory_space=pltpu.VMEM)
    return pl.pallas_call(
        functools.partial(fold_kernel, len(received)),
        in_specs=[inside] * (1 + len(received)),
        out_specs=[inside] * parts,
        out_shape=[pltpu.VMEM(shape, F32)] + [pltpu.VMEM(shape, BF16)] * (parts - 1),
        compiler_params=pltpu.CompilerParams(vmem_limit_bytes=FOLD_BYTES),
        cost_estimate=pl.CostEstimate(flops=500_000, bytes_accessed=1_000_000, transcendentals=0),
        name="fold",
    )(*in_vmem(own, *received))


def adamw_update(weight, gradient, first_old, second_old, step_rate):
    first_new = BETA_ONE * first_old + (1.0 - BETA_ONE) * gradient
    second_new = BETA_TWO * second_old + (1.0 - BETA_TWO) * gradient * gradient
    first_hat = first_new / (1.0 - BETA_ONE**STEP)
    second_hat = second_new / (1.0 - BETA_TWO**STEP)
    weight_new = weight - step_rate * (
        first_hat / (jnp.sqrt(second_hat) + EPSILON) + DECAY * weight
    )
    return (first_new, second_new, weight_new, weight_new.astype(BF16))


RATES = ((9.0 * C) ** (-0.5), (9.0 * HID) ** (-0.5), (9.0 * HID) ** (-0.5), 8.0)


def update_kernel(got, own_ref, *refs):
    received, refs = refs[:got], refs[got:]
    olds, news, total, rows_of_64 = refs[:15], refs[15:35], refs[35], refs[36]
    value = own_ref[0]
    for ref in received:
        value = value + ref[0].astype(F32)
    total[...] = value
    one, first, two, four = shard_layout(COMPACT[0] // olds[0].shape[0])

    def joined(rows):
        return jnp.where(
            low_lanes((rows, 128)),
            rows_of_64[pl.ds(0, rows, stride=2), :],
            swap_halves(rows_of_64[pl.ds(1, rows, stride=2), :]),
        )

    rows_of_64[0:first, :] = total[0:first, :]
    rows_of_64[first:one, :] = swap_halves(total[0 : one - first, :])
    gradients = [joined(one // 2)]
    rows_of_64[0:two, :] = total[first : first + two, :]
    gradients.append(joined(two // 2))
    rows_of_64[0:two, :] = swap_halves(total[first : first + two, :])
    gradients.append(joined(two // 2))
    gradients.append(total[first + two : first + two + four, :])
    rows = total[first - 8 : first, :]
    turned = swap_halves(rows)
    low = low_lanes((1, 128))
    parts = [jnp.where(low, turned[row : row + 1], rows[row + 1 : row + 2]) for row in (0, 2, 4)]
    parts.append(turned[6:7])
    gradients.append(jnp.concatenate(parts, axis=1)[:, 0:BIASES])
    rate = jnp.where(lax.broadcasted_iota(jnp.int32, (1, BIASES), 1) < 3 * HID, 0.5, 32.0)
    for which, gradient in enumerate(gradients):
        weight, first_old, second_old = (ref[...] for ref in olds[3 * which : 3 * which + 3])
        values = adamw_update(
            weight, gradient, first_old, second_old, rate if which == 4 else RATES[which]
        )
        for ref, value in zip(news[4 * which : 4 * which + 4], values):
            ref[...] = value.reshape(ref.shape)


def run_update(own, received, olds):
    shapes = []
    for which in range(5):
        shape = olds[3 * which].shape
        low_shape = shape if which < 4 else shape[1:]
        shapes += [jax.ShapeDtypeStruct(shape, F32)] * 3 + [jax.ShapeDtypeStruct(low_shape, BF16)]
    return pl.pallas_call(
        functools.partial(update_kernel, len(received)),
        out_shape=shapes,
        scratch_shapes=[pltpu.VMEM(own.shape[1:], F32), pltpu.VMEM((80, 128), F32)],
        compiler_params=pltpu.CompilerParams(vmem_limit_bytes=FOLD_BYTES),
        cost_estimate=pl.CostEstimate(flops=500_000, bytes_accessed=700_000, transcendentals=8192),
        name="update",
    )(*in_vmem(own, *received, *olds))


def exchange(value, mask, count):
    return lax.ppermute(value, AXES, [(i, i ^ mask) for i in range(count)])


def gather_shards(value, devices, beside):
    groups = bit_groups(devices)
    early, late = beside
    held = value[None]
    for low, top in groups[:-2]:
        parts = [held] + [
            exchange(held, mask << low, devices) for mask in range(1, 1 << (top - low))
        ]
        parts, early = lax.optimization_barrier((parts, early))
        held = jnp.concatenate(parts, axis=0)
    low, top = groups[-2]
    pieces = [exchange(held, mask << low, devices) for mask in range(1, 1 << (top - low))]
    pieces, late = lax.optimization_barrier((pieces, late))
    pieces = [held] + pieces
    return pieces + [exchange(piece, 1, devices) for piece in pieces], early, late


def bit_groups(devices):
    groups = []
    top = devices.bit_length() - 1
    while top > 1:
        low = max(top - 2, 1)
        groups.append((low, top))
        top = low
    groups.append((0, 1))
    return groups


def sent_mask(devices, place):
    mask = 0
    for low, top in bit_groups(devices)[:-1]:
        width = top - low
        mask = mask | ((place & ((1 << width) - 1)) << low)
        place = place >> width
    return mask


def place_mask(devices, place):
    mask = 0
    for low, top in bit_groups(devices):
        width = top - low
        mask = mask | ((place & ((1 << width) - 1)) << low)
        place = place >> width
    return mask


def local(devices, *args):
    (
        images,
        image_sizes,
        out_grad,
        weight_one,
        first_one,
        second_one,
        weight_two,
        first_two,
        second_two,
        weight_three,
        first_three,
        second_three,
        weight_four,
        first_four,
        second_four,
        biases,
        first_bias,
        second_bias,
    ) = args
    weights = (weight_one, weight_two, weight_three, weight_four)
    olds = (
        (weight_one, first_one, second_one),
        (weight_two, first_two, second_two),
        (weight_three, first_three, second_three),
        (weight_four, first_four, second_four),
    )
    count = images.shape[0]
    image_sizes = image_sizes.T
    images = images.reshape(count, HALF, 2, SIDE, C)
    sizes = [weight.shape[0] for weight in weights]
    total = sum(sizes)
    packed = (
        all(size % 128 == 0 for size in sizes)
        and sizes[3] % 256 == 0
        and devices >= 8
        and devices & (devices - 1) == 0
    )
    shards = devices if packed else 1
    held = shard_held(shards)
    beside = (
        run_spread(image_sizes, biases.reshape(1, BIASES), out_grad),
        run_active(image_sizes, images),
    )
    if packed:
        mine = run_pack(held, [weight.reshape(-1, 128) for weight in weights])
        pieces, *beside = gather_shards(mine, devices, beside)
    else:
        low = jnp.concatenate([weight.astype(BF16) for weight in weights])
        full = lax.all_gather(low, AXES, axis=0, tiled=False)
        parts = []
        at = 0
        for size in sizes:
            parts.append(full[:, at : at + size].reshape(-1))
            at += size
        one, first, two, four = shard_layout(1)
        rows = parts[0].reshape(one, HID)
        rows = jnp.concatenate(
            [rows[:first], jnp.pad(rows[first:], ((0, 2 * first - one), (0, 0)))], axis=1
        )
        both = jnp.concatenate([part.reshape(two, HID) for part in parts[1:3]], axis=1)
        full = jnp.concatenate([rows, both, parts[3].reshape(four, 128)], axis=0)
        pieces = [jnp.pad(full, ((0, held - full.shape[0]), (0, 0)))[None]]
    (spread, bias_rows), (even, odd, masks) = beside
    flat = []
    if packed:
        flat = [array.reshape(-1, 128) for three in olds for array in three]
        flat += [array.reshape(1, BIASES) for array in (biases, first_bias, second_bias)]
    keep, send, turned, act_three, back_one, fwd_four, base, *flat = run_block(
        shards, bias_rows, even, odd, masks, spread, images, flat, pieces
    )
    resident = [masks, bias_rows, base, spread, turned, act_three, back_one, fwd_four]
    outs = ()
    if packed:
        own, received = keep, [exchange(send, 1, devices)]
        groups = bit_groups(devices)[:-1][::-1]
        cuts = [0] + [FINISH_SPLIT] * (len(groups) - 1) + [count]
        for which, (low, top) in enumerate(groups):
            own, *sent = run_fold(own, received, 1 << (top - low))
            sent, resident, outs = lax.optimization_barrier((sent, resident, outs))
            received = [exchange(part, (at + 1) << low, devices) for at, part in enumerate(sent)]
            if cuts[which] < cuts[which + 1]:
                outs = run_finish(cuts[which], cuts[which + 1], outs, in_vmem(*resident))
            received, outs = lax.optimization_barrier((received, outs))
    else:
        outs = run_finish(0, count, outs, in_hbm(*resident))
    block_out, image_grad = outs
    image_grad = image_grad.reshape(count, SIDE, SIDE, C)
    if packed:
        updates = [array.reshape(-1) for array in run_update(own, received, flat)]
        return (block_out, image_grad, *updates)
    rows = keep[0]
    one, first, two, four = shard_layout(1)
    parts = [
        jnp.concatenate([rows[:first, :HID], rows[: one - first, HID:]], axis=0),
        rows[first : first + two, :HID],
        rows[first : first + two, HID:],
        rows[first + two : first + two + four],
    ]
    parts = [part.reshape(devices, -1) for part in parts]
    bias_part = rows[first - 8 : first - 1, HID:].reshape(-1)
    bias_total = lax.psum(bias_part, AXES)
    summed = lax.psum_scatter(
        jnp.concatenate(parts, axis=1).reshape(-1), AXES, scatter_dimension=0, tiled=True
    )
    updates = []
    at = 0
    for (weight, first, second), rate, size in zip(olds, RATES, sizes):
        updates += list(adamw_update(weight, summed[at : at + size], first, second, rate))
        at += size
    bias_rates = jnp.where(jnp.arange(BIASES) < 3 * HID, 0.5, 32.0)
    updates += list(adamw_update(biases, bias_total, first_bias, second_bias, bias_rates))
    return (block_out, image_grad, *updates)


def solution(mesh):
    devices = mesh.shape["dp"] * mesh.shape["fsdp"]
    split = P(AXES)
    return jax.shard_map(
        functools.partial(local, devices),
        mesh=mesh,
        in_specs=(
            P(AXES, None, None, None),
            P(AXES, None),
            P(AXES, None, None, None),
            *([split] * 12),
            P(),
            P(),
            P(),
        ),
        out_specs=(
            P(AXES, None, None, None),
            P(AXES, None, None, None),
            *([split] * 16),
            P(),
            P(),
            P(),
            P(),
        ),
        check_vma=False,
    )
```
